32 devices in a mesh: freq: 4 (over y, core), offset: 8 (over z, x).
Axes of the slice: x: 2, y: 2, z: 4, core: 2. Of those that a mesh axis runs over, the one named last changes fastest.
Arguments:
- raw_traces: bfloat16 [8192, 2048], P('offset', 'freq'), may hold values from -6 to 6
- trace_slot: int32 [32, 256], P(None, 'offset'), may hold values from 0 to 1023, as said below
- offset_index: int32 [256], replicated, may hold values from 1 to 1023
- slowness_index: int32 [256], replicated, may hold values from 0 to 511
Outputs:
- radon: float32 [256, 1024, 64], P('offset', 'freq')
The draws below stay inside these ranges and needn't reach their ends.
Inputs may be any that keep to these rules, and one draw needn't show every extreme that they name: `trace_slot`: in every aligned block of 32 columns, the 32 x 32 entries name each of 0 to 1023 exactly once.
All inputs are finite; a program needn't handle non-finite values.
Results may differ from the reference program's by a relative error of at most 0.0046.
Values may be sent and summed in bfloat16 or wider, within the bound.
No kernel may reach another device: no remote copies, remote signals or barrier semaphores. Data moves between devices by JAX's collectives and lax.ppermute only.
A program may use at most 64 MiB of HBM per device.

```python
import math
import jax
import jax.numpy as jnp
from jax import lax

NT = 2048
NF = 1024
NP = 256
GATHERS = 32
H_DEV = 32
NH = 256
N_OFFSET = 8


def draw_trace_slot(key, part):
    block_rows = GATHERS * H_DEV
    key_list = jax.random.split(jax.random.fold_in(key, 7), N_OFFSET)
    orders = jax.vmap(lambda single: jax.random.permutation(single, block_rows))(key_list)
    shaped = orders.reshape(N_OFFSET, GATHERS, H_DEV)
    return jnp.transpose(shaped, (1, 0, 2)).reshape(GATHERS, N_OFFSET * H_DEV).astype(jnp.int32)


def place_ends(drawn, stream_key, low, largest):
    place = [jax.random.randint(jax.random.fold_in(stream_key, axis), (), 0, length) for axis, length in enumerate(drawn.shape)]
    longest = drawn.shape.index(max(drawn.shape))
    beside = place[:longest] + [(place[longest] + 1) % drawn.shape[longest]] + place[longest + 1:]
    return drawn.at[tuple(place)].set(low).at[tuple(beside)].set(largest)


def shard_levels(stream_key, extent, cuts, smallest, top_value):
    factor_of, own = 1.0, jax.random.fold_in(stream_key, 6)
    for dim, parts in cuts:
        steps = jnp.exp(jax.random.uniform(jax.random.fold_in(own, dim), (parts,), jnp.float32, smallest / len(cuts), top_value / len(cuts)))
        factor_of = factor_of * jnp.repeat(steps, extent[dim] // parts).reshape([-1 if axis == dim else 1 for axis in range(len(extent))])
    return factor_of


def scatter_about(own_key, shape, scale, limit, cuts=(), kind=jnp.bfloat16):
    gain = shard_levels(own_key, shape, cuts, -0.22, 0.18) if cuts else 1.0
    result = jax.random.normal(own_key, shape, jnp.float32) * scale * gain
    return jnp.minimum(jnp.maximum(result, -limit), limit).astype(kind)


def setup_inputs(seed: int = 0) -> dict:
    streams_of = jax.random.split(jax.random.key(seed), 5)
    raw_traces = scatter_about(streams_of[0], (GATHERS * NH, NT), 1.0, 6.0, ((0, 8), (1, 4)))
    trace_slot = draw_trace_slot(jax.random.fold_in(streams_of[4], 71), 0)
    offset_index = place_ends(jax.random.randint(streams_of[2], (NH,), 1, 1024), jax.random.fold_in(streams_of[2], 1), 1, 1023).astype(jnp.int32)
    slowness_index = place_ends(jax.random.randint(streams_of[3], (NP,), 0, 512), jax.random.fold_in(streams_of[3], 1), 0, 511).astype(jnp.int32)
    return {"raw_traces": raw_traces, "trace_slot": trace_slot, "offset_index": offset_index, "slowness_index": slowness_index}


APEX_TIME = 100.0
CURVATURE = 0.0003

def moveout(slowness, offset_grid):
    spread = CURVATURE * slowness.astype(jnp.float32)[:, None] * offset_grid.astype(jnp.float32)[None, :]
    return jnp.sqrt(APEX_TIME * APEX_TIME + spread * spread) - APEX_TIME

def reference(raw_traces, trace_slot, offset_index, slowness_index):
    block_rows = GATHERS * H_DEV
    row_base = jnp.arange(NH, dtype=jnp.int32) // H_DEV * block_rows
    trace_rows = (trace_slot + row_base[None, :]).reshape(-1).astype(jnp.int32)
    gathered = raw_traces[trace_rows].astype(jnp.float32)
    sample_ids = jnp.arange(NT, dtype=jnp.int32)[:, None]
    freq_ids = jnp.arange(NF, dtype=jnp.int32)[None, :]
    turn_ids = sample_ids * (2 * freq_ids + 1) % (2 * NT)
    angles = turn_ids.astype(jnp.float32) * (math.pi / NT)
    fourier_table = (jnp.concatenate([jnp.cos(angles), -jnp.sin(angles)], axis=1) / math.sqrt(NT)).astype(jnp.bfloat16)
    spectrum = jnp.dot(gathered, fourier_table.astype(jnp.float32), preferred_element_type=jnp.float32, precision=lax.Precision.HIGHEST).astype(jnp.bfloat16)
    spectrum = spectrum.reshape(GATHERS, NH, 2 * NF)
    real_all = jnp.transpose(spectrum[:, :, :NF], (2, 1, 0))
    imag_all = jnp.transpose(spectrum[:, :, NF:], (2, 1, 0))
    delays = moveout(slowness_index, offset_index)

    def one_frequency(inputs):
        freq_one, real_in, imag_in = inputs
        angular = (2 * freq_one + 1).astype(jnp.float32) * (math.pi / NT)
        phases = angular * delays
        cosine = jnp.cos(phases).astype(jnp.bfloat16).astype(jnp.float32)
        sines = jnp.sin(phases).astype(jnp.bfloat16).astype(jnp.float32)
        real_data = real_in.astype(jnp.float32)
        imag_data = imag_in.astype(jnp.float32)
        high = lax.Precision.HIGHEST
        real_out = jnp.dot(cosine, real_data, precision=high) - jnp.dot(sines, imag_data, precision=high)
        imag_out = jnp.dot(sines, real_data, precision=high) + jnp.dot(cosine, imag_data, precision=high)
        return jnp.concatenate([real_out, imag_out], axis=1)
    panel = lax.map(one_frequency, (jnp.arange(NF, dtype=jnp.int32), real_all, imag_all))
    return jnp.transpose(panel, (1, 0, 2)) * (1.0 / math.sqrt(NH))
```

```python
import functools
import math

import jax
import jax.numpy as jnp
import ml_dtypes
import numpy as np
from jax import lax
from jax.experimental import pallas as pl
from jax.experimental.pallas import tpu as pltpu
from jax.sharding import PartitionSpec as P

NF = 1024
NP = 256
APEX_TIME = 100.0
CURVATURE = 0.0003
MIB = 1 << 20


def table_rows(total_time, freq_devices, offset_devices, halves, pairs):
    band = NF // freq_devices
    f, o, k, a = np.meshgrid(
        np.arange(freq_devices),
        np.arange(offset_devices),
        np.arange(pairs),
        np.arange(halves),
        indexing="ij",
    )
    freq_ids = (f * band + a * (band // halves) + o * pairs + k).reshape(-1)
    turns = (2 * freq_ids[:, None] + 1) * np.arange(total_time)[None, :] % (2 * total_time)
    angles = turns.astype(np.float32) * np.float32(math.pi / total_time)
    both = np.stack([np.cos(angles), -np.sin(angles)], axis=1).reshape(-1, total_time)
    return (both / np.float32(math.sqrt(total_time))).astype(ml_dtypes.bfloat16)


def transform_kernel(table_ref, series_ref, out_ref):
    blocks, _, local_times = series_ref.shape
    total = None
    for b in range(blocks):
        part = lax.dot_general(
            table_ref[:, b * local_times : (b + 1) * local_times],
            series_ref[b],
            (((1,), (1,)), ((), ())),
            preferred_element_type=jnp.float32,
        )
        total = part if total is None else total + part
    out_ref[...] = total.astype(out_ref.dtype)


def transform(table, series):
    columns, total_time = table.shape
    blocks, rows, local_times = series.shape
    step = min(columns, 256)
    return pl.pallas_call(
        transform_kernel,
        grid=(columns // step,),
        in_specs=[
            pl.BlockSpec((step, total_time), lambda i: (i, 0)),
            pl.BlockSpec((blocks, rows, local_times), lambda i: (0, 0, 0)),
        ],
        out_specs=pl.BlockSpec((step, rows), lambda i: (i, 0)),
        out_shape=jax.ShapeDtypeStruct((columns, rows), jnp.bfloat16),
        compiler_params=pltpu.CompilerParams(vmem_limit_bytes=32 * MIB),
    )(table, series)


def radon_kernel(shift, total_time, base_ref, slow_ref, offs_ref, data_ref, out_ref, cs, sn, tc, ts, held):
    pairs = data_ref.shape[0]
    slows = slow_ref.shape[0]
    half_lanes = data_ref.shape[2] // 2
    quarter = half_lanes // 2
    spread = CURVATURE * slow_ref[...] * offs_ref[...]
    delay = jnp.sqrt(APEX_TIME * APEX_TIME + spread * spread) - APEX_TIME
    phase = base_ref[0] * delay
    cs[0] = jnp.cos(phase)
    sn[0] = jnp.sin(phase)
    turn = delay * (2.0 * math.pi / total_time)
    tc[...] = jnp.cos(turn)
    ts[...] = jnp.sin(turn)
    far = delay * (2.0 * shift * math.pi / total_time)
    far_c = jnp.cos(far)
    far_s = jnp.sin(far)
    cs[1] = cs[0] * far_c - sn[0] * far_s
    sn[1] = sn[0] * far_c + cs[0] * far_s
    lane = lax.broadcasted_iota(jnp.int32, (1, data_ref.shape[2]), 1)
    first_half = lane < half_lanes
    real_lane = lane % half_lanes < quarter

    def step(k, carry):
        data = data_ref[k]
        wide = data.astype(jnp.float32)
        turned = jnp.where(
            real_lane,
            -pltpu.roll(wide, data_ref.shape[2] - quarter, 1),
            pltpu.roll(wide, quarter, 1),
        ).astype(jnp.bfloat16)
        results = []
        for a in range(2):
            c = cs[a]
            s = sn[a]
            results.append(
                jnp.dot(c.astype(jnp.bfloat16), data, preferred_element_type=jnp.float32)
                + jnp.dot(s.astype(jnp.bfloat16), turned, preferred_element_type=jnp.float32)
            )
            cs[a] = c * tc[...] - s * ts[...]
            sn[a] = s * tc[...] + c * ts[...]
        held[pl.ds(k, slows, stride=pairs), :] = jnp.where(first_half, results[0], results[1])
        return carry

    lax.fori_loop(0, pairs, step, 0)
    out_ref[...] = held[...].astype(out_ref.dtype)


def radon(base, slows, offs, data, shift, total_time):
    pairs, offsets, lanes = data.shape
    count = slows.shape[0]
    vmem = pl.BlockSpec(memory_space=pltpu.VMEM)
    return pl.pallas_call(
        functools.partial(radon_kernel, shift, total_time),
        in_specs=[pl.BlockSpec(memory_space=pltpu.SMEM), vmem, vmem, vmem],
        out_specs=vmem,
        out_shape=jax.ShapeDtypeStruct((count * pairs, lanes), jnp.bfloat16),
        scratch_shapes=[
            pltpu.VMEM((2, count, offsets), jnp.float32),
            pltpu.VMEM((2, count, offsets), jnp.float32),
            pltpu.VMEM((count, offsets), jnp.float32),
            pltpu.VMEM((count, offsets), jnp.float32),
            pltpu.VMEM((count * pairs, lanes), jnp.float32),
        ],
        compiler_params=pltpu.CompilerParams(vmem_limit_bytes=40 * MIB),
    )(base, slows, offs, data)


def finish_kernel(scale, in_ref, out_ref):
    devices, slows, pairs, lanes = in_ref.shape
    rows = devices * pairs
    for p in range(slows):
        block = in_ref[:, p].reshape(rows, lanes).astype(jnp.float32) * scale
        turned = block.T
        out_ref[p, :, :rows] = turned[: lanes // 2]
        out_ref[p, :, rows:] = turned[lanes // 2 :]


def finish(parts, scale):
    devices, slows, pairs, lanes = parts.shape
    rows = devices * pairs
    step = 8
    return pl.pallas_call(
        functools.partial(finish_kernel, scale),
        grid=(slows // step,),
        in_specs=[pl.BlockSpec((devices, step, pairs, lanes), lambda i: (0, i, 0, 0))],
        out_specs=pl.BlockSpec((step, lanes // 2, 2 * rows), lambda i: (i, 0, 0)),
        out_shape=jax.ShapeDtypeStruct((slows, lanes // 2, 2 * rows), jnp.float32),
        compiler_params=pltpu.CompilerParams(vmem_limit_bytes=32 * MIB),
    )(parts)


def local(raw_traces, trace_slot, offset_index, slowness_index):
    gathers, local_offsets = trace_slot.shape
    local_times = raw_traces.shape[1]
    freq_devices = lax.axis_size("freq")
    offset_devices = lax.axis_size("offset")
    devices = freq_devices * offset_devices
    total_time = local_times * freq_devices
    offsets = local_offsets * offset_devices
    band = NF // freq_devices
    own_freqs = NF // devices
    halves = 2
    pairs = own_freqs // halves
    own_offsets = local_offsets // freq_devices
    rows = own_offsets * gathers

    picked = raw_traces[trace_slot.T.reshape(-1)]
    series = lax.all_to_all(
        picked.reshape(freq_devices, rows, local_times), "freq", 0, 0, tiled=True
    )
    table = jnp.asarray(table_rows(total_time, freq_devices, offset_devices, halves, pairs))
    spectrum = transform(table, series).reshape(devices, 2 * own_freqs, rows)
    spectra = lax.all_to_all(spectrum, ("freq", "offset"), 0, 0, tiled=True)
    data = spectra.reshape(devices, pairs, 2 * halves, own_offsets, gathers)
    data = data.transpose(1, 0, 3, 2, 4).reshape(pairs, offsets, 2 * halves * gathers)

    offs = offset_index.reshape(offset_devices, freq_devices, own_offsets)
    offs = offs.transpose(1, 0, 2).reshape(1, offsets).astype(jnp.float32)
    slows = slowness_index.astype(jnp.float32)[:, None]
    first = lax.axis_index("freq") * band + lax.axis_index("offset") * pairs
    base = (2 * first + 1).astype(jnp.float32) * (math.pi / total_time)
    panel = radon(base.reshape(1), slows, offs, data, band // halves, total_time)
    panel = panel.reshape(offset_devices, NP // offset_devices, pairs, 2 * halves * gathers)
    parts = lax.all_to_all(panel, "offset", 0, 0, tiled=True)
    result = finish(parts, 1.0 / math.sqrt(offsets))
    return jnp.transpose(result, (0, 2, 1))


def solution(mesh):
    placed = (P("offset", "freq"), P(None, "offset"), P(), P())
    return jax.shard_map(
        local, mesh=mesh, in_specs=placed, out_specs=P("offset", "freq", None), check_vma=False
    )
```

```python
import functools
import math

import jax
import jax.numpy as jnp
import ml_dtypes
import numpy as np
from jax import lax
from jax.experimental import pallas as pl
from jax.experimental.pallas import tpu as pltpu
from jax.sharding import PartitionSpec as P

NF = 1024
NP = 256
APEX_TIME = 100.0
CURVATURE = 0.0003
MIB = 1 << 20


def table_rows(total_time, freq_devices, offset_devices, halves, pairs):
    band = NF // freq_devices
    f, o, a, k = np.meshgrid(
        np.arange(freq_devices),
        np.arange(offset_devices),
        np.arange(halves),
        np.arange(pairs),
        indexing="ij",
    )
    freq_ids = (f * band + a * (band // halves) + o * pairs + k).reshape(-1, pairs)
    turns = (2 * freq_ids[..., None] + 1) * np.arange(total_time) % (2 * total_time)
    angles = turns.astype(np.float32) * np.float32(math.pi / total_time)
    both = np.stack([np.cos(angles), -np.sin(angles)], axis=1).reshape(-1, total_time)
    return (both / np.float32(math.sqrt(total_time))).astype(ml_dtypes.bfloat16)


def transform_kernel(table_ref, series_ref, out_ref, held, sems):
    blocks, _, local_times = series_ref.shape
    chunks, step, _ = held.shape
    copies = [
        pltpu.make_async_copy(table_ref.at[pl.ds(i * step, step)], held.at[i], sems.at[i])
        for i in range(chunks)
    ]
    for copy in copies:
        copy.start()
    for i in range(chunks):
        copies[i].wait()
        total = None
        for b in range(blocks):
            part = lax.dot_general(
                held[i, :, b * local_times : (b + 1) * local_times],
                series_ref[b],
                (((1,), (1,)), ((), ())),
                preferred_element_type=jnp.float32,
            )
            total = part if total is None else total + part
        out_ref[i * step : (i + 1) * step] = total.astype(out_ref.dtype)


def transform(table, series):
    columns, total_time = table.shape
    blocks, rows, local_times = series.shape
    chunks = 4
    vmem = pl.BlockSpec(memory_space=pltpu.VMEM)
    return pl.pallas_call(
        transform_kernel,
        in_specs=[pl.BlockSpec(memory_space=pltpu.HBM), vmem],
        out_specs=vmem,
        out_shape=jax.ShapeDtypeStruct((columns, rows), jnp.bfloat16),
        scratch_shapes=[
            pltpu.VMEM((chunks, columns // chunks, total_time), jnp.bfloat16),
            pltpu.SemaphoreType.DMA((chunks,)),
        ],
        compiler_params=pltpu.CompilerParams(vmem_limit_bytes=32 * MIB),
    )(table, series)


def moveout_kernel(shift, total_time, base_ref, slow_ref, offs_ref, out_ref, cs, sn, tc, ts):
    @pl.when(pl.program_id(0) == 0)
    def start():
        spread = CURVATURE * slow_ref[...] * offs_ref[...]
        delay = jnp.sqrt(APEX_TIME * APEX_TIME + spread * spread) - APEX_TIME
        phase = base_ref[0] * delay
        cs[0] = jnp.cos(phase)
        sn[0] = jnp.sin(phase)
        turn = delay * (2.0 * math.pi / total_time)
        tc[...] = jnp.cos(turn)
        ts[...] = jnp.sin(turn)
        far = delay * (2.0 * shift * math.pi / total_time)
        far_c = jnp.cos(far)
        far_s = jnp.sin(far)
        cs[1] = cs[0] * far_c - sn[0] * far_s
        sn[1] = sn[0] * far_c + cs[0] * far_s

    for a in range(2):
        c = cs[a]
        s = sn[a]
        out_ref[0, 2 * a] = c.astype(out_ref.dtype)
        out_ref[0, 2 * a + 1] = s.astype(out_ref.dtype)
        cs[a] = c * tc[...] - s * ts[...]
        sn[a] = s * tc[...] + c * ts[...]


def moveout(base, slows, offs, pairs, shift, total_time):
    count = slows.shape[0]
    offsets = offs.shape[1]
    return pl.pallas_call(
        functools.partial(moveout_kernel, shift, total_time),
        grid=(pairs,),
        in_specs=[
            pl.BlockSpec(memory_space=pltpu.SMEM),
            pl.BlockSpec((count, 1), lambda k: (0, 0)),
            pl.BlockSpec((1, offsets), lambda k: (0, 0)),
        ],
        out_specs=pl.BlockSpec((1, 4, count, offsets), lambda k: (k, 0, 0, 0)),
        out_shape=jax.ShapeDtypeStruct((pairs, 4, count, offsets), jnp.bfloat16),
        scratch_shapes=[
            pltpu.VMEM((2, count, offsets), jnp.float32),
            pltpu.VMEM((2, count, offsets), jnp.float32),
            pltpu.VMEM((count, offsets), jnp.float32),
            pltpu.VMEM((count, offsets), jnp.float32),
        ],
        compiler_params=pltpu.CompilerParams(vmem_limit_bytes=24 * MIB),
        cost_estimate=pl.CostEstimate(
            flops=pairs * 40 * count * offsets,
            bytes_accessed=pairs * 8 * count * offsets,
            transcendentals=6 * count * offsets,
        ),
    )(base, slows, offs)


def regroup(data_ref, wide, gathers):
    devices, blocks, pairs, rows = data_ref.shape
    lanes = blocks * gathers
    own_offsets = rows // gathers

    def exact(d, carry):
        for h in range(own_offsets):
            cut = [
                data_ref[d, c, :, h * gathers : (h + 1) * gathers].astype(jnp.float32)
                for c in range(blocks)
            ]
            start = pl.multiple_of((d * own_offsets + h) * pairs, pairs)
            wide[pl.ds(start, pairs), :] = jnp.concatenate(cut, axis=1)
        return carry

    lane = lax.broadcasted_iota(jnp.int32, (1, lanes), 1)
    low_half = lane < 2 * gathers
    low_part = lane % (2 * gathers) < gathers

    def rolled(d, carry):
        for q in range(rows // lanes):
            x = [
                data_ref[d, c, :, q * lanes : (q + 1) * lanes].astype(jnp.float32)
                for c in range(blocks)
            ]
            for top in range(2):
                pair = []
                for part in range(2):
                    a, b = x[part], x[2 + part]
                    if top == 0:
                        pair.append(jnp.where(low_half, a, pltpu.roll(b, 2 * gathers, 1)))
                    else:
                        pair.append(jnp.where(low_half, pltpu.roll(a, 2 * gathers, 1), b))
                outs = (
                    jnp.where(low_part, pair[0], pltpu.roll(pair[1], gathers, 1)),
                    jnp.where(low_part, pltpu.roll(pair[0], lanes - gathers, 1), pair[1]),
                )
                for bit in range(2):
                    h = 4 * q + 2 * top + bit
                    start = pl.multiple_of((d * own_offsets + h) * pairs, pairs)
                    wide[pl.ds(start, pairs), :] = outs[bit]
        return carry

    lax.fori_loop(0, devices, rolled if rows % lanes == 0 else exact, 0, unroll=2)


def radon_kernel(gathers, turn_ref, data_ref, out_ref, wide, held):
    k = pl.program_id(0)
    pairs = data_ref.shape[2]
    lanes = wide.shape[1]
    offsets = wide.shape[0] // pairs
    slows = turn_ref.shape[2]

    @pl.when(k == 0)
    def start():
        regroup(data_ref, wide, gathers)

    lane = lax.broadcasted_iota(jnp.int32, (1, lanes), 1)
    first_half = lane < 2 * gathers
    real_lane = lane % (2 * gathers) < gathers
    block = wide[pl.ds(k, offsets, stride=pairs), :]
    turned = jnp.where(
        real_lane, -pltpu.roll(block, lanes - gathers, 1), pltpu.roll(block, gathers, 1)
    ).astype(jnp.bfloat16)
    data = block.astype(jnp.bfloat16)
    results = [
        jnp.dot(turn_ref[0, 2 * a], data, preferred_element_type=jnp.float32)
        + jnp.dot(turn_ref[0, 2 * a + 1], turned, preferred_element_type=jnp.float32)
        for a in range(2)
    ]
    held[pl.ds(k, slows, stride=pairs), :] = jnp.where(first_half, results[0], results[1])

    @pl.when(k == pairs - 1)
    def end():
        out_ref[...] = held[...].astype(out_ref.dtype)


def radon(turns, data, gathers):
    pairs, parts, count, offsets = turns.shape
    lanes = parts * gathers
    return pl.pallas_call(
        functools.partial(radon_kernel, gathers),
        grid=(pairs,),
        in_specs=[
            pl.BlockSpec((1, parts, count, offsets), lambda k: (k, 0, 0, 0)),
            pl.BlockSpec(data.shape, lambda k: (0, 0, 0, 0)),
        ],
        out_specs=pl.BlockSpec((count * pairs, lanes), lambda k: (0, 0)),
        out_shape=jax.ShapeDtypeStruct((count * pairs, lanes), jnp.bfloat16),
        scratch_shapes=[
            pltpu.VMEM((offsets * pairs, lanes), jnp.float32),
            pltpu.VMEM((count * pairs, lanes), jnp.float32),
        ],
        compiler_params=pltpu.CompilerParams(vmem_limit_bytes=24 * MIB),
    )(turns, data)


def finish_kernel(scale, in_ref, out_ref):
    devices, slows, pairs, lanes = in_ref.shape
    rows = devices * pairs
    for p in range(slows):
        block = in_ref[:, p].reshape(rows, lanes).astype(jnp.float32) * scale
        turned = block.T
        out_ref[p, :, :rows] = turned[: lanes // 2]
        out_ref[p, :, rows:] = turned[lanes // 2 :]


def finish(parts, scale):
    devices, slows, pairs, lanes = parts.shape
    rows = devices * pairs
    step = 8
    return pl.pallas_call(
        functools.partial(finish_kernel, scale),
        grid=(slows // step,),
        in_specs=[pl.BlockSpec((devices, step, pairs, lanes), lambda i: (0, i, 0, 0))],
        out_specs=pl.BlockSpec((step, lanes // 2, 2 * rows), lambda i: (i, 0, 0)),
        out_shape=jax.ShapeDtypeStruct((slows, lanes // 2, 2 * rows), jnp.float32),
        compiler_params=pltpu.CompilerParams(vmem_limit_bytes=32 * MIB),
    )(parts)


def local(raw_traces, trace_slot, offset_index, slowness_index):
    gathers, local_offsets = trace_slot.shape
    local_times = raw_traces.shape[1]
    freq_devices = lax.axis_size("freq")
    offset_devices = lax.axis_size("offset")
    devices = freq_devices * offset_devices
    total_time = local_times * freq_devices
    offsets = local_offsets * offset_devices
    band = NF // freq_devices
    own_freqs = NF // devices
    halves = 2
    pairs = own_freqs // halves
    own_offsets = local_offsets // freq_devices
    rows = own_offsets * gathers

    picked = raw_traces[trace_slot.T.reshape(-1)]
    series = lax.all_to_all(
        picked.reshape(freq_devices, rows, local_times), "freq", 0, 0, tiled=True
    )
    table = jnp.asarray(table_rows(total_time, freq_devices, offset_devices, halves, pairs))
    spectrum = transform(table, series).reshape(devices, 2 * own_freqs, rows)
    spectra = lax.all_to_all(spectrum, ("freq", "offset"), 0, 0, tiled=True)
    data = spectra.reshape(devices, 2 * halves, pairs, rows)

    offs = offset_index.reshape(offset_devices, freq_devices, own_offsets)
    offs = offs.transpose(1, 0, 2).reshape(1, offsets).astype(jnp.float32)
    slows = slowness_index.astype(jnp.float32)[:, None]
    first = lax.axis_index("freq") * band + lax.axis_index("offset") * pairs
    base = (2 * first + 1).astype(jnp.float32) * (math.pi / total_time)
    turns = moveout(base.reshape(1), slows, offs, pairs, band // halves, total_time)
    panel = radon(turns, data, gathers)
    panel = panel.reshape(offset_devices, NP // offset_devices, pairs, 2 * halves * gathers)
    parts = lax.all_to_all(panel, "offset", 0, 0, tiled=True)
    result = finish(parts, 1.0 / math.sqrt(offsets))
    return jnp.transpose(result, (0, 2, 1))


def solution(mesh):
    placed = (P("offset", "freq"), P(None, "offset"), P(), P())
    return jax.shard_map(
        local, mesh=mesh, in_specs=placed, out_specs=P("offset", "freq", None), check_vma=False
    )
```

```python
import functools
import math

import jax
import jax.numpy as jnp
import ml_dtypes
import numpy as np
from jax import lax
from jax.experimental import pallas as pl
from jax.experimental.pallas import tpu as pltpu
from jax.sharding import PartitionSpec as P

NF = 1024
NP = 256
APEX_TIME = 100.0
CURVATURE = 0.0003
MIB = 1 << 20


def table_rows(total_time, freq_devices, offset_devices, halves, pairs):
    band = NF // freq_devices
    f, o, a, k = np.meshgrid(
        np.arange(freq_devices),
        np.arange(offset_devices),
        np.arange(halves),
        np.arange(pairs),
        indexing="ij",
    )
    freq_ids = (f * band + a * (band // halves) + o * pairs + k).reshape(-1, pairs)
    turns = (2 * freq_ids[..., None] + 1) * np.arange(total_time) % (2 * total_time)
    angles = turns.astype(np.float32) * np.float32(math.pi / total_time)
    both = np.stack([np.cos(angles), -np.sin(angles)], axis=1).reshape(-1, total_time)
    return (both / np.float32(math.sqrt(total_time))).astype(ml_dtypes.bfloat16)


def pick_kernel(slot_ref, raw_ref, out_ref):
    gathers = slot_ref.shape[0]
    groups, rows, _ = out_ref.shape
    own_offsets = rows // gathers
    lane = lax.broadcasted_iota(jnp.int32, (gathers, raw_ref.shape[0]), 1)
    for f in range(groups):
        picks = [
            jnp.where(lane == slot_ref[:, h : h + 1], 1.0, 0.0).astype(jnp.bfloat16)
            for h in range(f * own_offsets, (f + 1) * own_offsets)
        ]
        out_ref[f] = jnp.dot(
            jnp.concatenate(picks, axis=0), raw_ref[...], preferred_element_type=jnp.float32
        ).astype(out_ref.dtype)


def pick(trace_slot, raw_traces, groups):
    gathers, local_offsets = trace_slot.shape
    rows = gathers * local_offsets // groups
    vmem = pl.BlockSpec(memory_space=pltpu.VMEM)
    return pl.pallas_call(
        pick_kernel,
        in_specs=[vmem, vmem],
        out_specs=vmem,
        out_shape=jax.ShapeDtypeStruct((groups, rows, raw_traces.shape[1]), raw_traces.dtype),
        compiler_params=pltpu.CompilerParams(vmem_limit_bytes=32 * MIB),
    )(trace_slot, raw_traces)


def regroup(total, pairs, gathers):
    lanes = 4 * gathers
    lane = lax.broadcasted_iota(jnp.int32, (1, lanes), 1)
    low_half = lane < 2 * gathers
    low_part = lane % (2 * gathers) < gathers
    found = []
    for q in range(total.shape[1] // lanes):
        x = [total[c * pairs : (c + 1) * pairs, q * lanes : (q + 1) * lanes] for c in range(4)]
        for top in range(2):
            pair = []
            for part in range(2):
                a, b = x[part], x[2 + part]
                if top == 0:
                    pair.append(jnp.where(low_half, a, pltpu.roll(b, 2 * gathers, 1)))
                else:
                    pair.append(jnp.where(low_half, pltpu.roll(a, 2 * gathers, 1), b))
            found.append(jnp.where(low_part, pair[0], pltpu.roll(pair[1], gathers, 1)))
            found.append(jnp.where(low_part, pltpu.roll(pair[0], lanes - gathers, 1), pair[1]))
    return found


def transform_kernel(pairs, gathers, table_ref, series_ref, out_ref, held, sems):
    blocks, rows, local_times = series_ref.shape
    chunks, step, _ = held.shape
    copies = [
        pltpu.make_async_copy(table_ref.at[pl.ds(i * step, step)], held.at[i], sems.at[i])
        for i in range(chunks)
    ]
    for copy in copies:
        copy.start()
    for i in range(chunks):
        copies[i].wait()
        total = None
        for b in range(blocks):
            part = lax.dot_general(
                held[i, :, b * local_times : (b + 1) * local_times],
                series_ref[b],
                (((1,), (1,)), ((), ())),
                preferred_element_type=jnp.float32,
            )
            total = part if total is None else total + part
        if len(out_ref.shape) == 2:
            out_ref[i * step : (i + 1) * step] = total.astype(out_ref.dtype)
            continue
        targets = step // (4 * pairs)
        for d in range(targets):
            found = regroup(total[d * 4 * pairs : (d + 1) * 4 * pairs], pairs, gathers)
            for h, value in enumerate(found):
                out_ref[i * targets + d, h] = value.astype(out_ref.dtype)


def transform(table, series, pairs, gathers):
    columns, total_time = table.shape
    blocks, rows, local_times = series.shape
    devices = columns // (4 * pairs)
    final = (devices, rows // gathers, pairs, 4 * gathers)
    chunks = 4
    aligned = rows % (4 * gathers) == 0 and pairs % 8 == 0 and devices % chunks == 0
    vmem = pl.BlockSpec(memory_space=pltpu.VMEM)
    out = pl.pallas_call(
        functools.partial(transform_kernel, pairs, gathers),
        in_specs=[pl.BlockSpec(memory_space=pl.ANY), vmem],
        out_specs=vmem,
        out_shape=jax.ShapeDtypeStruct(final if aligned else (columns, rows), jnp.bfloat16),
        scratch_shapes=[
            pltpu.VMEM((chunks, columns // chunks, total_time), jnp.bfloat16),
            pltpu.SemaphoreType.DMA((chunks,)),
        ],
        compiler_params=pltpu.CompilerParams(vmem_limit_bytes=56 * MIB),
    )(table, series)
    if aligned:
        return out
    out = out.reshape(devices, 4, pairs, rows // gathers, gathers)
    return out.transpose(0, 3, 2, 1, 4).reshape(final)


def moveout_kernel(shift, total_time, base_ref, slow_ref, offs_ref, out_ref, cs, sn, tc, ts):
    @pl.when(pl.program_id(0) == 0)
    def start():
        spread = CURVATURE * slow_ref[...] * offs_ref[...]
        delay = jnp.sqrt(APEX_TIME * APEX_TIME + spread * spread) - APEX_TIME
        phase = base_ref[0] * delay
        cs[0] = jnp.cos(phase)
        sn[0] = jnp.sin(phase)
        turn = delay * (2.0 * math.pi / total_time)
        tc[...] = jnp.cos(turn)
        ts[...] = jnp.sin(turn)
        far = delay * (2.0 * shift * math.pi / total_time)
        far_c = jnp.cos(far)
        far_s = jnp.sin(far)
        cs[1] = cs[0] * far_c - sn[0] * far_s
        sn[1] = sn[0] * far_c + cs[0] * far_s

    for a in range(2):
        c = cs[a]
        s = sn[a]
        out_ref[0, a] = c.astype(out_ref.dtype)
        out_ref[0, 2 + a] = s.astype(out_ref.dtype)
        cs[a] = c * tc[...] - s * ts[...]
        sn[a] = s * tc[...] + c * ts[...]


def moveout(base, slows, offs, pairs, shift, total_time):
    count = slows.shape[0]
    offsets = offs.shape[1]
    return pl.pallas_call(
        functools.partial(moveout_kernel, shift, total_time),
        grid=(pairs,),
        in_specs=[
            pl.BlockSpec(memory_space=pltpu.SMEM),
            pl.BlockSpec((count, 1), lambda k: (0, 0)),
            pl.BlockSpec((1, offsets), lambda k: (0, 0)),
        ],
        out_specs=pl.BlockSpec((1, 4, count, offsets), lambda k: (k, 0, 0, 0)),
        out_shape=jax.ShapeDtypeStruct((pairs, 4, count, offsets), jnp.bfloat16),
        scratch_shapes=[
            pltpu.VMEM((2, count, offsets), jnp.float32),
            pltpu.VMEM((2, count, offsets), jnp.float32),
            pltpu.VMEM((count, offsets), jnp.float32),
            pltpu.VMEM((count, offsets), jnp.float32),
        ],
        compiler_params=pltpu.CompilerParams(vmem_limit_bytes=56 * MIB),
        cost_estimate=pl.CostEstimate(
            flops=pairs * 40 * count * offsets,
            bytes_accessed=pairs * 8 * count * offsets,
            transcendentals=6 * count * offsets,
        ),
    )(base, slows, offs)


def radon_kernel(gathers, turn_ref, data_ref, out_ref, wide, held):
    step = pl.program_id(0)
    devices, own_offsets, pairs, lanes = data_ref.shape
    offsets = devices * own_offsets
    group, _, slows, _ = turn_ref.shape

    @pl.when(step == 0)
    def start():
        wide[...] = data_ref[...].reshape(offsets * pairs, lanes).astype(jnp.float32)

    lane = lax.broadcasted_iota(jnp.int32, (1, lanes), 1)
    first_half = lane < 2 * gathers
    real_lane = lane % (2 * gathers) < gathers
    for i in range(group):
        k = step * group + i
        block = wide[pl.ds(k, offsets, stride=pairs), :]
        turned = jnp.where(
            real_lane, -pltpu.roll(block, lanes - gathers, 1), pltpu.roll(block, gathers, 1)
        ).astype(jnp.bfloat16)
        data = block.astype(jnp.bfloat16)
        cosine = turn_ref[i, :2].reshape(2 * slows, offsets)
        sines = turn_ref[i, 2:].reshape(2 * slows, offsets)
        both = jnp.dot(cosine, data, preferred_element_type=jnp.float32) + jnp.dot(
            sines, turned, preferred_element_type=jnp.float32
        )
        held[pl.ds(k, slows, stride=pairs), :] = jnp.where(first_half, both[:slows], both[slows:])

    @pl.when(step == pairs // group - 1)
    def end():
        out_ref[...] = held[...].astype(out_ref.dtype)


def radon(turns, data, gathers):
    pairs, parts, count, offsets = turns.shape
    lanes = parts * gathers
    group = 2 if pairs % 2 == 0 else 1
    return pl.pallas_call(
        functools.partial(radon_kernel, gathers),
        grid=(pairs // group,),
        in_specs=[
            pl.BlockSpec((group, parts, count, offsets), lambda k: (k, 0, 0, 0)),
            pl.BlockSpec(data.shape, lambda k: (0, 0, 0, 0)),
        ],
        out_specs=pl.BlockSpec((count * pairs, lanes), lambda k: (0, 0)),
        out_shape=jax.ShapeDtypeStruct((count * pairs, lanes), jnp.bfloat16),
        scratch_shapes=[
            pltpu.VMEM((offsets * pairs, lanes), jnp.float32),
            pltpu.VMEM((count * pairs, lanes), jnp.float32),
        ],
        compiler_params=pltpu.CompilerParams(vmem_limit_bytes=56 * MIB),
    )(turns, data)


def finish_kernel(scale, in_ref, out_ref):
    devices, slows, pairs, lanes = in_ref.shape
    rows = devices * pairs
    for p in range(slows):
        block = in_ref[:, p].reshape(rows, lanes).astype(jnp.float32) * scale
        turned = block.T
        out_ref[p, :, :rows] = turned[: lanes // 2]
        out_ref[p, :, rows:] = turned[lanes // 2 :]


def finish(parts, scale):
    devices, slows, pairs, lanes = parts.shape
    rows = devices * pairs
    step = 8
    return pl.pallas_call(
        functools.partial(finish_kernel, scale),
        grid=(slows // step,),
        in_specs=[pl.BlockSpec((devices, step, pairs, lanes), lambda i: (0, i, 0, 0))],
        out_specs=pl.BlockSpec((step, lanes // 2, 2 * rows), lambda i: (i, 0, 0)),
        out_shape=jax.ShapeDtypeStruct((slows, lanes // 2, 2 * rows), jnp.float32),
        compiler_params=pltpu.CompilerParams(vmem_limit_bytes=32 * MIB),
    )(parts)


def local(raw_traces, trace_slot, offset_index, slowness_index):
    gathers, local_offsets = trace_slot.shape
    local_times = raw_traces.shape[1]
    freq_devices = lax.axis_size("freq")
    offset_devices = lax.axis_size("offset")
    devices = freq_devices * offset_devices
    total_time = local_times * freq_devices
    offsets = local_offsets * offset_devices
    band = NF // freq_devices
    own_freqs = NF // devices
    halves = 2
    pairs = own_freqs // halves
    own_offsets = local_offsets // freq_devices

    picked = pick(trace_slot, raw_traces, freq_devices)
    series = lax.all_to_all(picked, "freq", 0, 0, tiled=True)
    table = jnp.asarray(table_rows(total_time, freq_devices, offset_devices, halves, pairs))
    spectrum = transform(table, series, pairs, gathers)
    data = lax.all_to_all(spectrum, ("freq", "offset"), 0, 0, tiled=True)

    offs = offset_index.reshape(offset_devices, freq_devices, own_offsets)
    offs = offs.transpose(1, 0, 2).reshape(1, offsets).astype(jnp.float32)
    slows = slowness_index.astype(jnp.float32)[:, None]
    first = lax.axis_index("freq") * band + lax.axis_index("offset") * pairs
    base = (2 * first + 1).astype(jnp.float32) * (math.pi / total_time)
    turns = moveout(base.reshape(1), slows, offs, pairs, band // halves, total_time)
    panel = radon(turns, data, gathers)
    panel = panel.reshape(offset_devices, NP // offset_devices, pairs, 2 * halves * gathers)
    parts = lax.all_to_all(panel, "offset", 0, 0, tiled=True)
    result = finish(parts, 1.0 / math.sqrt(offsets))
    return jnp.transpose(result, (0, 2, 1))


def solution(mesh):
    placed = (P("offset", "freq"), P(None, "offset"), P(), P())
    return jax.shard_map(
        local, mesh=mesh, in_specs=placed, out_specs=P("offset", "freq", None), check_vma=False
    )
```

```python
import functools
import math

import jax
import jax.numpy as jnp
import ml_dtypes
import numpy as np
from jax import lax
from jax.experimental import pallas as pl
from jax.experimental.pallas import tpu as pltpu
from jax.sharding import PartitionSpec as P

NF = 1024
NP = 256
APEX_TIME = 100.0
CURVATURE = 0.0003
MIB = 1 << 20


def table_rows(total_time, freq_devices, offset_devices, halves, pairs):
    band = NF // freq_devices
    f, o, a, k = np.meshgrid(
        np.arange(freq_devices),
        np.arange(offset_devices),
        np.arange(halves),
        np.arange(pairs),
        indexing="ij",
    )
    freq_ids = (f * band + a * (band // halves) + o * pairs + k).reshape(-1, pairs)
    turns = (2 * freq_ids[..., None] + 1) * np.arange(total_time) % (2 * total_time)
    angles = turns.astype(np.float32) * np.float32(math.pi / total_time)
    both = np.stack([np.cos(angles), -np.sin(angles)], axis=1).reshape(-1, total_time)
    return (both / np.float32(math.sqrt(total_time))).astype(ml_dtypes.bfloat16)


def pick_kernel(slot_ref, raw_ref, out_ref):
    gathers = slot_ref.shape[0]
    groups, rows, _ = out_ref.shape
    own_offsets = rows // gathers
    lane = lax.broadcasted_iota(jnp.int32, (gathers, raw_ref.shape[0]), 1)
    for f in range(groups):
        picks = [
            jnp.where(lane == slot_ref[:, h : h + 1], 1.0, 0.0).astype(jnp.bfloat16)
            for h in range(f * own_offsets, (f + 1) * own_offsets)
        ]
        out_ref[f] = jnp.dot(
            jnp.concatenate(picks, axis=0), raw_ref[...], preferred_element_type=jnp.float32
        ).astype(out_ref.dtype)


def pick(trace_slot, raw_traces, groups):
    gathers, local_offsets = trace_slot.shape
    rows = gathers * local_offsets // groups
    vmem = pl.BlockSpec(memory_space=pltpu.VMEM)
    return pl.pallas_call(
        pick_kernel,
        in_specs=[vmem, vmem],
        out_specs=vmem,
        out_shape=jax.ShapeDtypeStruct((groups, rows, raw_traces.shape[1]), raw_traces.dtype),
        compiler_params=pltpu.CompilerParams(vmem_limit_bytes=63 * MIB),
    )(trace_slot, raw_traces)


def regroup(total, pairs, gathers):
    lanes = 4 * gathers
    lane = lax.broadcasted_iota(jnp.int32, (1, lanes), 1)
    low_half = lane < 2 * gathers
    low_part = lane % (2 * gathers) < gathers
    found = []
    for q in range(total.shape[1] // lanes):
        x = [total[c * pairs : (c + 1) * pairs, q * lanes : (q + 1) * lanes] for c in range(4)]
        for top in range(2):
            pair = []
            for part in range(2):
                a, b = x[part], x[2 + part]
                if top == 0:
                    pair.append(jnp.where(low_half, a, pltpu.roll(b, 2 * gathers, 1)))
                else:
                    pair.append(jnp.where(low_half, pltpu.roll(a, 2 * gathers, 1), b))
            found.append(jnp.where(low_part, pair[0], pltpu.roll(pair[1], gathers, 1)))
            found.append(jnp.where(low_part, pltpu.roll(pair[0], lanes - gathers, 1), pair[1]))
    return found


def transform_kernel(pairs, gathers, table_ref, series_ref, out_ref, held, turned, sems):
    blocks, rows, local_times = series_ref.shape
    chunks, step, _ = held.shape
    copies = [
        pltpu.make_async_copy(table_ref.at[pl.ds(i * step, step)], held.at[i], sems.at[i])
        for i in range(chunks)
    ]
    for copy in copies:
        copy.start()
    for b in range(blocks):
        turned[b * local_times : (b + 1) * local_times] = series_ref[b].T
    for i in range(chunks):
        copies[i].wait()
        total = jnp.dot(held[i], turned[...], preferred_element_type=jnp.float32)
        if len(out_ref.shape) == 2:
            out_ref[i * step : (i + 1) * step] = total.astype(out_ref.dtype)
            continue
        targets = step // (4 * pairs)
        for d in range(targets):
            found = regroup(total[d * 4 * pairs : (d + 1) * 4 * pairs], pairs, gathers)
            for h, value in enumerate(found):
                out_ref[i * targets + d, h] = value.astype(out_ref.dtype)


def transform(table, series, pairs, gathers):
    columns, total_time = table.shape
    blocks, rows, local_times = series.shape
    devices = columns // (4 * pairs)
    final = (devices, rows // gathers, pairs, 4 * gathers)
    chunks = 4
    aligned = rows % (4 * gathers) == 0 and pairs % 8 == 0 and devices % chunks == 0
    vmem = pl.BlockSpec(memory_space=pltpu.VMEM)
    out = pl.pallas_call(
        functools.partial(transform_kernel, pairs, gathers),
        in_specs=[pl.BlockSpec(memory_space=pl.ANY), vmem],
        out_specs=vmem,
        out_shape=jax.ShapeDtypeStruct(final if aligned else (columns, rows), jnp.bfloat16),
        scratch_shapes=[
            pltpu.VMEM((chunks, columns // chunks, total_time), jnp.bfloat16),
            pltpu.VMEM((total_time, rows), jnp.bfloat16),
            pltpu.SemaphoreType.DMA((chunks,)),
        ],
        compiler_params=pltpu.CompilerParams(vmem_limit_bytes=56 * MIB),
    )(table, series)
    if aligned:
        return out
    out = out.reshape(devices, 4, pairs, rows // gathers, gathers)
    return out.transpose(0, 3, 2, 1, 4).reshape(final)


def moveout_kernel(shift, total_time, base_ref, slow_ref, offs_ref, out_ref, cs, sn, tc, ts):
    @pl.when(pl.program_id(0) == 0)
    def start():
        spread = CURVATURE * slow_ref[...] * offs_ref[...]
        delay = jnp.sqrt(APEX_TIME * APEX_TIME + spread * spread) - APEX_TIME
        phase = base_ref[0] * delay
        cs[0] = jnp.cos(phase)
        sn[0] = jnp.sin(phase)
        turn = delay * (2.0 * math.pi / total_time)
        tc[...] = jnp.cos(turn)
        ts[...] = jnp.sin(turn)
        far = delay * (2.0 * shift * math.pi / total_time)
        far_c = jnp.cos(far)
        far_s = jnp.sin(far)
        cs[1] = cs[0] * far_c - sn[0] * far_s
        sn[1] = sn[0] * far_c + cs[0] * far_s

    for a in range(2):
        c = cs[a]
        s = sn[a]
        out_ref[0, a] = c.astype(out_ref.dtype)
        out_ref[0, 2 + a] = s.astype(out_ref.dtype)
        cs[a] = c * tc[...] - s * ts[...]
        sn[a] = s * tc[...] + c * ts[...]


def moveout(base, slows, offs, pairs, shift, total_time):
    count = slows.shape[0]
    offsets = offs.shape[1]
    return pl.pallas_call(
        functools.partial(moveout_kernel, shift, total_time),
        grid=(pairs,),
        in_specs=[
            pl.BlockSpec(memory_space=pltpu.SMEM),
            pl.BlockSpec((count, 1), lambda k: (0, 0)),
            pl.BlockSpec((1, offsets), lambda k: (0, 0)),
        ],
        out_specs=pl.BlockSpec((1, 4, count, offsets), lambda k: (k, 0, 0, 0)),
        out_shape=jax.ShapeDtypeStruct((pairs, 4, count, offsets), jnp.bfloat16),
        scratch_shapes=[
            pltpu.VMEM((2, count, offsets), jnp.float32),
            pltpu.VMEM((2, count, offsets), jnp.float32),
            pltpu.VMEM((count, offsets), jnp.float32),
            pltpu.VMEM((count, offsets), jnp.float32),
        ],
        compiler_params=pltpu.CompilerParams(vmem_limit_bytes=56 * MIB),
        cost_estimate=pl.CostEstimate(
            flops=pairs * 40 * count * offsets,
            bytes_accessed=pairs * 8 * count * offsets,
            transcendentals=6 * count * offsets,
        ),
    )(base, slows, offs)


def one_hot(rows, columns, source):
    row = lax.broadcasted_iota(jnp.int32, (rows, columns), 0)
    column = lax.broadcasted_iota(jnp.int32, (rows, columns), 1)
    return jnp.where(column == source(row), 1.0, 0.0).astype(jnp.bfloat16)


def radon_kernel(gathers, turn_ref, data_ref, out_ref, plain, turned, held):
    step = pl.program_id(0)
    devices, own_offsets, pairs, lanes = data_ref.shape
    offsets = devices * own_offsets
    group, _, slows, _ = turn_ref.shape
    tile = 16

    @pl.when(step == 0)
    def start():
        size = tile * pairs
        together = tile // own_offsets
        swap = one_hot(size, size, lambda r: r % tile * pairs + r // tile)
        for d in range(devices // together):
            block = data_ref[d * together : (d + 1) * together].reshape(size, lanes)
            if pairs > 1:
                block = jnp.dot(swap, block, preferred_element_type=jnp.float32)
                block = block.astype(jnp.bfloat16)
            plain[:, d * tile : (d + 1) * tile] = block.reshape(pairs, tile, lanes)
        row = lax.broadcasted_iota(jnp.int32, (lanes, lanes), 0)
        column = lax.broadcasted_iota(jnp.int32, (lanes, lanes), 1)
        real_lane = column % (2 * gathers) < gathers
        quarter = jnp.where(
            real_lane,
            jnp.where(row == column + gathers, -1.0, 0.0),
            jnp.where(row == column - gathers, 1.0, 0.0),
        ).astype(jnp.bfloat16)
        for k in range(pairs):
            turned[k] = jnp.dot(plain[k], quarter, preferred_element_type=jnp.float32).astype(
                jnp.bfloat16
            )

    first_half = lax.broadcasted_iota(jnp.int32, (1, lanes), 1) < 2 * gathers
    for i in range(group):
        k = step * group + i
        cosine = turn_ref[i, :2].reshape(2 * slows, offsets)
        sines = turn_ref[i, 2:].reshape(2 * slows, offsets)
        both = jnp.dot(cosine, plain[k], preferred_element_type=jnp.float32) + jnp.dot(
            sines, turned[k], preferred_element_type=jnp.float32
        )
        held[k] = jnp.where(first_half, both[:slows], both[slows:]).astype(jnp.bfloat16)

    @pl.when(step == pairs // group - 1)
    def end():
        size = tile * pairs
        swap = one_hot(size, size, lambda r: r % pairs * tile + r // pairs)
        for p in range(slows // tile):
            block = held[:, p * tile : (p + 1) * tile].reshape(size, lanes)
            if pairs > 1:
                block = jnp.dot(swap, block, preferred_element_type=jnp.float32)
            out_ref[p * size : (p + 1) * size] = block.astype(out_ref.dtype)


def radon(turns, data, gathers):
    pairs, parts, count, offsets = turns.shape
    lanes = parts * gathers
    group = 2 if pairs % 2 == 0 else 1
    return pl.pallas_call(
        functools.partial(radon_kernel, gathers),
        grid=(pairs // group,),
        in_specs=[
            pl.BlockSpec((group, parts, count, offsets), lambda k: (k, 0, 0, 0)),
            pl.BlockSpec(data.shape, lambda k: (0, 0, 0, 0)),
        ],
        out_specs=pl.BlockSpec((count * pairs, lanes), lambda k: (0, 0)),
        out_shape=jax.ShapeDtypeStruct((count * pairs, lanes), jnp.bfloat16),
        scratch_shapes=[
            pltpu.VMEM((pairs, offsets, lanes), jnp.bfloat16),
            pltpu.VMEM((pairs, offsets, lanes), jnp.bfloat16),
            pltpu.VMEM((pairs, count, lanes), jnp.bfloat16),
        ],
        compiler_params=pltpu.CompilerParams(vmem_limit_bytes=63 * MIB),
    )(turns, data)


def finish_kernel(scale, in_ref, out_ref):
    devices, slows, pairs, lanes = in_ref.shape
    rows = devices * pairs
    for p in range(slows):
        block = in_ref[:, p].reshape(rows, lanes).astype(jnp.float32) * scale
        turned = block.T
        out_ref[p, :, :rows] = turned[: lanes // 2]
        out_ref[p, :, rows:] = turned[lanes // 2 :]


def finish(parts, scale):
    devices, slows, pairs, lanes = parts.shape
    rows = devices * pairs
    step = 8
    return pl.pallas_call(
        functools.partial(finish_kernel, scale),
        grid=(slows // step,),
        in_specs=[pl.BlockSpec((devices, step, pairs, lanes), lambda i: (0, i, 0, 0))],
        out_specs=pl.BlockSpec((step, lanes // 2, 2 * rows), lambda i: (i, 0, 0)),
        out_shape=jax.ShapeDtypeStruct((slows, lanes // 2, 2 * rows), jnp.float32),
        compiler_params=pltpu.CompilerParams(vmem_limit_bytes=32 * MIB),
    )(parts)


def local(raw_traces, trace_slot, offset_index, slowness_index):
    gathers, local_offsets = trace_slot.shape
    local_times = raw_traces.shape[1]
    freq_devices = lax.axis_size("freq")
    offset_devices = lax.axis_size("offset")
    devices = freq_devices * offset_devices
    total_time = local_times * freq_devices
    offsets = local_offsets * offset_devices
    band = NF // freq_devices
    own_freqs = NF // devices
    halves = 2
    pairs = own_freqs // halves
    own_offsets = local_offsets // freq_devices

    picked = pick(trace_slot, raw_traces, freq_devices)
    series = lax.all_to_all(picked, "freq", 0, 0, tiled=True)
    table = jnp.asarray(table_rows(total_time, freq_devices, offset_devices, halves, pairs))
    spectrum = transform(table, series, pairs, gathers)
    data = lax.all_to_all(spectrum, ("freq", "offset"), 0, 0, tiled=True)

    offs = offset_index.reshape(offset_devices, freq_devices, own_offsets)
    offs = offs.transpose(1, 0, 2).reshape(1, offsets).astype(jnp.float32)
    slows = slowness_index.astype(jnp.float32)[:, None]
    first = lax.axis_index("freq") * band + lax.axis_index("offset") * pairs
    base = (2 * first + 1).astype(jnp.float32) * (math.pi / total_time)
    turns = moveout(base.reshape(1), slows, offs, pairs, band // halves, total_time)
    panel = radon(turns, data, gathers)
    panel = panel.reshape(offset_devices, NP // offset_devices, pairs, 2 * halves * gathers)
    parts = lax.all_to_all(panel, "offset", 0, 0, tiled=True)
    result = finish(parts, 1.0 / math.sqrt(offsets))
    return jnp.transpose(result, (0, 2, 1))


def solution(mesh):
    placed = (P("offset", "freq"), P(None, "offset"), P(), P())
    return jax.shard_map(
        local, mesh=mesh, in_specs=placed, out_specs=P("offset", "freq", None), check_vma=False
    )
```

```python
import functools
import math

import jax
import jax.numpy as jnp
import ml_dtypes
import numpy as np
from jax import lax
from jax.experimental import pallas as pl
from jax.experimental.pallas import tpu as pltpu
from jax.sharding import PartitionSpec as P

NF = 1024
NP = 256
APEX_TIME = 100.0
CURVATURE = 0.0003
MIB = 1 << 20


def table_rows(total_time, freq_devices, offset_devices, halves, pairs):
    band = NF // freq_devices
    f, o, a, k = np.meshgrid(
        np.arange(freq_devices // 2),
        np.arange(offset_devices),
        np.arange(halves),
        np.arange(pairs),
        indexing="ij",
    )
    freq_ids = (f * band + a * (band // halves) + o * pairs + k).reshape(-1, pairs)
    times = np.concatenate([np.arange(0, total_time, 2), np.arange(1, total_time, 2)])
    turns = (2 * freq_ids[..., None] + 1) * times % (2 * total_time)
    angles = turns.astype(np.float32) * np.float32(math.pi / total_time)
    both = np.stack([np.cos(angles), -np.sin(angles)], axis=1).reshape(-1, total_time)
    return (both / np.float32(math.sqrt(total_time))).astype(ml_dtypes.bfloat16)


def pick_kernel(slot_ref, raw_ref, out_ref):
    gathers = slot_ref.shape[0]
    groups, rows, _ = out_ref.shape
    own_offsets = rows // gathers
    times = raw_ref.shape[1]
    half = times // 2
    row = lax.broadcasted_iota(jnp.int32, (times, times), 0)
    column = lax.broadcasted_iota(jnp.int32, (times, times), 1)
    source = jnp.where(column < half, 2 * column, 2 * (column - half) + 1)
    split = jnp.where(row == source, 1.0, 0.0).astype(jnp.bfloat16)
    raw = jnp.dot(raw_ref[...], split, preferred_element_type=jnp.float32).astype(jnp.bfloat16)
    lane = lax.broadcasted_iota(jnp.int32, (gathers, raw_ref.shape[0]), 1)
    for f in range(groups):
        picks = [
            jnp.where(lane == slot_ref[:, h : h + 1], 1.0, 0.0).astype(jnp.bfloat16)
            for h in range(f * own_offsets, (f + 1) * own_offsets)
        ]
        out_ref[f] = jnp.dot(
            jnp.concatenate(picks, axis=0), raw, preferred_element_type=jnp.float32
        ).astype(out_ref.dtype)


def pick(trace_slot, raw_traces, groups):
    gathers, local_offsets = trace_slot.shape
    rows = gathers * local_offsets // groups
    vmem = pl.BlockSpec(memory_space=pltpu.VMEM)
    return pl.pallas_call(
        pick_kernel,
        in_specs=[vmem, vmem],
        out_specs=vmem,
        out_shape=jax.ShapeDtypeStruct((groups, rows, raw_traces.shape[1]), raw_traces.dtype),
        compiler_params=pltpu.CompilerParams(vmem_limit_bytes=61 * MIB),
    )(trace_slot, raw_traces)


def regroup(parts, gathers):
    lanes = 4 * gathers
    lane = lax.broadcasted_iota(jnp.int32, (1, lanes), 1)
    low_half = lane < 2 * gathers
    low_part = lane % (2 * gathers) < gathers
    found = []
    for q in range(parts[0].shape[1] // lanes):
        x = [part[:, q * lanes : (q + 1) * lanes] for part in parts]
        for top in range(2):
            pair = []
            for part in range(2):
                a, b = x[part], x[2 + part]
                if top == 0:
                    pair.append(jnp.where(low_half, a, pltpu.roll(b, 2 * gathers, 1)))
                else:
                    pair.append(jnp.where(low_half, pltpu.roll(a, 2 * gathers, 1), b))
            found.append(jnp.where(low_part, pair[0], pltpu.roll(pair[1], gathers, 1)))
            found.append(jnp.where(low_part, pltpu.roll(pair[0], lanes - gathers, 1), pair[1]))
    return found


def transform_kernel(pairs, gathers, table_ref, series_ref, out_ref, held, even, odd, sems):
    blocks, rows, local_times = series_ref.shape
    chunks, step, _ = held.shape
    half = local_times // 2
    copies = [
        pltpu.make_async_copy(table_ref.at[pl.ds(i * step, step)], held.at[i], sems.at[i])
        for i in range(chunks)
    ]
    for copy in copies:
        copy.start()
    for b in range(blocks):
        turned = series_ref[b].T
        even[b * half : (b + 1) * half] = turned[:half]
        odd[b * half : (b + 1) * half] = turned[half:]
    depth = blocks * half
    for i in range(chunks):
        copies[i].wait()
        evens = jnp.dot(held[i, :, :depth], even[...], preferred_element_type=jnp.float32)
        odds = jnp.dot(held[i, :, depth:], odd[...], preferred_element_type=jnp.float32)
        low = evens + odds
        high = evens - odds
        if len(out_ref.shape) == 3:
            row = lax.broadcasted_iota(jnp.int32, (step, 1), 0)
            out_ref[0, i * step : (i + 1) * step] = low.astype(out_ref.dtype)
            out_ref[1, i * step : (i + 1) * step] = jnp.where(
                row // pairs % 2 == 0, high, -high
            ).astype(out_ref.dtype)
            continue
        targets = step // (4 * pairs)
        devices = out_ref.shape[0]
        for d in range(targets):
            cuts = [slice((4 * d + c) * pairs, (4 * d + c + 1) * pairs) for c in range(4)]
            place = i * targets + d
            for h, value in enumerate(regroup([low[cut] for cut in cuts], gathers)):
                out_ref[place, h] = value.astype(out_ref.dtype)
            mirrored = [high[cuts[2]], -high[cuts[3]], high[cuts[0]], -high[cuts[1]]]
            for h, value in enumerate(regroup(mirrored, gathers)):
                out_ref[devices - 1 - place, h] = value.astype(out_ref.dtype)


def transform(table, series, pairs, gathers):
    columns, total_time = table.shape
    blocks, rows, local_times = series.shape
    own_offsets = rows // gathers
    devices = columns // (2 * pairs)
    final = (devices, own_offsets, pairs, 4 * gathers)
    chunks = 4
    aligned = rows % (4 * gathers) == 0 and pairs % 8 == 0 and devices % (2 * chunks) == 0
    vmem = pl.BlockSpec(memory_space=pltpu.VMEM)
    out = pl.pallas_call(
        functools.partial(transform_kernel, pairs, gathers),
        in_specs=[pl.BlockSpec(memory_space=pl.ANY), vmem],
        out_specs=vmem,
        out_shape=jax.ShapeDtypeStruct(final if aligned else (2, columns, rows), jnp.bfloat16),
        scratch_shapes=[
            pltpu.VMEM((chunks, columns // chunks, total_time), jnp.bfloat16),
            pltpu.VMEM((total_time // 2, rows), jnp.bfloat16),
            pltpu.VMEM((total_time // 2, rows), jnp.bfloat16),
            pltpu.SemaphoreType.DMA((chunks,)),
        ],
        compiler_params=pltpu.CompilerParams(vmem_limit_bytes=61 * MIB),
    )(table, series)
    if aligned:
        return out
    out = out.reshape(2, devices // 2, 2, 2, pairs, own_offsets, gathers)
    out = jnp.concatenate([out[0], jnp.flip(out[1], (0, 1))], axis=0)
    return out.transpose(0, 4, 3, 1, 2, 5).reshape(final)


def moveout_kernel(shift, total_time, base_ref, slow_ref, offs_ref, out_ref, cs, sn, tc, ts):
    @pl.when(pl.program_id(0) == 0)
    def start():
        spread = CURVATURE * slow_ref[...] * offs_ref[...]
        delay = jnp.sqrt(APEX_TIME * APEX_TIME + spread * spread) - APEX_TIME
        phase = base_ref[0] * delay
        cs[0] = jnp.cos(phase)
        sn[0] = jnp.sin(phase)
        turn = delay * (2.0 * math.pi / total_time)
        tc[...] = jnp.cos(turn)
        ts[...] = jnp.sin(turn)
        far = delay * (2.0 * shift * math.pi / total_time)
        far_c = jnp.cos(far)
        far_s = jnp.sin(far)
        cs[1] = cs[0] * far_c - sn[0] * far_s
        sn[1] = sn[0] * far_c + cs[0] * far_s

    for a in range(2):
        c = cs[a]
        s = sn[a]
        out_ref[0, a] = c.astype(out_ref.dtype)
        out_ref[0, 2 + a] = s.astype(out_ref.dtype)
        cs[a] = c * tc[...] - s * ts[...]
        sn[a] = s * tc[...] + c * ts[...]


def moveout(base, slows, offs, pairs, shift, total_time):
    count = slows.shape[0]
    offsets = offs.shape[1]
    return pl.pallas_call(
        functools.partial(moveout_kernel, shift, total_time),
        grid=(pairs,),
        in_specs=[
            pl.BlockSpec(memory_space=pltpu.SMEM),
            pl.BlockSpec((count, 1), lambda k: (0, 0)),
            pl.BlockSpec((1, offsets), lambda k: (0, 0)),
        ],
        out_specs=pl.BlockSpec((1, 4, count, offsets), lambda k: (k, 0, 0, 0)),
        out_shape=jax.ShapeDtypeStruct((pairs, 4, count, offsets), jnp.bfloat16),
        scratch_shapes=[
            pltpu.VMEM((2, count, offsets), jnp.float32),
            pltpu.VMEM((2, count, offsets), jnp.float32),
            pltpu.VMEM((count, offsets), jnp.float32),
            pltpu.VMEM((count, offsets), jnp.float32),
        ],
        compiler_params=pltpu.CompilerParams(vmem_limit_bytes=61 * MIB),
        cost_estimate=pl.CostEstimate(
            flops=pairs * 40 * count * offsets,
            bytes_accessed=pairs * 8 * count * offsets,
            transcendentals=6 * count * offsets,
        ),
    )(base, slows, offs)


def one_hot(rows, columns, source):
    row = lax.broadcasted_iota(jnp.int32, (rows, columns), 0)
    column = lax.broadcasted_iota(jnp.int32, (rows, columns), 1)
    return jnp.where(column == source(row), 1.0, 0.0).astype(jnp.bfloat16)


def radon_kernel(gathers, down_ref, turn_ref, data_ref, out_ref, turns, plain, turned, held, sems):
    devices, own_offsets, pairs, lanes = data_ref.shape
    offsets = devices * own_offsets
    slows = turn_ref.shape[2]
    tile = 16
    size = tile * pairs
    copies = [
        pltpu.make_async_copy(turn_ref.at[k], turns.at[k], sems.at[k]) for k in range(pairs)
    ]
    for copy in copies:
        copy.start()

    together = tile // own_offsets
    down = down_ref[0]

    def received(r):
        k = r // tile
        return r % tile * pairs + k + down * (pairs - 1 - 2 * k)

    swap = one_hot(size, size, received)
    for d in range(devices // together):
        block = data_ref[d * together : (d + 1) * together].reshape(size, lanes)
        if pairs > 1:
            block = jnp.dot(swap, block, preferred_element_type=jnp.float32).astype(jnp.bfloat16)
        plain[:, d * tile : (d + 1) * tile] = block.reshape(pairs, tile, lanes)
    row = lax.broadcasted_iota(jnp.int32, (lanes, lanes), 0)
    column = lax.broadcasted_iota(jnp.int32, (lanes, lanes), 1)
    quarter = jnp.where(
        column % (2 * gathers) < gathers,
        jnp.where(row == column + gathers, -1.0, 0.0),
        jnp.where(row == column - gathers, 1.0, 0.0),
    ).astype(jnp.bfloat16)
    for k in range(pairs):
        turned[k] = jnp.dot(plain[k], quarter, preferred_element_type=jnp.float32).astype(
            jnp.bfloat16
        )

    first_half = lax.broadcasted_iota(jnp.int32, (1, lanes), 1) < 2 * gathers
    for k in range(pairs):
        copies[k].wait()
        cosine = turns[k, :2].reshape(2 * slows, offsets)
        sines = turns[k, 2:].reshape(2 * slows, offsets)
        both = jnp.dot(cosine, plain[k], preferred_element_type=jnp.float32) + jnp.dot(
            sines, turned[k], preferred_element_type=jnp.float32
        )
        held[k] = jnp.where(first_half, both[:slows], both[slows:]).astype(jnp.bfloat16)

    swap = one_hot(size, size, lambda r: r % pairs * tile + r // pairs)
    for p in range(slows // tile):
        block = held[:, p * tile : (p + 1) * tile].reshape(size, lanes)
        if pairs > 1:
            block = jnp.dot(swap, block, preferred_element_type=jnp.float32)
        out_ref[p * size : (p + 1) * size] = block.astype(out_ref.dtype)


def radon(down, turns, data, gathers):
    pairs, parts, count, offsets = turns.shape
    lanes = parts * gathers
    vmem = pl.BlockSpec(memory_space=pltpu.VMEM)
    return pl.pallas_call(
        functools.partial(radon_kernel, gathers),
        in_specs=[
            pl.BlockSpec(memory_space=pltpu.SMEM),
            pl.BlockSpec(memory_space=pl.ANY),
            vmem,
        ],
        out_specs=vmem,
        out_shape=jax.ShapeDtypeStruct((count * pairs, lanes), jnp.bfloat16),
        scratch_shapes=[
            pltpu.VMEM(turns.shape, jnp.bfloat16),
            pltpu.VMEM((pairs, offsets, lanes), jnp.bfloat16),
            pltpu.VMEM((pairs, offsets, lanes), jnp.bfloat16),
            pltpu.VMEM((pairs, count, lanes), jnp.bfloat16),
            pltpu.SemaphoreType.DMA((pairs,)),
        ],
        compiler_params=pltpu.CompilerParams(vmem_limit_bytes=61 * MIB),
    )(down, turns, data)


def finish_kernel(scale, in_ref, out_ref):
    devices, slows, pairs, lanes = in_ref.shape
    rows = devices * pairs
    for p in range(slows):
        block = in_ref[:, p].reshape(rows, lanes).astype(jnp.float32) * scale
        turned = block.T
        out_ref[p, :, :rows] = turned[: lanes // 2]
        out_ref[p, :, rows:] = turned[lanes // 2 :]


def finish(parts, scale):
    devices, slows, pairs, lanes = parts.shape
    rows = devices * pairs
    step = 8
    return pl.pallas_call(
        functools.partial(finish_kernel, scale),
        grid=(slows // step,),
        in_specs=[pl.BlockSpec((devices, step, pairs, lanes), lambda i: (0, i, 0, 0))],
        out_specs=pl.BlockSpec((step, lanes // 2, 2 * rows), lambda i: (i, 0, 0)),
        out_shape=jax.ShapeDtypeStruct((slows, lanes // 2, 2 * rows), jnp.float32),
        compiler_params=pltpu.CompilerParams(vmem_limit_bytes=32 * MIB),
    )(parts)


def local(raw_traces, trace_slot, offset_index, slowness_index):
    gathers, local_offsets = trace_slot.shape
    local_times = raw_traces.shape[1]
    freq_devices = lax.axis_size("freq")
    offset_devices = lax.axis_size("offset")
    devices = freq_devices * offset_devices
    total_time = local_times * freq_devices
    offsets = local_offsets * offset_devices
    band = NF // freq_devices
    own_freqs = NF // devices
    halves = 2
    pairs = own_freqs // halves
    own_offsets = local_offsets // freq_devices

    picked = pick(trace_slot, raw_traces, freq_devices)
    series = lax.all_to_all(picked, "freq", 0, 0, tiled=True)
    table = jnp.asarray(table_rows(total_time, freq_devices, offset_devices, halves, pairs))
    spectrum = transform(table, series, pairs, gathers)
    data = lax.all_to_all(spectrum, ("freq", "offset"), 0, 0, tiled=True)

    offs = offset_index.reshape(offset_devices, freq_devices, own_offsets)
    offs = offs.transpose(1, 0, 2).reshape(1, offsets).astype(jnp.float32)
    slows = slowness_index.astype(jnp.float32)[:, None]
    first = lax.axis_index("freq") * band + lax.axis_index("offset") * pairs
    base = (2 * first + 1).astype(jnp.float32) * (math.pi / total_time)
    turns = moveout(base.reshape(1), slows, offs, pairs, band // halves, total_time)
    down = (2 * lax.axis_index("freq") // freq_devices).astype(jnp.int32).reshape(1)
    panel = radon(down, turns, data, gathers)
    panel = panel.reshape(offset_devices, NP // offset_devices, pairs, 2 * halves * gathers)
    parts = lax.all_to_all(panel, "offset", 0, 0, tiled=True)
    result = finish(parts, 1.0 / math.sqrt(offsets))
    return jnp.transpose(result, (0, 2, 1))


def solution(mesh):
    placed = (P("offset", "freq"), P(None, "offset"), P(), P())
    return jax.shard_map(
        local, mesh=mesh, in_specs=placed, out_specs=P("offset", "freq", None), check_vma=False
    )
```

```python
import functools
import math

import jax
import jax.numpy as jnp
import ml_dtypes
import numpy as np
from jax import lax
from jax.experimental import pallas as pl
from jax.experimental.pallas import tpu as pltpu
from jax.sharding import PartitionSpec as P

NF = 1024
NP = 256
APEX_TIME = 100.0
CURVATURE = 0.0003
MIB = 1 << 20


def table_rows(total_time, freq_devices, offset_devices, halves, pairs):
    band = NF // freq_devices
    f, o, a, k = np.meshgrid(
        np.arange(freq_devices // 2),
        np.arange(offset_devices),
        np.arange(halves),
        np.arange(pairs),
        indexing="ij",
    )
    freq_ids = (f * band + a * (band // halves) + o * pairs + k).reshape(-1, pairs)
    times = np.concatenate([np.arange(0, total_time, 2), np.arange(1, total_time, 2)])
    turns = (2 * freq_ids[..., None] + 1) * times % (2 * total_time)
    angles = turns.astype(np.float32) * np.float32(math.pi / total_time)
    both = np.stack([np.cos(angles), -np.sin(angles)], axis=1).reshape(-1, total_time)
    return (both / np.float32(math.sqrt(total_time))).astype(ml_dtypes.bfloat16)


def pick_kernel(slot_ref, raw_ref, out_ref):
    gathers = slot_ref.shape[0]
    groups, rows, _ = out_ref.shape
    own_offsets = rows // gathers
    times = raw_ref.shape[1]
    half = times // 2
    row = lax.broadcasted_iota(jnp.int32, (times, times), 0)
    column = lax.broadcasted_iota(jnp.int32, (times, times), 1)
    source = jnp.where(column < half, 2 * column, 2 * (column - half) + 1)
    split = jnp.where(row == source, 1.0, 0.0).astype(jnp.bfloat16)
    raw = jnp.dot(raw_ref[...], split, preferred_element_type=jnp.float32).astype(jnp.bfloat16)
    lane = lax.broadcasted_iota(jnp.int32, (gathers, raw_ref.shape[0]), 1)
    for f in range(groups):
        picks = [
            jnp.where(lane == slot_ref[:, h : h + 1], 1.0, 0.0).astype(jnp.bfloat16)
            for h in range(f * own_offsets, (f + 1) * own_offsets)
        ]
        out_ref[f] = jnp.dot(
            jnp.concatenate(picks, axis=0), raw, preferred_element_type=jnp.float32
        ).astype(out_ref.dtype)


def pick(trace_slot, raw_traces, groups):
    gathers, local_offsets = trace_slot.shape
    rows = gathers * local_offsets // groups
    vmem = pl.BlockSpec(memory_space=pltpu.VMEM)
    return pl.pallas_call(
        pick_kernel,
        in_specs=[vmem, vmem],
        out_specs=vmem,
        out_shape=jax.ShapeDtypeStruct((groups, rows, raw_traces.shape[1]), raw_traces.dtype),
        compiler_params=pltpu.CompilerParams(vmem_limit_bytes=24 * MIB),
    )(trace_slot, raw_traces)


def regroup(parts, gathers):
    lanes = 4 * gathers
    lane = lax.broadcasted_iota(jnp.int32, (1, lanes), 1)
    low_half = lane < 2 * gathers
    low_part = lane % (2 * gathers) < gathers
    found = []
    for q in range(parts[0].shape[1] // lanes):
        x = [part[:, q * lanes : (q + 1) * lanes] for part in parts]
        for top in range(2):
            pair = []
            for part in range(2):
                a, b = x[part], x[2 + part]
                if top == 0:
                    pair.append(jnp.where(low_half, a, pltpu.roll(b, 2 * gathers, 1)))
                else:
                    pair.append(jnp.where(low_half, pltpu.roll(a, 2 * gathers, 1), b))
            found.append(jnp.where(low_part, pair[0], pltpu.roll(pair[1], gathers, 1)))
            found.append(jnp.where(low_part, pltpu.roll(pair[0], lanes - gathers, 1), pair[1]))
    return found


def transform_kernel(pairs, gathers, chunks, table_ref, series_ref, out_ref, even, odd):
    blocks, rows, local_times = series_ref.shape
    step = table_ref.shape[0] // chunks
    half = local_times // 2
    for b in range(blocks):
        turned = series_ref[b].T
        even[b * half : (b + 1) * half] = turned[:half]
        odd[b * half : (b + 1) * half] = turned[half:]
    depth = blocks * half
    for i in range(chunks):
        own = slice(i * step, (i + 1) * step)
        evens = jnp.dot(table_ref[own, :depth], even[...], preferred_element_type=jnp.float32)
        odds = jnp.dot(table_ref[own, depth:], odd[...], preferred_element_type=jnp.float32)
        low = evens + odds
        high = evens - odds
        if len(out_ref.shape) == 3:
            row = lax.broadcasted_iota(jnp.int32, (step, 1), 0)
            out_ref[0, own] = low.astype(out_ref.dtype)
            out_ref[1, own] = jnp.where(
                row // pairs % 2 == 0, high, -high
            ).astype(out_ref.dtype)
            continue
        targets = step // (4 * pairs)
        devices = out_ref.shape[0]
        for d in range(targets):
            cuts = [slice((4 * d + c) * pairs, (4 * d + c + 1) * pairs) for c in range(4)]
            place = i * targets + d
            for h, value in enumerate(regroup([low[cut] for cut in cuts], gathers)):
                out_ref[place, h] = value.astype(out_ref.dtype)
            mirrored = [high[cuts[2]], -high[cuts[3]], high[cuts[0]], -high[cuts[1]]]
            for h, value in enumerate(regroup(mirrored, gathers)):
                out_ref[devices - 1 - place, h] = value.astype(out_ref.dtype)


def transform(table, series, pairs, gathers):
    columns, total_time = table.shape
    blocks, rows, local_times = series.shape
    own_offsets = rows // gathers
    devices = columns // (2 * pairs)
    final = (devices, own_offsets, pairs, 4 * gathers)
    chunks = 4
    aligned = rows % (4 * gathers) == 0 and pairs % 8 == 0 and devices % (2 * chunks) == 0
    vmem = pl.BlockSpec(memory_space=pltpu.VMEM)
    out = pl.pallas_call(
        functools.partial(transform_kernel, pairs, gathers, chunks),
        in_specs=[vmem, vmem],
        out_specs=vmem,
        out_shape=jax.ShapeDtypeStruct(final if aligned else (2, columns, rows), jnp.bfloat16),
        scratch_shapes=[
            pltpu.VMEM((total_time // 2, rows), jnp.bfloat16),
            pltpu.VMEM((total_time // 2, rows), jnp.bfloat16),
        ],
        compiler_params=pltpu.CompilerParams(vmem_limit_bytes=24 * MIB),
    )(table, series)
    if aligned:
        return out
    out = out.reshape(2, devices // 2, 2, 2, pairs, own_offsets, gathers)
    out = jnp.concatenate([out[0], jnp.flip(out[1], (0, 1))], axis=0)
    return out.transpose(0, 4, 3, 1, 2, 5).reshape(final)


def moveout_kernel(shift, total_time, base_ref, slow_ref, offs_ref, out_ref):
    spread = CURVATURE * slow_ref[...] * offs_ref[...]
    delay = jnp.sqrt(APEX_TIME * APEX_TIME + spread * spread) - APEX_TIME
    phase = base_ref[0] * delay
    c = jnp.cos(phase)
    s = jnp.sin(phase)
    far = delay * (2.0 * shift * math.pi / total_time)
    far_c = jnp.cos(far)
    far_s = jnp.sin(far)
    turn = delay * (2.0 * math.pi / total_time)
    out_ref[0] = c
    out_ref[1] = c * far_c - s * far_s
    out_ref[2] = s
    out_ref[3] = s * far_c + c * far_s
    out_ref[4] = jnp.cos(turn)
    out_ref[5] = jnp.sin(turn)


def moveout(base, slows, offs, shift, total_time):
    count = slows.shape[0]
    offsets = offs.shape[1]
    rows = min(count, 64)
    return pl.pallas_call(
        functools.partial(moveout_kernel, shift, total_time),
        grid=(count // rows,),
        in_specs=[
            pl.BlockSpec(memory_space=pltpu.SMEM),
            pl.BlockSpec((rows, 1), lambda i: (i, 0)),
            pl.BlockSpec((1, offsets), lambda i: (0, 0)),
        ],
        out_specs=pl.BlockSpec((6, rows, offsets), lambda i: (0, i, 0)),
        out_shape=jax.ShapeDtypeStruct((6, count, offsets), jnp.float32),
        compiler_params=pltpu.CompilerParams(vmem_limit_bytes=24 * MIB),
        cost_estimate=pl.CostEstimate(
            flops=300 * count * offsets,
            bytes_accessed=24 * count * offsets,
            transcendentals=6 * count * offsets,
        ),
    )(base, slows, offs)


def quotient(value, divisor):
    if divisor & (divisor - 1):
        return value // divisor
    return lax.shift_right_logical(value, jnp.int32(divisor.bit_length() - 1))


def remainder(value, divisor):
    if divisor & (divisor - 1):
        return value % divisor
    return value & (divisor - 1)


def one_hot(rows, columns, source):
    row = lax.broadcasted_iota(jnp.int32, (rows, 1), 0)
    column = lax.broadcasted_iota(jnp.int32, (rows, columns), 1)
    return jnp.where(column == source(row), 1.0, 0.0).astype(jnp.bfloat16)


def radon_kernel(gathers, down_ref, state_ref, data_ref, out_ref, turns, plain, turned, held):
    devices, own_offsets, pairs, lanes = data_ref.shape
    offsets = devices * own_offsets
    slows = state_ref.shape[1]
    tile = 16
    size = tile * pairs
    together = tile // own_offsets
    down = down_ref[0]

    def received(r):
        k = quotient(r, tile)
        return remainder(r, tile) * pairs + k + down * (pairs - 1 - 2 * k)

    swap = one_hot(size, size, received)
    for d in range(devices // together):
        block = data_ref[d * together : (d + 1) * together].reshape(size, lanes)
        if pairs > 1:
            block = jnp.dot(swap, block, preferred_element_type=jnp.float32).astype(jnp.bfloat16)
        plain[:, d * tile : (d + 1) * tile] = block.reshape(pairs, tile, lanes)
    row = lax.broadcasted_iota(jnp.int32, (lanes, lanes), 0)
    column = lax.broadcasted_iota(jnp.int32, (lanes, lanes), 1)
    quarter = jnp.where(
        remainder(column, 2 * gathers) < gathers,
        jnp.where(row == column + gathers, -1.0, 0.0),
        jnp.where(row == column - gathers, 1.0, 0.0),
    ).astype(jnp.bfloat16)
    for k in range(pairs):
        turned[k] = jnp.dot(plain[k], quarter, preferred_element_type=jnp.float32).astype(
            jnp.bfloat16
        )

    def fill(t, carry):
        own = pl.ds(pl.multiple_of(t * tile, tile), tile)
        step_c = state_ref[4, own]
        step_s = state_ref[5, own]
        twice = 2.0 * step_c
        now = [state_ref[i, own] for i in range(4)]
        past = [now[a] * step_c + now[2 + a] * step_s for a in range(2)]
        past += [now[2 + a] * step_c - now[a] * step_s for a in range(2)]
        for k in range(pairs):
            for i in range(4):
                turns[k, i, own] = now[i].astype(jnp.bfloat16)
                now[i], past[i] = twice * now[i] - past[i], now[i]
        return carry

    lax.fori_loop(0, slows // tile, fill, 0)

    first_half = lax.broadcasted_iota(jnp.int32, (1, lanes), 1) < 2 * gathers
    for k in range(pairs):
        cosine = turns[k, :2].reshape(2 * slows, offsets)
        sines = turns[k, 2:].reshape(2 * slows, offsets)
        both = jnp.dot(cosine, plain[k], preferred_element_type=jnp.float32) + jnp.dot(
            sines, turned[k], preferred_element_type=jnp.float32
        )
        held[k] = jnp.where(first_half, both[:slows], both[slows:]).astype(jnp.bfloat16)

    swap = one_hot(size, size, lambda r: remainder(r, pairs) * tile + quotient(r, pairs))
    for p in range(slows // tile):
        block = held[:, p * tile : (p + 1) * tile].reshape(size, lanes)
        if pairs > 1:
            block = jnp.dot(swap, block, preferred_element_type=jnp.float32)
        out_ref[p * size : (p + 1) * size] = block.astype(out_ref.dtype)


def radon(down, state, data, gathers):
    _, count, offsets = state.shape
    pairs, lanes = data.shape[2:]
    vmem = pl.BlockSpec(memory_space=pltpu.VMEM)
    return pl.pallas_call(
        functools.partial(radon_kernel, gathers),
        in_specs=[pl.BlockSpec(memory_space=pltpu.SMEM), vmem, vmem],
        out_specs=vmem,
        out_shape=jax.ShapeDtypeStruct((count * pairs, lanes), jnp.bfloat16),
        scratch_shapes=[
            pltpu.VMEM((pairs, 4, count, offsets), jnp.bfloat16),
            pltpu.VMEM((pairs, offsets, lanes), jnp.bfloat16),
            pltpu.VMEM((pairs, offsets, lanes), jnp.bfloat16),
            pltpu.VMEM((pairs, count, lanes), jnp.bfloat16),
        ],
        compiler_params=pltpu.CompilerParams(vmem_limit_bytes=24 * MIB),
    )(down, state, data)


def finish_kernel(scale, in_ref, out_ref):
    devices, slows, pairs, lanes = in_ref.shape
    rows = devices * pairs
    for p in range(slows):
        block = in_ref[:, p].reshape(rows, lanes).astype(jnp.float32) * scale
        turned = block.T
        out_ref[p, :, :rows] = turned[: lanes // 2]
        out_ref[p, :, rows:] = turned[lanes // 2 :]


def finish(parts, scale):
    devices, slows, pairs, lanes = parts.shape
    rows = devices * pairs
    step = 8
    return pl.pallas_call(
        functools.partial(finish_kernel, scale),
        grid=(slows // step,),
        in_specs=[pl.BlockSpec((devices, step, pairs, lanes), lambda i: (0, i, 0, 0))],
        out_specs=pl.BlockSpec((step, lanes // 2, 2 * rows), lambda i: (i, 0, 0)),
        out_shape=jax.ShapeDtypeStruct((slows, lanes // 2, 2 * rows), jnp.float32),
        compiler_params=pltpu.CompilerParams(vmem_limit_bytes=32 * MIB),
    )(parts)


def local(raw_traces, trace_slot, offset_index, slowness_index):
    gathers, local_offsets = trace_slot.shape
    local_times = raw_traces.shape[1]
    freq_devices = lax.axis_size("freq")
    offset_devices = lax.axis_size("offset")
    devices = freq_devices * offset_devices
    total_time = local_times * freq_devices
    offsets = local_offsets * offset_devices
    band = NF // freq_devices
    own_freqs = NF // devices
    halves = 2
    pairs = own_freqs // halves
    own_offsets = local_offsets // freq_devices

    picked = pick(trace_slot, raw_traces, freq_devices)
    series = lax.all_to_all(picked, "freq", 0, 0, tiled=True)
    table = jnp.asarray(table_rows(total_time, freq_devices, offset_devices, halves, pairs))
    spectrum = transform(table, series, pairs, gathers)
    data = lax.all_to_all(spectrum, ("freq", "offset"), 0, 0, tiled=True)

    offs = offset_index.reshape(offset_devices, freq_devices, own_offsets)
    offs = offs.transpose(1, 0, 2).reshape(1, offsets).astype(jnp.float32)
    slows = slowness_index.astype(jnp.float32)[:, None]
    first = lax.axis_index("freq") * band + lax.axis_index("offset") * pairs
    base = (2 * first + 1).astype(jnp.float32) * (math.pi / total_time)
    state = moveout(base.reshape(1), slows, offs, band // halves, total_time)
    down = (2 * lax.axis_index("freq") // freq_devices).astype(jnp.int32).reshape(1)
    panel = radon(down, state, data, gathers)
    panel = panel.reshape(offset_devices, NP // offset_devices, pairs, 2 * halves * gathers)
    parts = lax.all_to_all(panel, "offset", 0, 0, tiled=True)
    result = finish(parts, 1.0 / math.sqrt(offsets))
    return jnp.transpose(result, (0, 2, 1))


def solution(mesh):
    placed = (P("offset", "freq"), P(None, "offset"), P(), P())
    return jax.shard_map(
        local, mesh=mesh, in_specs=placed, out_specs=P("offset", "freq", None), check_vma=False
    )
```

```python
import functools
import math

import jax
import jax.numpy as jnp
import ml_dtypes
import numpy as np
from jax import lax
from jax.experimental import pallas as pl
from jax.experimental.pallas import tpu as pltpu
from jax.sharding import PartitionSpec as P

NF = 1024
NP = 256
APEX_TIME = 100.0
CURVATURE = 0.0003
MIB = 1 << 20


def table_rows(total_time, freq_devices, offset_devices, halves, pairs):
    band = NF // freq_devices
    f, o, a, k = np.meshgrid(
        np.arange(freq_devices // 2),
        np.arange(offset_devices),
        np.arange(halves),
        np.arange(pairs),
        indexing="ij",
    )
    freq_ids = (f * band + a * (band // halves) + o * pairs + k).reshape(-1, pairs)
    times = np.concatenate([np.arange(0, total_time, 2), np.arange(1, total_time, 2)])
    turns = (2 * freq_ids[..., None] + 1) * times % (2 * total_time)
    angles = turns.astype(np.float32) * np.float32(math.pi / total_time)
    both = np.stack([np.cos(angles), -np.sin(angles)], axis=1).reshape(-1, total_time)
    return (both / np.float32(math.sqrt(total_time))).astype(ml_dtypes.bfloat16)


def pick_kernel(me_ref, slot_ref, raw_ref, *out_refs):
    gathers, local_offsets = slot_ref.shape
    own_offsets = local_offsets // len(out_refs)
    times = raw_ref.shape[1]
    half = times // 2
    row = lax.broadcasted_iota(jnp.int32, (times, times), 0)
    column = lax.broadcasted_iota(jnp.int32, (times, times), 1)
    source = jnp.where(column < half, 2 * column, 2 * (column - half) + 1)
    split = jnp.where(row == source, 1.0, 0.0).astype(jnp.bfloat16)
    raw = jnp.dot(raw_ref[...], split, preferred_element_type=jnp.float32).astype(jnp.bfloat16)
    lane = lax.broadcasted_iota(jnp.int32, (gathers, raw_ref.shape[0]), 1)
    slot = slot_ref[...]
    place = lax.broadcasted_iota(jnp.int32, slot.shape, 1)
    for s, out_ref in enumerate(out_refs):
        first = (me_ref[0] ^ s) * own_offsets
        picks = []
        for h in range(own_offsets):
            wanted = jnp.sum(jnp.where(place == first + h, slot, 0.0), axis=1, keepdims=True)
            picks.append(
                jnp.where(lane == wanted.astype(jnp.int32), 1.0, 0.0).astype(jnp.bfloat16)
            )
        out_ref[...] = jnp.dot(
            jnp.concatenate(picks, axis=0), raw, preferred_element_type=jnp.float32
        ).astype(out_ref.dtype)


def pick(me, trace_slot, raw_traces, groups):
    gathers, local_offsets = trace_slot.shape
    rows = gathers * local_offsets // groups
    vmem = pl.BlockSpec(memory_space=pltpu.VMEM)
    block = jax.ShapeDtypeStruct((rows, raw_traces.shape[1]), raw_traces.dtype)
    return pl.pallas_call(
        pick_kernel,
        in_specs=[pl.BlockSpec(memory_space=pltpu.SMEM), vmem, vmem],
        out_specs=[vmem] * groups,
        out_shape=[block] * groups,
        compiler_params=pltpu.CompilerParams(vmem_limit_bytes=24 * MIB),
    )(me, trace_slot, raw_traces)


def regroup(parts, gathers):
    lanes = 4 * gathers
    lane = lax.broadcasted_iota(jnp.int32, (1, lanes), 1)
    low_half = lane < 2 * gathers
    low_part = lane % (2 * gathers) < gathers
    found = []
    for q in range(parts[0].shape[1] // lanes):
        x = [part[:, q * lanes : (q + 1) * lanes] for part in parts]
        for top in range(2):
            pair = []
            for part in range(2):
                a, b = x[part], x[2 + part]
                if top == 0:
                    pair.append(jnp.where(low_half, a, pltpu.roll(b, 2 * gathers, 1)))
                else:
                    pair.append(jnp.where(low_half, pltpu.roll(a, 2 * gathers, 1), b))
            found.append(jnp.where(low_part, pair[0], pltpu.roll(pair[1], gathers, 1)))
            found.append(jnp.where(low_part, pltpu.roll(pair[0], lanes - gathers, 1), pair[1]))
    return found


def transform_kernel(pairs, gathers, chunks, me_ref, table_ref, *refs):
    *series_refs, out_ref, even, odd = refs
    blocks = len(series_refs)
    _, local_times = series_refs[0].shape
    step = table_ref.shape[0] // chunks
    half = local_times // 2
    for s, series_ref in enumerate(series_refs):
        turned = series_ref[...].T
        place = pl.ds(pl.multiple_of((me_ref[0] ^ s) * half, half), half)
        even[place] = turned[:half]
        odd[place] = turned[half:]
    depth = blocks * half
    for i in range(chunks):
        own = slice(i * step, (i + 1) * step)
        evens = jnp.dot(table_ref[own, :depth], even[...], preferred_element_type=jnp.float32)
        odds = jnp.dot(table_ref[own, depth:], odd[...], preferred_element_type=jnp.float32)
        low = evens + odds
        high = evens - odds
        if len(out_ref.shape) == 3:
            row = lax.broadcasted_iota(jnp.int32, (step, 1), 0)
            out_ref[0, own] = low.astype(out_ref.dtype)
            out_ref[1, own] = jnp.where(
                row // pairs % 2 == 0, high, -high
            ).astype(out_ref.dtype)
            continue
        targets = step // (4 * pairs)
        devices = out_ref.shape[0]
        for d in range(targets):
            cuts = [slice((4 * d + c) * pairs, (4 * d + c + 1) * pairs) for c in range(4)]
            place = i * targets + d
            for h, value in enumerate(regroup([low[cut] for cut in cuts], gathers)):
                out_ref[place, h] = value.astype(out_ref.dtype)
            mirrored = [high[cuts[2]], -high[cuts[3]], high[cuts[0]], -high[cuts[1]]]
            for h, value in enumerate(regroup(mirrored, gathers)):
                out_ref[devices - 1 - place, h] = value.astype(out_ref.dtype)


def transform(me, table, series, pairs, gathers):
    columns, total_time = table.shape
    rows = series[0].shape[0]
    own_offsets = rows // gathers
    devices = columns // (2 * pairs)
    final = (devices, own_offsets, pairs, 4 * gathers)
    chunks = 4
    aligned = rows % (4 * gathers) == 0 and pairs % 8 == 0 and devices % (2 * chunks) == 0
    vmem = pl.BlockSpec(memory_space=pltpu.VMEM)
    out = pl.pallas_call(
        functools.partial(transform_kernel, pairs, gathers, chunks),
        in_specs=[pl.BlockSpec(memory_space=pltpu.SMEM)] + [vmem] * (1 + len(series)),
        out_specs=vmem,
        out_shape=jax.ShapeDtypeStruct(final if aligned else (2, columns, rows), jnp.bfloat16),
        scratch_shapes=[
            pltpu.VMEM((total_time // 2, rows), jnp.bfloat16),
            pltpu.VMEM((total_time // 2, rows), jnp.bfloat16),
        ],
        compiler_params=pltpu.CompilerParams(vmem_limit_bytes=24 * MIB),
    )(me, table, *series)
    if aligned:
        return out
    out = out.reshape(2, devices // 2, 2, 2, pairs, own_offsets, gathers)
    out = jnp.concatenate([out[0], jnp.flip(out[1], (0, 1))], axis=0)
    return out.transpose(0, 4, 3, 1, 2, 5).reshape(final)


def moveout_kernel(shift, total_time, base_ref, slow_ref, offs_ref, out_ref):
    spread = CURVATURE * slow_ref[...] * offs_ref[...]
    delay = jnp.sqrt(APEX_TIME * APEX_TIME + spread * spread) - APEX_TIME
    phase = base_ref[0] * delay
    c = jnp.cos(phase)
    s = jnp.sin(phase)
    far = delay * (2.0 * shift * math.pi / total_time)
    far_c = jnp.cos(far)
    far_s = jnp.sin(far)
    turn = delay * (2.0 * math.pi / total_time)
    out_ref[0] = c
    out_ref[1] = c * far_c - s * far_s
    out_ref[2] = s
    out_ref[3] = s * far_c + c * far_s
    out_ref[4] = jnp.cos(turn)
    out_ref[5] = jnp.sin(turn)


def moveout(base, slows, offs, shift, total_time):
    count = slows.shape[0]
    offsets = offs.shape[1]
    rows = min(count, 64)
    return pl.pallas_call(
        functools.partial(moveout_kernel, shift, total_time),
        grid=(count // rows,),
        in_specs=[
            pl.BlockSpec(memory_space=pltpu.SMEM),
            pl.BlockSpec((rows, 1), lambda i: (i, 0)),
            pl.BlockSpec((1, offsets), lambda i: (0, 0)),
        ],
        out_specs=pl.BlockSpec((6, rows, offsets), lambda i: (0, i, 0)),
        out_shape=jax.ShapeDtypeStruct((6, count, offsets), jnp.float32),
        compiler_params=pltpu.CompilerParams(vmem_limit_bytes=24 * MIB),
        cost_estimate=pl.CostEstimate(
            flops=300 * count * offsets,
            bytes_accessed=24 * count * offsets,
            transcendentals=6 * count * offsets,
        ),
    )(base, slows, offs)


def quotient(value, divisor):
    if divisor & (divisor - 1):
        return value // divisor
    return lax.shift_right_logical(value, jnp.int32(divisor.bit_length() - 1))


def remainder(value, divisor):
    if divisor & (divisor - 1):
        return value % divisor
    return value & (divisor - 1)


def one_hot(rows, columns, source):
    row = lax.broadcasted_iota(jnp.int32, (rows, 1), 0)
    column = lax.broadcasted_iota(jnp.int32, (rows, columns), 1)
    return jnp.where(column == source(row), 1.0, 0.0).astype(jnp.bfloat16)


def radon_kernel(gathers, down_ref, state_ref, data_ref, out_ref, turns, plain, turned, held):
    devices, own_offsets, pairs, lanes = data_ref.shape
    offsets = devices * own_offsets
    slows = state_ref.shape[1]
    tile = 16
    size = tile * pairs
    together = tile // own_offsets
    down = down_ref[0]

    def received(r):
        k = quotient(r, tile)
        return remainder(r, tile) * pairs + k + down * (pairs - 1 - 2 * k)

    swap = one_hot(size, size, received)
    for d in range(devices // together):
        block = data_ref[d * together : (d + 1) * together].reshape(size, lanes)
        if pairs > 1:
            block = jnp.dot(swap, block, preferred_element_type=jnp.float32).astype(jnp.bfloat16)
        plain[:, d * tile : (d + 1) * tile] = block.reshape(pairs, tile, lanes)
    row = lax.broadcasted_iota(jnp.int32, (lanes, lanes), 0)
    column = lax.broadcasted_iota(jnp.int32, (lanes, lanes), 1)
    quarter = jnp.where(
        remainder(column, 2 * gathers) < gathers,
        jnp.where(row == column + gathers, -1.0, 0.0),
        jnp.where(row == column - gathers, 1.0, 0.0),
    ).astype(jnp.bfloat16)
    for k in range(pairs):
        turned[k] = jnp.dot(plain[k], quarter, preferred_element_type=jnp.float32).astype(
            jnp.bfloat16
        )

    def fill(t, carry):
        own = pl.ds(pl.multiple_of(t * tile, tile), tile)
        step_c = state_ref[4, own]
        step_s = state_ref[5, own]
        twice = 2.0 * step_c
        now = [state_ref[i, own] for i in range(4)]
        past = [now[a] * step_c + now[2 + a] * step_s for a in range(2)]
        past += [now[2 + a] * step_c - now[a] * step_s for a in range(2)]
        for k in range(pairs):
            for i in range(4):
                turns[k, i, own] = now[i].astype(jnp.bfloat16)
                now[i], past[i] = twice * now[i] - past[i], now[i]
        return carry

    lax.fori_loop(0, slows // tile, fill, 0)

    first_half = lax.broadcasted_iota(jnp.int32, (1, lanes), 1) < 2 * gathers
    for k in range(pairs):
        cosine = turns[k, :2].reshape(2 * slows, offsets)
        sines = turns[k, 2:].reshape(2 * slows, offsets)
        both = jnp.dot(cosine, plain[k], preferred_element_type=jnp.float32) + jnp.dot(
            sines, turned[k], preferred_element_type=jnp.float32
        )
        held[k] = jnp.where(first_half, both[:slows], both[slows:]).astype(jnp.bfloat16)

    swap = one_hot(size, size, lambda r: remainder(r, pairs) * tile + quotient(r, pairs))
    for p in range(slows // tile):
        block = held[:, p * tile : (p + 1) * tile].reshape(size, lanes)
        if pairs > 1:
            block = jnp.dot(swap, block, preferred_element_type=jnp.float32)
        out_ref[p * size : (p + 1) * size] = block.astype(out_ref.dtype)


def radon(down, state, data, gathers):
    _, count, offsets = state.shape
    pairs, lanes = data.shape[2:]
    vmem = pl.BlockSpec(memory_space=pltpu.VMEM)
    return pl.pallas_call(
        functools.partial(radon_kernel, gathers),
        in_specs=[pl.BlockSpec(memory_space=pltpu.SMEM), vmem, vmem],
        out_specs=vmem,
        out_shape=jax.ShapeDtypeStruct((count * pairs, lanes), jnp.bfloat16),
        scratch_shapes=[
            pltpu.VMEM((pairs, 4, count, offsets), jnp.bfloat16),
            pltpu.VMEM((pairs, offsets, lanes), jnp.bfloat16),
            pltpu.VMEM((pairs, offsets, lanes), jnp.bfloat16),
            pltpu.VMEM((pairs, count, lanes), jnp.bfloat16),
        ],
        compiler_params=pltpu.CompilerParams(vmem_limit_bytes=24 * MIB),
    )(down, state, data)


def finish_kernel(scale, in_ref, out_ref):
    devices, slows, pairs, lanes = in_ref.shape
    rows = devices * pairs
    for p in range(slows):
        block = in_ref[:, p].reshape(rows, lanes).astype(jnp.float32) * scale
        turned = block.T
        out_ref[p, :, :rows] = turned[: lanes // 2]
        out_ref[p, :, rows:] = turned[lanes // 2 :]


def finish(parts, scale):
    devices, slows, pairs, lanes = parts.shape
    rows = devices * pairs
    step = 8
    return pl.pallas_call(
        functools.partial(finish_kernel, scale),
        grid=(slows // step,),
        in_specs=[pl.BlockSpec((devices, step, pairs, lanes), lambda i: (0, i, 0, 0))],
        out_specs=pl.BlockSpec((step, lanes // 2, 2 * rows), lambda i: (i, 0, 0)),
        out_shape=jax.ShapeDtypeStruct((slows, lanes // 2, 2 * rows), jnp.float32),
        compiler_params=pltpu.CompilerParams(vmem_limit_bytes=32 * MIB),
    )(parts)


def local(raw_traces, trace_slot, offset_index, slowness_index):
    gathers, local_offsets = trace_slot.shape
    local_times = raw_traces.shape[1]
    freq_devices = lax.axis_size("freq")
    offset_devices = lax.axis_size("offset")
    devices = freq_devices * offset_devices
    total_time = local_times * freq_devices
    offsets = local_offsets * offset_devices
    band = NF // freq_devices
    own_freqs = NF // devices
    halves = 2
    pairs = own_freqs // halves
    own_offsets = local_offsets // freq_devices

    me = lax.axis_index("freq").astype(jnp.int32).reshape(1)
    series = list(pick(me, trace_slot.astype(jnp.float32), raw_traces, freq_devices))
    for s in range(1, freq_devices):
        swaps = [(f, f ^ s) for f in range(freq_devices)]
        series[s] = lax.ppermute(series[s], "freq", swaps)
    table = jnp.asarray(table_rows(total_time, freq_devices, offset_devices, halves, pairs))
    spectrum = transform(me, table, series, pairs, gathers)
    data = lax.all_to_all(spectrum, ("freq", "offset"), 0, 0, tiled=True)

    offs = offset_index.reshape(offset_devices, freq_devices, own_offsets)
    offs = offs.transpose(1, 0, 2).reshape(1, offsets).astype(jnp.float32)
    slows = slowness_index.astype(jnp.float32)[:, None]
    first = lax.axis_index("freq") * band + lax.axis_index("offset") * pairs
    base = (2 * first + 1).astype(jnp.float32) * (math.pi / total_time)
    state = moveout(base.reshape(1), slows, offs, band // halves, total_time)
    down = (2 * lax.axis_index("freq") // freq_devices).astype(jnp.int32).reshape(1)
    panel = radon(down, state, data, gathers)
    panel = panel.reshape(offset_devices, NP // offset_devices, pairs, 2 * halves * gathers)
    parts = lax.all_to_all(panel, "offset", 0, 0, tiled=True)
    result = finish(parts, 1.0 / math.sqrt(offsets))
    return jnp.transpose(result, (0, 2, 1))


def solution(mesh):
    placed = (P("offset", "freq"), P(None, "offset"), P(), P())
    return jax.shard_map(
        local, mesh=mesh, in_specs=placed, out_specs=P("offset", "freq", None), check_vma=False
    )
```

```python
import functools
import math

import jax
import jax.numpy as jnp
import ml_dtypes
import numpy as np
from jax import lax
from jax.experimental import pallas as pl
from jax.experimental.pallas import tpu as pltpu
from jax.sharding import PartitionSpec as P

NF = 1024
NP = 256
APEX_TIME = 100.0
CURVATURE = 0.0003
MIB = 1 << 20


def table_rows(total_time, freq_devices, offset_devices, halves, pairs):
    band = NF // freq_devices
    f, o, a, k = np.meshgrid(
        np.arange(freq_devices // 2),
        np.arange(offset_devices),
        np.arange(halves),
        np.arange(pairs),
        indexing="ij",
    )
    freq_ids = (f * band + a * (band // halves) + o * pairs + k).reshape(-1, pairs)
    times = np.concatenate([np.arange(0, total_time, 2), np.arange(1, total_time, 2)])
    turns = (2 * freq_ids[..., None] + 1) * times % (2 * total_time)
    angles = turns.astype(np.float32) * np.float32(math.pi / total_time)
    both = np.stack([np.cos(angles), -np.sin(angles)], axis=1).reshape(-1, total_time)
    return (both / np.float32(math.sqrt(total_time))).astype(ml_dtypes.bfloat16)


def pick_kernel(slot_ref, raw_ref, out_ref):
    gathers = slot_ref.shape[0]
    groups, rows, _ = out_ref.shape
    own_offsets = rows // gathers
    times = raw_ref.shape[1]
    half = times // 2
    row = lax.broadcasted_iota(jnp.int32, (times, times), 0)
    column = lax.broadcasted_iota(jnp.int32, (times, times), 1)
    source = jnp.where(column < half, 2 * column, 2 * (column - half) + 1)
    split = jnp.where(row == source, 1.0, 0.0).astype(jnp.bfloat16)
    raw = jnp.dot(raw_ref[...], split, preferred_element_type=jnp.float32).astype(jnp.bfloat16)
    lane = lax.broadcasted_iota(jnp.int32, (gathers, raw_ref.shape[0]), 1)
    for f in range(groups):
        picks = [
            jnp.where(lane == slot_ref[:, h : h + 1].astype(jnp.int32), 1.0, 0.0).astype(jnp.bfloat16)
            for h in range(f * own_offsets, (f + 1) * own_offsets)
        ]
        out_ref[f] = jnp.dot(
            jnp.concatenate(picks, axis=0), raw, preferred_element_type=jnp.float32
        ).astype(out_ref.dtype)


def pick(trace_slot, raw_traces, groups):
    gathers, local_offsets = trace_slot.shape
    rows = gathers * local_offsets // groups
    vmem = pl.BlockSpec(memory_space=pltpu.VMEM)
    return pl.pallas_call(
        pick_kernel,
        in_specs=[vmem, vmem],
        out_specs=vmem,
        out_shape=jax.ShapeDtypeStruct((groups, rows, raw_traces.shape[1]), raw_traces.dtype),
        compiler_params=pltpu.CompilerParams(vmem_limit_bytes=24 * MIB),
    )(trace_slot, raw_traces)


def regroup(parts, gathers):
    lanes = 4 * gathers
    lane = lax.broadcasted_iota(jnp.int32, (1, lanes), 1)
    low_half = lane < 2 * gathers
    low_part = lane % (2 * gathers) < gathers
    found = []
    for q in range(parts[0].shape[1] // lanes):
        x = [part[:, q * lanes : (q + 1) * lanes] for part in parts]
        for top in range(2):
            pair = []
            for part in range(2):
                a, b = x[part], x[2 + part]
                if top == 0:
                    pair.append(jnp.where(low_half, a, pltpu.roll(b, 2 * gathers, 1)))
                else:
                    pair.append(jnp.where(low_half, pltpu.roll(a, 2 * gathers, 1), b))
            found.append(jnp.where(low_part, pair[0], pltpu.roll(pair[1], gathers, 1)))
            found.append(jnp.where(low_part, pltpu.roll(pair[0], lanes - gathers, 1), pair[1]))
    return found


def transform_kernel(pairs, gathers, chunks, table_ref, series_ref, out_ref, even, odd):
    blocks, rows, local_times = series_ref.shape
    step = table_ref.shape[0] // chunks
    half = local_times // 2
    for b in range(blocks):
        turned = series_ref[b].T
        even[b * half : (b + 1) * half] = turned[:half]
        odd[b * half : (b + 1) * half] = turned[half:]
    depth = blocks * half
    for i in range(chunks):
        own = slice(i * step, (i + 1) * step)
        evens = jnp.dot(table_ref[own, :depth], even[...], preferred_element_type=jnp.float32)
        odds = jnp.dot(table_ref[own, depth:], odd[...], preferred_element_type=jnp.float32)
        low = evens + odds
        high = evens - odds
        if len(out_ref.shape) == 3:
            row = lax.broadcasted_iota(jnp.int32, (step, 1), 0)
            out_ref[0, own] = low.astype(out_ref.dtype)
            out_ref[1, own] = jnp.where(
                row // pairs % 2 == 0, high, -high
            ).astype(out_ref.dtype)
            continue
        targets = step // (4 * pairs)
        devices = out_ref.shape[0]
        for d in range(targets):
            cuts = [slice((4 * d + c) * pairs, (4 * d + c + 1) * pairs) for c in range(4)]
            place = i * targets + d
            for h, value in enumerate(regroup([low[cut] for cut in cuts], gathers)):
                out_ref[place, h] = value.astype(out_ref.dtype)
            mirrored = [high[cuts[2]], -high[cuts[3]], high[cuts[0]], -high[cuts[1]]]
            for h, value in enumerate(regroup(mirrored, gathers)):
                out_ref[devices - 1 - place, h] = value.astype(out_ref.dtype)


def transform(table, series, pairs, gathers):
    columns, total_time = table.shape
    blocks, rows, local_times = series.shape
    own_offsets = rows // gathers
    devices = columns // (2 * pairs)
    final = (devices, own_offsets, pairs, 4 * gathers)
    chunks = 4
    aligned = rows % (4 * gathers) == 0 and pairs % 8 == 0 and devices % (2 * chunks) == 0
    vmem = pl.BlockSpec(memory_space=pltpu.VMEM)
    out = pl.pallas_call(
        functools.partial(transform_kernel, pairs, gathers, chunks),
        in_specs=[vmem, vmem],
        out_specs=vmem,
        out_shape=jax.ShapeDtypeStruct(final if aligned else (2, columns, rows), jnp.bfloat16),
        scratch_shapes=[
            pltpu.VMEM((total_time // 2, rows), jnp.bfloat16),
            pltpu.VMEM((total_time // 2, rows), jnp.bfloat16),
        ],
        compiler_params=pltpu.CompilerParams(vmem_limit_bytes=24 * MIB),
    )(table, series)
    if aligned:
        return out
    out = out.reshape(2, devices // 2, 2, 2, pairs, own_offsets, gathers)
    out = jnp.concatenate([out[0], jnp.flip(out[1], (0, 1))], axis=0)
    return out.transpose(0, 4, 3, 1, 2, 5).reshape(final)


def moveout_kernel(shift, total_time, base_ref, slow_ref, offs_ref, out_ref):
    spread = CURVATURE * slow_ref[...] * offs_ref[...]
    delay = jnp.sqrt(APEX_TIME * APEX_TIME + spread * spread) - APEX_TIME
    phase = base_ref[0] * delay
    c = jnp.cos(phase)
    s = jnp.sin(phase)
    far = delay * (2.0 * shift * math.pi / total_time)
    far_c = jnp.cos(far)
    far_s = jnp.sin(far)
    turn = delay * (2.0 * math.pi / total_time)
    out_ref[0] = c
    out_ref[1] = c * far_c - s * far_s
    out_ref[2] = s
    out_ref[3] = s * far_c + c * far_s
    out_ref[4] = jnp.cos(turn)
    out_ref[5] = jnp.sin(turn)


def moveout(base, slows, offs, shift, total_time):
    count = slows.shape[0]
    offsets = offs.shape[1]
    rows = min(count, 64)
    return pl.pallas_call(
        functools.partial(moveout_kernel, shift, total_time),
        grid=(count // rows,),
        in_specs=[
            pl.BlockSpec(memory_space=pltpu.SMEM),
            pl.BlockSpec((rows, 1), lambda i: (i, 0)),
            pl.BlockSpec((1, offsets), lambda i: (0, 0)),
        ],
        out_specs=pl.BlockSpec((6, rows, offsets), lambda i: (0, i, 0)),
        out_shape=jax.ShapeDtypeStruct((6, count, offsets), jnp.float32),
        compiler_params=pltpu.CompilerParams(vmem_limit_bytes=24 * MIB),
        cost_estimate=pl.CostEstimate(
            flops=300 * count * offsets,
            bytes_accessed=24 * count * offsets,
            transcendentals=6 * count * offsets,
        ),
    )(base, slows, offs)


def quotient(value, divisor):
    if divisor & (divisor - 1):
        return value // divisor
    return lax.shift_right_logical(value, jnp.int32(divisor.bit_length() - 1))


def remainder(value, divisor):
    if divisor & (divisor - 1):
        return value % divisor
    return value & (divisor - 1)


def one_hot(rows, columns, source):
    row = lax.broadcasted_iota(jnp.int32, (rows, 1), 0)
    column = lax.broadcasted_iota(jnp.int32, (rows, columns), 1)
    return jnp.where(column == source(row), 1.0, 0.0).astype(jnp.bfloat16)


TILE = 16


def prepare(gathers, down, data_ref, plain, turned):
    devices, own_offsets, pairs, lanes = data_ref.shape
    size = TILE * pairs
    together = TILE // own_offsets

    def received(r):
        k = quotient(r, TILE)
        return remainder(r, TILE) * pairs + k + down * (pairs - 1 - 2 * k)

    swap = one_hot(size, size, received)
    for d in range(devices // together):
        block = data_ref[d * together : (d + 1) * together].reshape(size, lanes)
        if pairs > 1:
            block = jnp.dot(swap, block, preferred_element_type=jnp.float32).astype(jnp.bfloat16)
        plain[:, d * TILE : (d + 1) * TILE] = block.reshape(pairs, TILE, lanes)
    row = lax.broadcasted_iota(jnp.int32, (lanes, lanes), 0)
    column = lax.broadcasted_iota(jnp.int32, (lanes, lanes), 1)
    quarter = jnp.where(
        remainder(column, 2 * gathers) < gathers,
        jnp.where(row == column + gathers, -1.0, 0.0),
        jnp.where(row == column - gathers, 1.0, 0.0),
    ).astype(jnp.bfloat16)
    for k in range(pairs):
        turned[k] = jnp.dot(plain[k], quarter, preferred_element_type=jnp.float32).astype(
            jnp.bfloat16
        )


def sum_offsets(gathers, first, state_ref, plain, turned, turns, held):
    pairs, slows, lanes = held.shape
    offsets = plain.shape[1]

    def fill(t, carry):
        source = pl.ds(pl.multiple_of(first + t * TILE, TILE), TILE)
        own = pl.ds(pl.multiple_of(t * TILE, TILE), TILE)
        step_c = state_ref[4, source]
        step_s = state_ref[5, source]
        twice = 2.0 * step_c
        now = [state_ref[i, source] for i in range(4)]
        past = [now[a] * step_c + now[2 + a] * step_s for a in range(2)]
        past += [now[2 + a] * step_c - now[a] * step_s for a in range(2)]
        for k in range(pairs):
            for i in range(4):
                turns[k, i, own] = now[i].astype(jnp.bfloat16)
                now[i], past[i] = twice * now[i] - past[i], now[i]
        return carry

    lax.fori_loop(0, slows // TILE, fill, 0)
    first_half = lax.broadcasted_iota(jnp.int32, (1, lanes), 1) < 2 * gathers
    for k in range(pairs):
        cosine = turns[k, :2].reshape(2 * slows, offsets)
        sines = turns[k, 2:].reshape(2 * slows, offsets)
        both = jnp.dot(cosine, plain[k], preferred_element_type=jnp.float32) + jnp.dot(
            sines, turned[k], preferred_element_type=jnp.float32
        )
        held[k] = jnp.where(first_half, both[:slows], both[slows:]).astype(jnp.bfloat16)


def deal(held, first, out_ref):
    pairs, _, lanes = held.shape
    size = TILE * pairs
    swap = one_hot(size, size, lambda r: remainder(r, pairs) * TILE + quotient(r, pairs))
    for p in range(out_ref.shape[0] // size):
        start = first + p * TILE
        if not isinstance(start, int):
            start = pl.multiple_of(start, TILE)
        block = held[:, pl.ds(start, TILE)].reshape(size, lanes)
        if pairs > 1:
            block = jnp.dot(swap, block, preferred_element_type=jnp.float32)
        out_ref[p * size : (p + 1) * size] = block.astype(out_ref.dtype)


def radon_kernel(gathers, down_ref, state_ref, data_ref, out_ref, turns, plain, turned, held):
    prepare(gathers, down_ref[0], data_ref, plain, turned)
    sum_offsets(gathers, 0, state_ref, plain, turned, turns, held)
    deal(held, 0, out_ref)


def radon(down, state, data, gathers):
    _, count, offsets = state.shape
    pairs, lanes = data.shape[2:]
    vmem = pl.BlockSpec(memory_space=pltpu.VMEM)
    return pl.pallas_call(
        functools.partial(radon_kernel, gathers),
        in_specs=[pl.BlockSpec(memory_space=pltpu.SMEM), vmem, vmem],
        out_specs=vmem,
        out_shape=jax.ShapeDtypeStruct((count * pairs, lanes), jnp.bfloat16),
        scratch_shapes=[
            pltpu.VMEM((pairs, 4, count, offsets), jnp.bfloat16),
            pltpu.VMEM((pairs, offsets, lanes), jnp.bfloat16),
            pltpu.VMEM((pairs, offsets, lanes), jnp.bfloat16),
            pltpu.VMEM((pairs, count, lanes), jnp.bfloat16),
        ],
        compiler_params=pltpu.CompilerParams(vmem_limit_bytes=24 * MIB),
    )(down, state, data)


def deal_half(held, me, first, out_refs):
    half = len(out_refs)
    each = held.shape[1] // half
    for s, out_ref in enumerate(out_refs):
        deal(held, remainder(me ^ (first + s), half) * each, out_ref)


def far_kernel(gathers, half, place_ref, state_ref, data_ref, plain, turned, *refs):
    *out_refs, turns, held = refs
    me = place_ref[1]
    prepare(gathers, place_ref[0], data_ref, plain, turned)
    other = (1 - quotient(me, half)) * held.shape[1]
    sum_offsets(gathers, other, state_ref, plain, turned, turns, held)
    deal_half(held, me, half, out_refs)


def near_kernel(gathers, half, place_ref, state_ref, plain, turned, *refs):
    *out_refs, turns, held = refs
    me = place_ref[1]
    own = quotient(me, half) * held.shape[1]
    sum_offsets(gathers, own, state_ref, plain, turned, turns, held)
    deal_half(held, me, 0, out_refs)


def radon_swapped(place, state, data, gathers, offset_devices):
    _, count, offsets = state.shape
    pairs, lanes = data.shape[2:]
    half = offset_devices // 2
    vmem = pl.BlockSpec(memory_space=pltpu.VMEM)
    smem = pl.BlockSpec(memory_space=pltpu.SMEM)
    block = jax.ShapeDtypeStruct((count // offset_devices * pairs, lanes), jnp.bfloat16)
    spectra = jax.ShapeDtypeStruct((pairs, offsets, lanes), jnp.bfloat16)
    scratch = [
        pltpu.VMEM((pairs, 4, count // 2, offsets), jnp.bfloat16),
        pltpu.VMEM((pairs, count // 2, lanes), jnp.bfloat16),
    ]
    cost = pl.CostEstimate(
        flops=8 * count * offsets * pairs * lanes,
        bytes_accessed=8 * count * offsets,
        transcendentals=0,
    )
    plain, turned, *far = pl.pallas_call(
        functools.partial(far_kernel, gathers, half),
        in_specs=[smem, vmem, vmem],
        out_specs=[vmem] * (2 + half),
        out_shape=[spectra, spectra] + [block] * half,
        scratch_shapes=scratch,
        compiler_params=pltpu.CompilerParams(vmem_limit_bytes=20 * MIB),
        cost_estimate=cost,
    )(place, state, data)
    near = pl.pallas_call(
        functools.partial(near_kernel, gathers, half),
        in_specs=[smem, vmem, vmem, vmem],
        out_specs=[vmem] * half,
        out_shape=[block] * half,
        scratch_shapes=scratch,
        compiler_params=pltpu.CompilerParams(vmem_limit_bytes=20 * MIB),
        cost_estimate=cost,
    )(place, state, plain, turned)
    blocks = list(near) + list(far)
    for s in reversed(range(1, offset_devices)):
        swaps = [(o, o ^ s) for o in range(offset_devices)]
        blocks[s] = lax.ppermute(blocks[s], "offset", swaps)
    return blocks


def join_kernel(scale, place_ref, *refs):
    *parts, out_ref, wide, ready, sems = refs
    groups, step, half_lanes, _ = ready.shape
    rows = wide.shape[1]
    pairs = rows // len(parts)
    copies = []
    for g in range(groups):
        for s, part in enumerate(parts):
            own = pl.ds(pl.multiple_of((place_ref[1] ^ s) * pairs, pairs), pairs)
            for i in range(step):
                p = g * step + i
                wide[p, own] = part[p * pairs : (p + 1) * pairs].astype(jnp.float32) * scale
        for i in range(step):
            block = wide[g * step + i].T
            ready[g, i, :, :rows] = block[:half_lanes]
            ready[g, i, :, rows:] = block[half_lanes:]
        copies.append(
            pltpu.make_async_copy(ready.at[g], out_ref.at[pl.ds(g * step, step)], sems.at[g])
        )
        copies[-1].start()
    for copy in copies:
        copy.wait()


def join(place, parts, slows, scale):
    pairs = parts[0].shape[0] // slows
    lanes = parts[0].shape[1]
    rows = len(parts) * pairs
    step = 4
    vmem = pl.BlockSpec(memory_space=pltpu.VMEM)
    return pl.pallas_call(
        functools.partial(join_kernel, scale),
        in_specs=[pl.BlockSpec(memory_space=pltpu.SMEM)] + [vmem] * len(parts),
        out_specs=pl.BlockSpec(memory_space=pl.ANY),
        out_shape=jax.ShapeDtypeStruct((slows, lanes // 2, 2 * rows), jnp.float32),
        scratch_shapes=[
            pltpu.VMEM((slows, rows, lanes), jnp.float32),
            pltpu.VMEM((slows // step, step, lanes // 2, 2 * rows), jnp.float32),
            pltpu.SemaphoreType.DMA((slows // step,)),
        ],
        compiler_params=pltpu.CompilerParams(vmem_limit_bytes=16 * MIB),
    )(place, *parts)


def finish_kernel(scale, in_ref, out_ref):
    devices, slows, pairs, lanes = in_ref.shape
    rows = devices * pairs
    for p in range(slows):
        block = in_ref[:, p].reshape(rows, lanes).astype(jnp.float32) * scale
        turned = block.T
        out_ref[p, :, :rows] = turned[: lanes // 2]
        out_ref[p, :, rows:] = turned[lanes // 2 :]


def finish(parts, scale):
    devices, slows, pairs, lanes = parts.shape
    rows = devices * pairs
    step = 8
    return pl.pallas_call(
        functools.partial(finish_kernel, scale),
        grid=(slows // step,),
        in_specs=[pl.BlockSpec((devices, step, pairs, lanes), lambda i: (0, i, 0, 0))],
        out_specs=pl.BlockSpec((step, lanes // 2, 2 * rows), lambda i: (i, 0, 0)),
        out_shape=jax.ShapeDtypeStruct((slows, lanes // 2, 2 * rows), jnp.float32),
        compiler_params=pltpu.CompilerParams(vmem_limit_bytes=32 * MIB),
    )(parts)


def local(raw_traces, trace_slot, offset_index, slowness_index):
    gathers, local_offsets = trace_slot.shape
    local_times = raw_traces.shape[1]
    freq_devices = lax.axis_size("freq")
    offset_devices = lax.axis_size("offset")
    devices = freq_devices * offset_devices
    total_time = local_times * freq_devices
    offsets = local_offsets * offset_devices
    band = NF // freq_devices
    own_freqs = NF // devices
    halves = 2
    pairs = own_freqs // halves
    own_offsets = local_offsets // freq_devices

    picked = pick(trace_slot.astype(jnp.float32), raw_traces, freq_devices)
    series = lax.all_to_all(picked, "freq", 0, 0, tiled=True)
    table = jnp.asarray(table_rows(total_time, freq_devices, offset_devices, halves, pairs))
    spectrum = transform(table, series, pairs, gathers)
    data = lax.all_to_all(spectrum, ("freq", "offset"), 0, 0, tiled=True)

    offs = offset_index.reshape(offset_devices, freq_devices, own_offsets)
    offs = offs.transpose(1, 0, 2).reshape(1, offsets).astype(jnp.float32)
    slows = slowness_index.astype(jnp.float32)[:, None]
    first = lax.axis_index("freq") * band + lax.axis_index("offset") * pairs
    base = (2 * first + 1).astype(jnp.float32) * (math.pi / total_time)
    state = moveout(base.reshape(1), slows, offs, band // halves, total_time)
    down = (2 * lax.axis_index("freq") // freq_devices).astype(jnp.int32)
    place = jnp.stack([down, lax.axis_index("offset").astype(jnp.int32)])
    slows_each = NP // offset_devices
    scale = 1.0 / math.sqrt(offsets)
    if slows_each % TILE == 0:
        blocks = radon_swapped(place, state, data, gathers, offset_devices)
        result = join(place, blocks, slows_each, scale)
    else:
        panel = radon(place, state, data, gathers)
        panel = panel.reshape(offset_devices, slows_each, pairs, 2 * halves * gathers)
        result = finish(lax.all_to_all(panel, "offset", 0, 0, tiled=True), scale)
    return jnp.transpose(result, (0, 2, 1))


def solution(mesh):
    placed = (P("offset", "freq"), P(None, "offset"), P(), P())
    return jax.shard_map(
        local, mesh=mesh, in_specs=placed, out_specs=P("offset", "freq", None), check_vma=False
    )
```

```python
import functools
import math

import jax
import jax.numpy as jnp
import ml_dtypes
import numpy as np
from jax import lax
from jax.experimental import pallas as pl
from jax.experimental.pallas import tpu as pltpu
from jax.sharding import PartitionSpec as P

NF = 1024
NP = 256
APEX_TIME = 100.0
CURVATURE = 0.0003
MIB = 1 << 20


def table_rows(total_time, freq_devices, offset_devices, halves, pairs):
    band = NF // freq_devices
    f, o, a, k = np.meshgrid(
        np.arange(freq_devices // 2),
        np.arange(offset_devices),
        np.arange(halves),
        np.arange(pairs),
        indexing="ij",
    )
    freq_ids = (f * band + a * (band // halves) + o * pairs + k).reshape(-1, pairs)
    times = np.concatenate([np.arange(0, total_time, 2), np.arange(1, total_time, 2)])
    turns = (2 * freq_ids[..., None] + 1) * times % (2 * total_time)
    angles = turns.astype(np.float32) * np.float32(math.pi / total_time)
    both = np.stack([np.cos(angles), -np.sin(angles)], axis=1).reshape(-1, total_time)
    return (both / np.float32(math.sqrt(total_time))).astype(ml_dtypes.bfloat16)


def pick_kernel(slot_ref, raw_ref, out_ref):
    gathers = slot_ref.shape[0]
    groups, rows, _ = out_ref.shape
    own_offsets = rows // gathers
    times = raw_ref.shape[1]
    half = times // 2
    row = lax.broadcasted_iota(jnp.int32, (times, times), 0)
    column = lax.broadcasted_iota(jnp.int32, (times, times), 1)
    source = jnp.where(column < half, 2 * column, 2 * (column - half) + 1)
    split = jnp.where(row == source, 1.0, 0.0).astype(jnp.bfloat16)
    raw = jnp.dot(raw_ref[...], split, preferred_element_type=jnp.float32).astype(jnp.bfloat16)
    lane = lax.broadcasted_iota(jnp.int32, (gathers, raw_ref.shape[0]), 1)
    for f in range(groups):
        picks = [
            jnp.where(lane == slot_ref[:, h : h + 1].astype(jnp.int32), 1.0, 0.0).astype(jnp.bfloat16)
            for h in range(f * own_offsets, (f + 1) * own_offsets)
        ]
        out_ref[f] = jnp.dot(
            jnp.concatenate(picks, axis=0), raw, preferred_element_type=jnp.float32
        ).astype(out_ref.dtype)


def pick(trace_slot, raw_traces, groups):
    gathers, local_offsets = trace_slot.shape
    rows = gathers * local_offsets // groups
    vmem = pl.BlockSpec(memory_space=pltpu.VMEM)
    return pl.pallas_call(
        pick_kernel,
        in_specs=[vmem, vmem],
        out_specs=vmem,
        out_shape=jax.ShapeDtypeStruct((groups, rows, raw_traces.shape[1]), raw_traces.dtype),
        compiler_params=pltpu.CompilerParams(vmem_limit_bytes=24 * MIB),
    )(trace_slot, raw_traces)


def regroup(parts, gathers):
    lanes = 4 * gathers
    lane = lax.broadcasted_iota(jnp.int32, (1, lanes), 1)
    low_half = lane < 2 * gathers
    low_part = lane % (2 * gathers) < gathers
    found = []
    for q in range(parts[0].shape[1] // lanes):
        x = [part[:, q * lanes : (q + 1) * lanes] for part in parts]
        for top in range(2):
            pair = []
            for part in range(2):
                a, b = x[part], x[2 + part]
                if top == 0:
                    pair.append(jnp.where(low_half, a, pltpu.roll(b, 2 * gathers, 1)))
                else:
                    pair.append(jnp.where(low_half, pltpu.roll(a, 2 * gathers, 1), b))
            found.append(jnp.where(low_part, pair[0], pltpu.roll(pair[1], gathers, 1)))
            found.append(jnp.where(low_part, pltpu.roll(pair[0], lanes - gathers, 1), pair[1]))
    return found


def transform_kernel(pairs, gathers, chunks, table_ref, series_ref, out_ref, even, odd):
    blocks, rows, local_times = series_ref.shape
    step = table_ref.shape[0] // chunks
    half = local_times // 2
    for b in range(blocks):
        turned = series_ref[b].T
        even[b * half : (b + 1) * half] = turned[:half]
        odd[b * half : (b + 1) * half] = turned[half:]
    depth = blocks * half
    for i in range(chunks):
        own = slice(i * step, (i + 1) * step)
        evens = jnp.dot(table_ref[own, :depth], even[...], preferred_element_type=jnp.float32)
        odds = jnp.dot(table_ref[own, depth:], odd[...], preferred_element_type=jnp.float32)
        low = evens + odds
        high = evens - odds
        if len(out_ref.shape) == 3:
            row = lax.broadcasted_iota(jnp.int32, (step, 1), 0)
            out_ref[0, own] = low.astype(out_ref.dtype)
            out_ref[1, own] = jnp.where(
                row // pairs % 2 == 0, high, -high
            ).astype(out_ref.dtype)
            continue
        targets = step // (4 * pairs)
        devices = out_ref.shape[0]
        for d in range(targets):
            cuts = [slice((4 * d + c) * pairs, (4 * d + c + 1) * pairs) for c in range(4)]
            place = i * targets + d
            for h, value in enumerate(regroup([low[cut] for cut in cuts], gathers)):
                out_ref[place, h] = value.astype(out_ref.dtype)
            mirrored = [high[cuts[2]], -high[cuts[3]], high[cuts[0]], -high[cuts[1]]]
            for h, value in enumerate(regroup(mirrored, gathers)):
                out_ref[devices - 1 - place, h] = value.astype(out_ref.dtype)


def transform(table, series, pairs, gathers):
    columns, total_time = table.shape
    blocks, rows, local_times = series.shape
    own_offsets = rows // gathers
    devices = columns // (2 * pairs)
    final = (devices, own_offsets, pairs, 4 * gathers)
    chunks = 4
    aligned = rows % (4 * gathers) == 0 and pairs % 8 == 0 and devices % (2 * chunks) == 0
    vmem = pl.BlockSpec(memory_space=pltpu.VMEM)
    out = pl.pallas_call(
        functools.partial(transform_kernel, pairs, gathers, chunks),
        in_specs=[vmem, vmem],
        out_specs=vmem,
        out_shape=jax.ShapeDtypeStruct(final if aligned else (2, columns, rows), jnp.bfloat16),
        scratch_shapes=[
            pltpu.VMEM((total_time // 2, rows), jnp.bfloat16),
            pltpu.VMEM((total_time // 2, rows), jnp.bfloat16),
        ],
        compiler_params=pltpu.CompilerParams(vmem_limit_bytes=24 * MIB),
    )(table, series)
    if aligned:
        return out
    out = out.reshape(2, devices // 2, 2, 2, pairs, own_offsets, gathers)
    out = jnp.concatenate([out[0], jnp.flip(out[1], (0, 1))], axis=0)
    return out.transpose(0, 4, 3, 1, 2, 5).reshape(final)


def moveout_kernel(shift, total_time, base_ref, slow_ref, offs_ref, out_ref):
    spread = CURVATURE * slow_ref[...] * offs_ref[...]
    delay = jnp.sqrt(APEX_TIME * APEX_TIME + spread * spread) - APEX_TIME
    phase = base_ref[0] * delay
    c = jnp.cos(phase)
    s = jnp.sin(phase)
    far = delay * (2.0 * shift * math.pi / total_time)
    far_c = jnp.cos(far)
    far_s = jnp.sin(far)
    turn = delay * (2.0 * math.pi / total_time)
    out_ref[0] = c
    out_ref[1] = c * far_c - s * far_s
    out_ref[2] = s
    out_ref[3] = s * far_c + c * far_s
    out_ref[4] = jnp.cos(turn)
    out_ref[5] = jnp.sin(turn)


def moveout(base, slows, offs, shift, total_time):
    count = slows.shape[0]
    offsets = offs.shape[1]
    rows = min(count, 64)
    return pl.pallas_call(
        functools.partial(moveout_kernel, shift, total_time),
        grid=(count // rows,),
        in_specs=[
            pl.BlockSpec(memory_space=pltpu.SMEM),
            pl.BlockSpec((rows, 1), lambda i: (i, 0)),
            pl.BlockSpec((1, offsets), lambda i: (0, 0)),
        ],
        out_specs=pl.BlockSpec((6, rows, offsets), lambda i: (0, i, 0)),
        out_shape=jax.ShapeDtypeStruct((6, count, offsets), jnp.float32),
        compiler_params=pltpu.CompilerParams(vmem_limit_bytes=24 * MIB),
        cost_estimate=pl.CostEstimate(
            flops=300 * count * offsets,
            bytes_accessed=24 * count * offsets,
            transcendentals=6 * count * offsets,
        ),
    )(base, slows, offs)


def quotient(value, divisor):
    if divisor & (divisor - 1):
        return value // divisor
    return lax.shift_right_logical(value, jnp.int32(divisor.bit_length() - 1))


def remainder(value, divisor):
    if divisor & (divisor - 1):
        return value % divisor
    return value & (divisor - 1)


def one_hot(rows, columns, source):
    row = lax.broadcasted_iota(jnp.int32, (rows, 1), 0)
    column = lax.broadcasted_iota(jnp.int32, (rows, columns), 1)
    return jnp.where(column == source(row), 1.0, 0.0).astype(jnp.bfloat16)


TILE = 16


def prepare(gathers, down, data_ref, plain, turned):
    devices, own_offsets, pairs, lanes = data_ref.shape
    size = TILE * pairs
    together = TILE // own_offsets

    def received(r):
        k = quotient(r, TILE)
        return remainder(r, TILE) * pairs + k + down * (pairs - 1 - 2 * k)

    swap = one_hot(size, size, received)
    for d in range(devices // together):
        block = data_ref[d * together : (d + 1) * together].reshape(size, lanes)
        if pairs > 1:
            block = jnp.dot(swap, block, preferred_element_type=jnp.float32).astype(jnp.bfloat16)
        plain[:, d * TILE : (d + 1) * TILE] = block.reshape(pairs, TILE, lanes)
    row = lax.broadcasted_iota(jnp.int32, (lanes, lanes), 0)
    column = lax.broadcasted_iota(jnp.int32, (lanes, lanes), 1)
    quarter = jnp.where(
        remainder(column, 2 * gathers) < gathers,
        jnp.where(row == column + gathers, -1.0, 0.0),
        jnp.where(row == column - gathers, 1.0, 0.0),
    ).astype(jnp.bfloat16)
    for k in range(pairs):
        turned[k] = jnp.dot(plain[k], quarter, preferred_element_type=jnp.float32).astype(
            jnp.bfloat16
        )


def sum_offsets(gathers, first, state_ref, plain, turned, turns, held):
    pairs, slows, lanes = held.shape
    offsets = plain.shape[1]

    def fill(t, carry):
        source = pl.ds(pl.multiple_of(first + t * TILE, TILE), TILE)
        own = pl.ds(pl.multiple_of(t * TILE, TILE), TILE)
        step_c = state_ref[4, source]
        step_s = state_ref[5, source]
        twice = 2.0 * step_c
        now = [state_ref[i, source] for i in range(4)]
        past = [now[a] * step_c + now[2 + a] * step_s for a in range(2)]
        past += [now[2 + a] * step_c - now[a] * step_s for a in range(2)]
        for k in range(pairs):
            for i in range(4):
                turns[k, i, own] = now[i].astype(jnp.bfloat16)
                now[i], past[i] = twice * now[i] - past[i], now[i]
        return carry

    lax.fori_loop(0, slows // TILE, fill, 0)
    first_half = lax.broadcasted_iota(jnp.int32, (1, lanes), 1) < 2 * gathers
    for k in range(pairs):
        cosine = turns[k, :2].reshape(2 * slows, offsets)
        sines = turns[k, 2:].reshape(2 * slows, offsets)
        both = jnp.dot(cosine, plain[k], preferred_element_type=jnp.float32) + jnp.dot(
            sines, turned[k], preferred_element_type=jnp.float32
        )
        held[k] = jnp.where(first_half, both[:slows], both[slows:]).astype(jnp.bfloat16)


def deal(held, first, out_ref):
    pairs, _, lanes = held.shape
    size = TILE * pairs
    swap = one_hot(size, size, lambda r: remainder(r, pairs) * TILE + quotient(r, pairs))
    for p in range(out_ref.shape[0] // size):
        start = first + p * TILE
        if not isinstance(start, int):
            start = pl.multiple_of(start, TILE)
        block = held[:, pl.ds(start, TILE)].reshape(size, lanes)
        if pairs > 1:
            block = jnp.dot(swap, block, preferred_element_type=jnp.float32)
        out_ref[p * size : (p + 1) * size] = block.astype(out_ref.dtype)


def radon_kernel(gathers, down_ref, state_ref, data_ref, out_ref, turns, plain, turned, held):
    prepare(gathers, down_ref[0], data_ref, plain, turned)
    sum_offsets(gathers, 0, state_ref, plain, turned, turns, held)
    deal(held, 0, out_ref)


def radon(down, state, data, gathers):
    _, count, offsets = state.shape
    pairs, lanes = data.shape[2:]
    vmem = pl.BlockSpec(memory_space=pltpu.VMEM)
    return pl.pallas_call(
        functools.partial(radon_kernel, gathers),
        in_specs=[pl.BlockSpec(memory_space=pltpu.SMEM), vmem, vmem],
        out_specs=vmem,
        out_shape=jax.ShapeDtypeStruct((count * pairs, lanes), jnp.bfloat16),
        scratch_shapes=[
            pltpu.VMEM((pairs, 4, count, offsets), jnp.bfloat16),
            pltpu.VMEM((pairs, offsets, lanes), jnp.bfloat16),
            pltpu.VMEM((pairs, offsets, lanes), jnp.bfloat16),
            pltpu.VMEM((pairs, count, lanes), jnp.bfloat16),
        ],
        compiler_params=pltpu.CompilerParams(vmem_limit_bytes=24 * MIB),
    )(down, state, data)


def deal_half(held, me, first, out_refs):
    half = len(out_refs)
    each = held.shape[1] // half
    for s, out_ref in enumerate(out_refs):
        deal(held, remainder(me ^ (first + s), half) * each, out_ref)


def far_kernel(gathers, half, place_ref, state_ref, data_ref, plain, turned, *refs):
    *out_refs, turns, held = refs
    me = place_ref[1]
    prepare(gathers, place_ref[0], data_ref, plain, turned)
    other = (1 - quotient(me, half)) * held.shape[1]
    sum_offsets(gathers, other, state_ref, plain, turned, turns, held)
    deal_half(held, me, half, out_refs)


def near_kernel(gathers, half, place_ref, state_ref, plain, turned, *refs):
    *out_refs, turns, held = refs
    me = place_ref[1]
    own = quotient(me, half) * held.shape[1]
    sum_offsets(gathers, own, state_ref, plain, turned, turns, held)
    deal_half(held, me, 0, out_refs)


def radon_swapped(place, state, data, gathers, offset_devices):
    _, count, offsets = state.shape
    pairs, lanes = data.shape[2:]
    half = offset_devices // 2
    vmem = pl.BlockSpec(memory_space=pltpu.VMEM)
    smem = pl.BlockSpec(memory_space=pltpu.SMEM)
    block = jax.ShapeDtypeStruct((count // offset_devices * pairs, lanes), jnp.bfloat16)
    spectra = jax.ShapeDtypeStruct((pairs, offsets, lanes), jnp.bfloat16)
    scratch = [
        pltpu.VMEM((pairs, 4, count // 2, offsets), jnp.bfloat16),
        pltpu.VMEM((pairs, count // 2, lanes), jnp.bfloat16),
    ]
    cost = pl.CostEstimate(
        flops=8 * count * offsets * pairs * lanes,
        bytes_accessed=8 * count * offsets,
        transcendentals=0,
    )
    plain, turned, *far = pl.pallas_call(
        functools.partial(far_kernel, gathers, half),
        in_specs=[smem, vmem, vmem],
        out_specs=[vmem] * (2 + half),
        out_shape=[spectra, spectra] + [block] * half,
        scratch_shapes=scratch,
        compiler_params=pltpu.CompilerParams(vmem_limit_bytes=20 * MIB),
        cost_estimate=cost,
    )(place, state, data)
    near = pl.pallas_call(
        functools.partial(near_kernel, gathers, half),
        in_specs=[smem, vmem, vmem, vmem],
        out_specs=[vmem] * half,
        out_shape=[block] * half,
        scratch_shapes=scratch,
        compiler_params=pltpu.CompilerParams(vmem_limit_bytes=20 * MIB),
        cost_estimate=cost,
    )(place, state, plain, turned)
    order = list(range(half, offset_devices)) + list(range(half))
    blocks = []
    for s, part in zip(order, list(far) + list(near)):
        swaps = [(o, o ^ s) for o in range(offset_devices)]
        blocks.append(lax.ppermute(part, "offset", swaps) if s else part)
    return order, blocks


def join_kernel(scale, order, place_ref, *refs):
    *parts, out_ref, wide, ready, sems = refs
    groups, step, half_lanes, _ = ready.shape
    rows = wide.shape[1]
    pairs = rows // len(parts)
    copies = []
    for g in range(groups):
        for s, part in zip(order, parts):
            own = pl.ds(pl.multiple_of((place_ref[1] ^ s) * pairs, pairs), pairs)
            for i in range(step):
                p = g * step + i
                wide[p, own] = part[p * pairs : (p + 1) * pairs].astype(jnp.float32) * scale
        for i in range(step):
            block = wide[g * step + i].T
            ready[g, i, :, :rows] = block[:half_lanes]
            ready[g, i, :, rows:] = block[half_lanes:]
        copies.append(
            pltpu.make_async_copy(ready.at[g], out_ref.at[pl.ds(g * step, step)], sems.at[g])
        )
        copies[-1].start()
    for copy in copies:
        copy.wait()


def join(place, order, parts, slows, scale):
    pairs = parts[0].shape[0] // slows
    lanes = parts[0].shape[1]
    rows = len(parts) * pairs
    step = 4
    vmem = pl.BlockSpec(memory_space=pltpu.VMEM)
    return pl.pallas_call(
        functools.partial(join_kernel, scale, order),
        in_specs=[pl.BlockSpec(memory_space=pltpu.SMEM)] + [vmem] * len(parts),
        out_specs=pl.BlockSpec(memory_space=pl.ANY),
        out_shape=jax.ShapeDtypeStruct((slows, lanes // 2, 2 * rows), jnp.float32),
        scratch_shapes=[
            pltpu.VMEM((slows, rows, lanes), jnp.float32),
            pltpu.VMEM((slows // step, step, lanes // 2, 2 * rows), jnp.float32),
            pltpu.SemaphoreType.DMA((slows // step,)),
        ],
        compiler_params=pltpu.CompilerParams(vmem_limit_bytes=16 * MIB),
    )(place, *parts)


def finish_kernel(scale, in_ref, out_ref):
    devices, slows, pairs, lanes = in_ref.shape
    rows = devices * pairs
    for p in range(slows):
        block = in_ref[:, p].reshape(rows, lanes).astype(jnp.float32) * scale
        turned = block.T
        out_ref[p, :, :rows] = turned[: lanes // 2]
        out_ref[p, :, rows:] = turned[lanes // 2 :]


def finish(parts, scale):
    devices, slows, pairs, lanes = parts.shape
    rows = devices * pairs
    step = 8
    return pl.pallas_call(
        functools.partial(finish_kernel, scale),
        grid=(slows // step,),
        in_specs=[pl.BlockSpec((devices, step, pairs, lanes), lambda i: (0, i, 0, 0))],
        out_specs=pl.BlockSpec((step, lanes // 2, 2 * rows), lambda i: (i, 0, 0)),
        out_shape=jax.ShapeDtypeStruct((slows, lanes // 2, 2 * rows), jnp.float32),
        compiler_params=pltpu.CompilerParams(vmem_limit_bytes=32 * MIB),
    )(parts)


def local(raw_traces, trace_slot, offset_index, slowness_index):
    gathers, local_offsets = trace_slot.shape
    local_times = raw_traces.shape[1]
    freq_devices = lax.axis_size("freq")
    offset_devices = lax.axis_size("offset")
    devices = freq_devices * offset_devices
    total_time = local_times * freq_devices
    offsets = local_offsets * offset_devices
    band = NF // freq_devices
    own_freqs = NF // devices
    halves = 2
    pairs = own_freqs // halves
    own_offsets = local_offsets // freq_devices

    picked = pick(trace_slot.astype(jnp.float32), raw_traces, freq_devices)
    series = lax.all_to_all(picked, "freq", 0, 0, tiled=True)
    table = jnp.asarray(table_rows(total_time, freq_devices, offset_devices, halves, pairs))
    spectrum = transform(table, series, pairs, gathers)
    data = lax.all_to_all(spectrum, ("freq", "offset"), 0, 0, tiled=True)

    offs = offset_index.reshape(offset_devices, freq_devices, own_offsets)
    offs = offs.transpose(1, 0, 2).reshape(1, offsets).astype(jnp.float32)
    slows = slowness_index.astype(jnp.float32)[:, None]
    first = lax.axis_index("freq") * band + lax.axis_index("offset") * pairs
    base = (2 * first + 1).astype(jnp.float32) * (math.pi / total_time)
    state = moveout(base.reshape(1), slows, offs, band // halves, total_time)
    down = (2 * lax.axis_index("freq") // freq_devices).astype(jnp.int32)
    place = jnp.stack([down, lax.axis_index("offset").astype(jnp.int32)])
    slows_each = NP // offset_devices
    scale = 1.0 / math.sqrt(offsets)
    if slows_each % TILE == 0:
        order, blocks = radon_swapped(place, state, data, gathers, offset_devices)
        result = join(place, order, blocks, slows_each, scale)
    else:
        panel = radon(place, state, data, gathers)
        panel = panel.reshape(offset_devices, slows_each, pairs, 2 * halves * gathers)
        result = finish(lax.all_to_all(panel, "offset", 0, 0, tiled=True), scale)
    return jnp.transpose(result, (0, 2, 1))


def solution(mesh):
    placed = (P("offset", "freq"), P(None, "offset"), P(), P())
    return jax.shard_map(
        local, mesh=mesh, in_specs=placed, out_specs=P("offset", "freq", None), check_vma=False
    )
```

```python
import functools
import math

import jax
import jax.numpy as jnp
import ml_dtypes
import numpy as np
from jax import lax
from jax.experimental import pallas as pl
from jax.experimental.pallas import tpu as pltpu
from jax.sharding import PartitionSpec as P

NF = 1024
NP = 256
APEX_TIME = 100.0
CURVATURE = 0.0003
MIB = 1 << 20


def table_rows(total_time, freq_devices, offset_devices, halves, pairs):
    band = NF // freq_devices
    f, o, a, k = np.meshgrid(
        np.arange(freq_devices // 2),
        np.arange(offset_devices),
        np.arange(halves),
        np.arange(pairs),
        indexing="ij",
    )
    freq_ids = (f * band + a * (band // halves) + o * pairs + k).reshape(-1, pairs)
    times = np.concatenate([np.arange(0, total_time, 2), np.arange(1, total_time, 2)])
    turns = (2 * freq_ids[..., None] + 1) * times % (2 * total_time)
    angles = turns.astype(np.float32) * np.float32(math.pi / total_time)
    both = np.stack([np.cos(angles), -np.sin(angles)], axis=1).reshape(-1, total_time)
    return (both / np.float32(math.sqrt(total_time))).astype(ml_dtypes.bfloat16)


def pick_kernel(slot_ref, raw_ref, out_ref):
    gathers = slot_ref.shape[0]
    groups, rows, _ = out_ref.shape
    own_offsets = rows // gathers
    times = raw_ref.shape[1]
    half = times // 2
    row = lax.broadcasted_iota(jnp.int32, (times, times), 0)
    column = lax.broadcasted_iota(jnp.int32, (times, times), 1)
    source = jnp.where(column < half, 2 * column, 2 * (column - half) + 1)
    split = jnp.where(row == source, 1.0, 0.0).astype(jnp.bfloat16)
    raw = jnp.dot(raw_ref[...], split, preferred_element_type=jnp.float32).astype(jnp.bfloat16)
    lane = lax.broadcasted_iota(jnp.int32, (gathers, raw_ref.shape[0]), 1)
    for f in range(groups):
        picks = [
            jnp.where(lane == slot_ref[:, h : h + 1].astype(jnp.int32), 1.0, 0.0).astype(jnp.bfloat16)
            for h in range(f * own_offsets, (f + 1) * own_offsets)
        ]
        out_ref[f] = jnp.dot(
            jnp.concatenate(picks, axis=0), raw, preferred_element_type=jnp.float32
        ).astype(out_ref.dtype)


def pick(trace_slot, raw_traces, groups):
    gathers, local_offsets = trace_slot.shape
    rows = gathers * local_offsets // groups
    vmem = pl.BlockSpec(memory_space=pltpu.VMEM)
    return pl.pallas_call(
        pick_kernel,
        in_specs=[vmem, vmem],
        out_specs=vmem,
        out_shape=jax.ShapeDtypeStruct((groups, rows, raw_traces.shape[1]), raw_traces.dtype),
        compiler_params=pltpu.CompilerParams(vmem_limit_bytes=24 * MIB),
    )(trace_slot, raw_traces)


def regroup(parts, gathers):
    lanes = 4 * gathers
    lane = lax.broadcasted_iota(jnp.int32, (1, lanes), 1)
    low_half = lane < 2 * gathers
    low_part = lane % (2 * gathers) < gathers
    found = []
    for q in range(parts[0].shape[1] // lanes):
        x = [part[:, q * lanes : (q + 1) * lanes] for part in parts]
        for top in range(2):
            pair = []
            for part in range(2):
                a, b = x[part], x[2 + part]
                if top == 0:
                    pair.append(jnp.where(low_half, a, pltpu.roll(b, 2 * gathers, 1)))
                else:
                    pair.append(jnp.where(low_half, pltpu.roll(a, 2 * gathers, 1), b))
            found.append(jnp.where(low_part, pair[0], pltpu.roll(pair[1], gathers, 1)))
            found.append(jnp.where(low_part, pltpu.roll(pair[0], lanes - gathers, 1), pair[1]))
    return found


def transform_kernel(pairs, gathers, chunks, table_ref, series_ref, out_ref, even, odd):
    blocks, rows, local_times = series_ref.shape
    step = table_ref.shape[0] // chunks
    half = local_times // 2
    for b in range(blocks):
        turned = series_ref[b].T
        even[b * half : (b + 1) * half] = turned[:half]
        odd[b * half : (b + 1) * half] = turned[half:]
    depth = blocks * half
    for i in range(chunks):
        own = slice(i * step, (i + 1) * step)
        evens = jnp.dot(table_ref[own, :depth], even[...], preferred_element_type=jnp.float32)
        odds = jnp.dot(table_ref[own, depth:], odd[...], preferred_element_type=jnp.float32)
        low = evens + odds
        high = evens - odds
        if len(out_ref.shape) == 3:
            row = lax.broadcasted_iota(jnp.int32, (step, 1), 0)
            out_ref[0, own] = low.astype(out_ref.dtype)
            out_ref[1, own] = jnp.where(
                row // pairs % 2 == 0, high, -high
            ).astype(out_ref.dtype)
            continue
        targets = step // (4 * pairs)
        devices = out_ref.shape[0]
        for d in range(targets):
            cuts = [slice((4 * d + c) * pairs, (4 * d + c + 1) * pairs) for c in range(4)]
            place = i * targets + d
            for h, value in enumerate(regroup([low[cut] for cut in cuts], gathers)):
                out_ref[place, h] = value.astype(out_ref.dtype)
            mirrored = [high[cuts[2]], -high[cuts[3]], high[cuts[0]], -high[cuts[1]]]
            for h, value in enumerate(regroup(mirrored, gathers)):
                out_ref[devices - 1 - place, h] = value.astype(out_ref.dtype)


def transform(table, series, pairs, gathers):
    columns, total_time = table.shape
    blocks, rows, local_times = series.shape
    own_offsets = rows // gathers
    devices = columns // (2 * pairs)
    final = (devices, own_offsets, pairs, 4 * gathers)
    chunks = 4
    aligned = rows % (4 * gathers) == 0 and pairs % 8 == 0 and devices % (2 * chunks) == 0
    vmem = pl.BlockSpec(memory_space=pltpu.VMEM)
    out = pl.pallas_call(
        functools.partial(transform_kernel, pairs, gathers, chunks),
        in_specs=[vmem, vmem],
        out_specs=vmem,
        out_shape=jax.ShapeDtypeStruct(final if aligned else (2, columns, rows), jnp.bfloat16),
        scratch_shapes=[
            pltpu.VMEM((total_time // 2, rows), jnp.bfloat16),
            pltpu.VMEM((total_time // 2, rows), jnp.bfloat16),
        ],
        compiler_params=pltpu.CompilerParams(vmem_limit_bytes=24 * MIB),
    )(table, series)
    if aligned:
        return out
    out = out.reshape(2, devices // 2, 2, 2, pairs, own_offsets, gathers)
    out = jnp.concatenate([out[0], jnp.flip(out[1], (0, 1))], axis=0)
    return out.transpose(0, 4, 3, 1, 2, 5).reshape(final)


def moveout_kernel(shift, total_time, base_ref, slow_ref, offs_ref, out_ref):
    spread = CURVATURE * slow_ref[...] * offs_ref[...]
    delay = jnp.sqrt(APEX_TIME * APEX_TIME + spread * spread) - APEX_TIME
    phase = base_ref[0] * delay
    c = jnp.cos(phase)
    s = jnp.sin(phase)
    far = delay * (2.0 * shift * math.pi / total_time)
    far_c = jnp.cos(far)
    far_s = jnp.sin(far)
    turn = delay * (2.0 * math.pi / total_time)
    out_ref[0] = c
    out_ref[1] = c * far_c - s * far_s
    out_ref[2] = s
    out_ref[3] = s * far_c + c * far_s
    out_ref[4] = jnp.cos(turn)
    out_ref[5] = jnp.sin(turn)


def moveout(base, slows, offs, shift, total_time):
    count = slows.shape[0]
    offsets = offs.shape[1]
    rows = min(count, 64)
    return pl.pallas_call(
        functools.partial(moveout_kernel, shift, total_time),
        grid=(count // rows,),
        in_specs=[
            pl.BlockSpec(memory_space=pltpu.SMEM),
            pl.BlockSpec((rows, 1), lambda i: (i, 0)),
            pl.BlockSpec((1, offsets), lambda i: (0, 0)),
        ],
        out_specs=pl.BlockSpec((6, rows, offsets), lambda i: (0, i, 0)),
        out_shape=jax.ShapeDtypeStruct((6, count, offsets), jnp.float32),
        compiler_params=pltpu.CompilerParams(vmem_limit_bytes=24 * MIB),
        cost_estimate=pl.CostEstimate(
            flops=300 * count * offsets,
            bytes_accessed=24 * count * offsets,
            transcendentals=6 * count * offsets,
        ),
    )(base, slows, offs)


def quotient(value, divisor):
    if divisor & (divisor - 1):
        return value // divisor
    return lax.shift_right_logical(value, jnp.int32(divisor.bit_length() - 1))


def remainder(value, divisor):
    if divisor & (divisor - 1):
        return value % divisor
    return value & (divisor - 1)


def one_hot(rows, columns, source):
    row = lax.broadcasted_iota(jnp.int32, (rows, 1), 0)
    column = lax.broadcasted_iota(jnp.int32, (rows, columns), 1)
    return jnp.where(column == source(row), 1.0, 0.0).astype(jnp.bfloat16)


TILE = 16


def prepare(gathers, down, data_ref, plain, turned):
    devices, own_offsets, pairs, lanes = data_ref.shape
    size = TILE * pairs
    together = TILE // own_offsets

    def received(r):
        k = quotient(r, TILE)
        return remainder(r, TILE) * pairs + k + down * (pairs - 1 - 2 * k)

    swap = one_hot(size, size, received)
    for d in range(devices // together):
        block = data_ref[d * together : (d + 1) * together].reshape(size, lanes)
        if pairs > 1:
            block = jnp.dot(swap, block, preferred_element_type=jnp.float32).astype(jnp.bfloat16)
        plain[:, d * TILE : (d + 1) * TILE] = block.reshape(pairs, TILE, lanes)
    row = lax.broadcasted_iota(jnp.int32, (lanes, lanes), 0)
    column = lax.broadcasted_iota(jnp.int32, (lanes, lanes), 1)
    quarter = jnp.where(
        remainder(column, 2 * gathers) < gathers,
        jnp.where(row == column + gathers, -1.0, 0.0),
        jnp.where(row == column - gathers, 1.0, 0.0),
    ).astype(jnp.bfloat16)
    for k in range(pairs):
        turned[k] = jnp.dot(plain[k], quarter, preferred_element_type=jnp.float32).astype(
            jnp.bfloat16
        )


def sum_offsets(gathers, first, state_ref, plain, turned, turns, held):
    pairs, slows, lanes = held.shape
    offsets = plain.shape[1]

    def fill(t, carry):
        source = pl.ds(pl.multiple_of(first + t * TILE, TILE), TILE)
        own = pl.ds(pl.multiple_of(t * TILE, TILE), TILE)
        step_c = state_ref[4, source]
        step_s = state_ref[5, source]
        twice = 2.0 * step_c
        now = [state_ref[i, source] for i in range(4)]
        past = [now[a] * step_c + now[2 + a] * step_s for a in range(2)]
        past += [now[2 + a] * step_c - now[a] * step_s for a in range(2)]
        for k in range(pairs):
            for i in range(4):
                turns[k, i, own] = now[i].astype(jnp.bfloat16)
                now[i], past[i] = twice * now[i] - past[i], now[i]
        return carry

    lax.fori_loop(0, slows // TILE, fill, 0)
    first_half = lax.broadcasted_iota(jnp.int32, (1, lanes), 1) < 2 * gathers
    for k in range(pairs):
        cosine = turns[k, :2].reshape(2 * slows, offsets)
        sines = turns[k, 2:].reshape(2 * slows, offsets)
        both = jnp.dot(cosine, plain[k], preferred_element_type=jnp.float32) + jnp.dot(
            sines, turned[k], preferred_element_type=jnp.float32
        )
        held[k] = jnp.where(first_half, both[:slows], both[slows:]).astype(jnp.bfloat16)


def deal(held, first, out_ref):
    pairs, _, lanes = held.shape
    size = TILE * pairs
    swap = one_hot(size, size, lambda r: remainder(r, pairs) * TILE + quotient(r, pairs))
    for p in range(out_ref.shape[0] // size):
        start = first + p * TILE
        if not isinstance(start, int):
            start = pl.multiple_of(start, TILE)
        block = held[:, pl.ds(start, TILE)].reshape(size, lanes)
        if pairs > 1:
            block = jnp.dot(swap, block, preferred_element_type=jnp.float32)
        out_ref[p * size : (p + 1) * size] = block.astype(out_ref.dtype)


def radon_kernel(gathers, down_ref, state_ref, data_ref, out_ref, turns, plain, turned, held):
    prepare(gathers, down_ref[0], data_ref, plain, turned)
    sum_offsets(gathers, 0, state_ref, plain, turned, turns, held)
    deal(held, 0, out_ref)


def radon(down, state, data, gathers):
    _, count, offsets = state.shape
    pairs, lanes = data.shape[2:]
    vmem = pl.BlockSpec(memory_space=pltpu.VMEM)
    return pl.pallas_call(
        functools.partial(radon_kernel, gathers),
        in_specs=[pl.BlockSpec(memory_space=pltpu.SMEM), vmem, vmem],
        out_specs=vmem,
        out_shape=jax.ShapeDtypeStruct((count * pairs, lanes), jnp.bfloat16),
        scratch_shapes=[
            pltpu.VMEM((pairs, 4, count, offsets), jnp.bfloat16),
            pltpu.VMEM((pairs, offsets, lanes), jnp.bfloat16),
            pltpu.VMEM((pairs, offsets, lanes), jnp.bfloat16),
            pltpu.VMEM((pairs, count, lanes), jnp.bfloat16),
        ],
        compiler_params=pltpu.CompilerParams(vmem_limit_bytes=24 * MIB),
    )(down, state, data)


def far_kernel(gathers, half, place_ref, state_ref, data_ref, plain, turned, *refs):
    *out_refs, turns, held = refs
    me = place_ref[1]
    prepare(gathers, place_ref[0], data_ref, plain, turned)
    other = (1 - quotient(me, half)) * held.shape[1]
    sum_offsets(gathers, other, state_ref, plain, turned, turns, held)
    for s, out_ref in enumerate(out_refs):
        deal(held, remainder(me ^ s, half) * (held.shape[1] // half), out_ref)


def near_kernel(gathers, half, place_ref, state_ref, plain, turned, out_ref, turns, held):
    own = quotient(place_ref[1], half) * held.shape[1]
    sum_offsets(gathers, own, state_ref, plain, turned, turns, held)
    for b in range(half):
        deal(held, b * (held.shape[1] // half), out_ref.at[b])


def radon_swapped(place, state, data, gathers, offset_devices):
    _, count, offsets = state.shape
    pairs, lanes = data.shape[2:]
    half = offset_devices // 2
    vmem = pl.BlockSpec(memory_space=pltpu.VMEM)
    smem = pl.BlockSpec(memory_space=pltpu.SMEM)
    block = jax.ShapeDtypeStruct((count // offset_devices * pairs, lanes), jnp.bfloat16)
    spectra = jax.ShapeDtypeStruct((pairs, offsets, lanes), jnp.bfloat16)
    scratch = [
        pltpu.VMEM((pairs, 4, count // 2, offsets), jnp.bfloat16),
        pltpu.VMEM((pairs, count // 2, lanes), jnp.bfloat16),
    ]
    cost = pl.CostEstimate(
        flops=8 * count * offsets * pairs * lanes,
        bytes_accessed=8 * count * offsets,
        transcendentals=0,
    )
    plain, turned, *far = pl.pallas_call(
        functools.partial(far_kernel, gathers, half),
        in_specs=[smem, vmem, vmem],
        out_specs=[vmem] * (2 + half),
        out_shape=[spectra, spectra] + [block] * half,
        scratch_shapes=scratch,
        compiler_params=pltpu.CompilerParams(vmem_limit_bytes=20 * MIB),
        cost_estimate=cost,
    )(place, state, data)
    near = pl.pallas_call(
        functools.partial(near_kernel, gathers, half),
        in_specs=[smem, vmem, vmem, vmem],
        out_specs=vmem,
        out_shape=jax.ShapeDtypeStruct((half,) + block.shape, block.dtype),
        scratch_shapes=scratch,
        compiler_params=pltpu.CompilerParams(vmem_limit_bytes=20 * MIB),
        cost_estimate=cost,
    )(place, state, plain, turned)
    blocks = []
    for s, part in enumerate(far):
        swaps = [(o, o ^ (half + s)) for o in range(offset_devices)]
        blocks.append(lax.ppermute(part, "offset", swaps))
    sides = [list(range(half)), list(range(half, offset_devices))]
    blocks.append(lax.all_to_all(near, "offset", 0, 0, axis_index_groups=sides, tiled=True))
    return blocks


def join_kernel(scale, place_ref, *refs):
    *far, near, out_ref, wide, ready, sems = refs
    half = len(far)
    me = place_ref[1]
    parts = [(me ^ (half + s), part) for s, part in enumerate(far)]
    parts += [(quotient(me, half) * half + b, near.at[b]) for b in range(half)]
    groups, step, half_lanes, _ = ready.shape
    rows = wide.shape[1]
    pairs = rows // len(parts)
    copies = []
    for g in range(groups):
        for source, part in parts:
            own = pl.ds(pl.multiple_of(source * pairs, pairs), pairs)
            for i in range(step):
                p = g * step + i
                wide[p, own] = part[p * pairs : (p + 1) * pairs].astype(jnp.float32) * scale
        for i in range(step):
            block = wide[g * step + i].T
            ready[g, i, :, :rows] = block[:half_lanes]
            ready[g, i, :, rows:] = block[half_lanes:]
        copies.append(
            pltpu.make_async_copy(ready.at[g], out_ref.at[pl.ds(g * step, step)], sems.at[g])
        )
        copies[-1].start()
    for copy in copies:
        copy.wait()


def join(place, parts, slows, scale):
    pairs = parts[0].shape[0] // slows
    lanes = parts[0].shape[1]
    rows = 2 * (len(parts) - 1) * pairs
    step = 4
    vmem = pl.BlockSpec(memory_space=pltpu.VMEM)
    return pl.pallas_call(
        functools.partial(join_kernel, scale),
        in_specs=[pl.BlockSpec(memory_space=pltpu.SMEM)] + [vmem] * len(parts),
        out_specs=pl.BlockSpec(memory_space=pl.ANY),
        out_shape=jax.ShapeDtypeStruct((slows, lanes // 2, 2 * rows), jnp.float32),
        scratch_shapes=[
            pltpu.VMEM((slows, rows, lanes), jnp.float32),
            pltpu.VMEM((slows // step, step, lanes // 2, 2 * rows), jnp.float32),
            pltpu.SemaphoreType.DMA((slows // step,)),
        ],
        compiler_params=pltpu.CompilerParams(vmem_limit_bytes=16 * MIB),
    )(place, *parts)


def finish_kernel(scale, in_ref, out_ref):
    devices, slows, pairs, lanes = in_ref.shape
    rows = devices * pairs
    for p in range(slows):
        block = in_ref[:, p].reshape(rows, lanes).astype(jnp.float32) * scale
        turned = block.T
        out_ref[p, :, :rows] = turned[: lanes // 2]
        out_ref[p, :, rows:] = turned[lanes // 2 :]


def finish(parts, scale):
    devices, slows, pairs, lanes = parts.shape
    rows = devices * pairs
    step = 8
    return pl.pallas_call(
        functools.partial(finish_kernel, scale),
        grid=(slows // step,),
        in_specs=[pl.BlockSpec((devices, step, pairs, lanes), lambda i: (0, i, 0, 0))],
        out_specs=pl.BlockSpec((step, lanes // 2, 2 * rows), lambda i: (i, 0, 0)),
        out_shape=jax.ShapeDtypeStruct((slows, lanes // 2, 2 * rows), jnp.float32),
        compiler_params=pltpu.CompilerParams(vmem_limit_bytes=32 * MIB),
    )(parts)


def local(raw_traces, trace_slot, offset_index, slowness_index):
    gathers, local_offsets = trace_slot.shape
    local_times = raw_traces.shape[1]
    freq_devices = lax.axis_size("freq")
    offset_devices = lax.axis_size("offset")
    devices = freq_devices * offset_devices
    total_time = local_times * freq_devices
    offsets = local_offsets * offset_devices
    band = NF // freq_devices
    own_freqs = NF // devices
    halves = 2
    pairs = own_freqs // halves
    own_offsets = local_offsets // freq_devices

    picked = pick(trace_slot.astype(jnp.float32), raw_traces, freq_devices)
    series = lax.all_to_all(picked, "freq", 0, 0, tiled=True)
    table = jnp.asarray(table_rows(total_time, freq_devices, offset_devices, halves, pairs))
    spectrum = transform(table, series, pairs, gathers)
    data = lax.all_to_all(spectrum, ("freq", "offset"), 0, 0, tiled=True)

    offs = offset_index.reshape(offset_devices, freq_devices, own_offsets)
    offs = offs.transpose(1, 0, 2).reshape(1, offsets).astype(jnp.float32)
    slows = slowness_index.astype(jnp.float32)[:, None]
    first = lax.axis_index("freq") * band + lax.axis_index("offset") * pairs
    base = (2 * first + 1).astype(jnp.float32) * (math.pi / total_time)
    state = moveout(base.reshape(1), slows, offs, band // halves, total_time)
    down = (2 * lax.axis_index("freq") // freq_devices).astype(jnp.int32)
    place = jnp.stack([down, lax.axis_index("offset").astype(jnp.int32)])
    slows_each = NP // offset_devices
    scale = 1.0 / math.sqrt(offsets)
    if slows_each % TILE == 0:
        blocks = radon_swapped(place, state, data, gathers, offset_devices)
        result = join(place, blocks, slows_each, scale)
    else:
        panel = radon(place, state, data, gathers)
        panel = panel.reshape(offset_devices, slows_each, pairs, 2 * halves * gathers)
        result = finish(lax.all_to_all(panel, "offset", 0, 0, tiled=True), scale)
    return jnp.transpose(result, (0, 2, 1))


def solution(mesh):
    placed = (P("offset", "freq"), P(None, "offset"), P(), P())
    return jax.shard_map(
        local, mesh=mesh, in_specs=placed, out_specs=P("offset", "freq", None), check_vma=False
    )
```

```python
import functools
import math

import jax
import jax.numpy as jnp
import ml_dtypes
import numpy as np
from jax import lax
from jax.experimental import pallas as pl
from jax.experimental.pallas import tpu as pltpu
from jax.sharding import PartitionSpec as P

NF = 1024
NP = 256
APEX_TIME = 100.0
CURVATURE = 0.0003
MIB = 1 << 20


def table_rows(total_time, freq_devices, offset_devices, halves, pairs):
    band = NF // freq_devices
    f, o, a, k = np.meshgrid(
        np.arange(freq_devices // 2),
        np.arange(offset_devices),
        np.arange(halves),
        np.arange(pairs),
        indexing="ij",
    )
    freq_ids = (f * band + a * (band // halves) + o * pairs + k).reshape(-1, pairs)
    times = np.concatenate([np.arange(0, total_time, 2), np.arange(1, total_time, 2)])
    turns = (2 * freq_ids[..., None] + 1) * times % (2 * total_time)
    angles = turns.astype(np.float32) * np.float32(math.pi / total_time)
    both = np.stack([np.cos(angles), -np.sin(angles)], axis=1).reshape(-1, total_time)
    return (both / np.float32(math.sqrt(total_time))).astype(ml_dtypes.bfloat16)


def pick_kernel(slot_ref, raw_ref, out_ref):
    gathers = slot_ref.shape[0]
    groups, rows, _ = out_ref.shape
    own_offsets = rows // gathers
    times = raw_ref.shape[1]
    half = times // 2
    row = lax.broadcasted_iota(jnp.int32, (times, times), 0)
    column = lax.broadcasted_iota(jnp.int32, (times, times), 1)
    source = jnp.where(column < half, 2 * column, 2 * (column - half) + 1)
    split = jnp.where(row == source, 1.0, 0.0).astype(jnp.bfloat16)
    raw = jnp.dot(raw_ref[...], split, preferred_element_type=jnp.float32).astype(jnp.bfloat16)
    lane = lax.broadcasted_iota(jnp.int32, (gathers, raw_ref.shape[0]), 1)
    for f in range(groups):
        picks = [
            jnp.where(lane == slot_ref[:, h : h + 1].astype(jnp.int32), 1.0, 0.0).astype(jnp.bfloat16)
            for h in range(f * own_offsets, (f + 1) * own_offsets)
        ]
        out_ref[f] = jnp.dot(
            jnp.concatenate(picks, axis=0), raw, preferred_element_type=jnp.float32
        ).astype(out_ref.dtype)


def pick(trace_slot, raw_traces, groups):
    gathers, local_offsets = trace_slot.shape
    rows = gathers * local_offsets // groups
    vmem = pl.BlockSpec(memory_space=pltpu.VMEM)
    return pl.pallas_call(
        pick_kernel,
        in_specs=[vmem, vmem],
        out_specs=vmem,
        out_shape=jax.ShapeDtypeStruct((groups, rows, raw_traces.shape[1]), raw_traces.dtype),
        compiler_params=pltpu.CompilerParams(vmem_limit_bytes=24 * MIB),
    )(trace_slot, raw_traces)


def regroup(parts, gathers):
    lanes = 4 * gathers
    lane = lax.broadcasted_iota(jnp.int32, (1, lanes), 1)
    low_half = lane < 2 * gathers
    low_part = lane % (2 * gathers) < gathers
    found = []
    for q in range(parts[0].shape[1] // lanes):
        x = [part[:, q * lanes : (q + 1) * lanes] for part in parts]
        for top in range(2):
            pair = []
            for part in range(2):
                a, b = x[part], x[2 + part]
                if top == 0:
                    pair.append(jnp.where(low_half, a, pltpu.roll(b, 2 * gathers, 1)))
                else:
                    pair.append(jnp.where(low_half, pltpu.roll(a, 2 * gathers, 1), b))
            found.append(jnp.where(low_part, pair[0], pltpu.roll(pair[1], gathers, 1)))
            found.append(jnp.where(low_part, pltpu.roll(pair[0], lanes - gathers, 1), pair[1]))
    return found


def transform_kernel(pairs, gathers, chunks, table_ref, series_ref, out_ref, even, odd):
    blocks, rows, local_times = series_ref.shape
    step = table_ref.shape[0] // chunks
    half = local_times // 2
    for b in range(blocks):
        turned = series_ref[b].T
        even[b * half : (b + 1) * half] = turned[:half]
        odd[b * half : (b + 1) * half] = turned[half:]
    depth = blocks * half
    for i in range(chunks):
        own = slice(i * step, (i + 1) * step)
        evens = jnp.dot(table_ref[own, :depth], even[...], preferred_element_type=jnp.float32)
        odds = jnp.dot(table_ref[own, depth:], odd[...], preferred_element_type=jnp.float32)
        low = evens + odds
        high = evens - odds
        if len(out_ref.shape) == 3:
            row = lax.broadcasted_iota(jnp.int32, (step, 1), 0)
            out_ref[0, own] = low.astype(out_ref.dtype)
            out_ref[1, own] = jnp.where(
                row // pairs % 2 == 0, high, -high
            ).astype(out_ref.dtype)
            continue
        targets = step // (4 * pairs)
        devices = out_ref.shape[0]
        for d in range(targets):
            cuts = [slice((4 * d + c) * pairs, (4 * d + c + 1) * pairs) for c in range(4)]
            place = i * targets + d
            for h, value in enumerate(regroup([low[cut] for cut in cuts], gathers)):
                out_ref[place, h] = value.astype(out_ref.dtype)
            mirrored = [high[cuts[2]], -high[cuts[3]], high[cuts[0]], -high[cuts[1]]]
            for h, value in enumerate(regroup(mirrored, gathers)):
                out_ref[devices - 1 - place, h] = value.astype(out_ref.dtype)


def transform(table, series, pairs, gathers):
    columns, total_time = table.shape
    blocks, rows, local_times = series.shape
    own_offsets = rows // gathers
    devices = columns // (2 * pairs)
    final = (devices, own_offsets, pairs, 4 * gathers)
    chunks = 4
    aligned = rows % (4 * gathers) == 0 and pairs % 8 == 0 and devices % (2 * chunks) == 0
    vmem = pl.BlockSpec(memory_space=pltpu.VMEM)
    out = pl.pallas_call(
        functools.partial(transform_kernel, pairs, gathers, chunks),
        in_specs=[vmem, vmem],
        out_specs=vmem,
        out_shape=jax.ShapeDtypeStruct(final if aligned else (2, columns, rows), jnp.bfloat16),
        scratch_shapes=[
            pltpu.VMEM((total_time // 2, rows), jnp.bfloat16),
            pltpu.VMEM((total_time // 2, rows), jnp.bfloat16),
        ],
        compiler_params=pltpu.CompilerParams(vmem_limit_bytes=24 * MIB),
    )(table, series)
    if aligned:
        return out
    out = out.reshape(2, devices // 2, 2, 2, pairs, own_offsets, gathers)
    out = jnp.concatenate([out[0], jnp.flip(out[1], (0, 1))], axis=0)
    return out.transpose(0, 4, 3, 1, 2, 5).reshape(final)


def moveout_kernel(shift, total_time, base_ref, slow_ref, offs_ref, out_ref):
    spread = CURVATURE * slow_ref[...] * offs_ref[...]
    delay = jnp.sqrt(APEX_TIME * APEX_TIME + spread * spread) - APEX_TIME
    phase = base_ref[0] * delay
    c = jnp.cos(phase)
    s = jnp.sin(phase)
    far = delay * (2.0 * shift * math.pi / total_time)
    far_c = jnp.cos(far)
    far_s = jnp.sin(far)
    turn = delay * (2.0 * math.pi / total_time)
    out_ref[0] = c
    out_ref[1] = c * far_c - s * far_s
    out_ref[2] = s
    out_ref[3] = s * far_c + c * far_s
    out_ref[4] = jnp.cos(turn)
    out_ref[5] = jnp.sin(turn)


def moveout(base, slows, offs, shift, total_time):
    count = slows.shape[0]
    offsets = offs.shape[1]
    rows = min(count, 64)
    return pl.pallas_call(
        functools.partial(moveout_kernel, shift, total_time),
        grid=(count // rows,),
        in_specs=[
            pl.BlockSpec(memory_space=pltpu.SMEM),
            pl.BlockSpec((rows, 1), lambda i: (i, 0)),
            pl.BlockSpec((1, offsets), lambda i: (0, 0)),
        ],
        out_specs=pl.BlockSpec((6, rows, offsets), lambda i: (0, i, 0)),
        out_shape=jax.ShapeDtypeStruct((6, count, offsets), jnp.float32),
        compiler_params=pltpu.CompilerParams(vmem_limit_bytes=24 * MIB),
        cost_estimate=pl.CostEstimate(
            flops=300 * count * offsets,
            bytes_accessed=24 * count * offsets,
            transcendentals=6 * count * offsets,
        ),
    )(base, slows, offs)


def quotient(value, divisor):
    if divisor & (divisor - 1):
        return value // divisor
    return lax.shift_right_logical(value, jnp.int32(divisor.bit_length() - 1))


def remainder(value, divisor):
    if divisor & (divisor - 1):
        return value % divisor
    return value & (divisor - 1)


def one_hot(rows, columns, source):
    row = lax.broadcasted_iota(jnp.int32, (rows, 1), 0)
    column = lax.broadcasted_iota(jnp.int32, (rows, columns), 1)
    return jnp.where(column == source(row), 1.0, 0.0).astype(jnp.bfloat16)


TILE = 16


def prepare(gathers, down, data_ref, plain, turned):
    devices, own_offsets, pairs, lanes = data_ref.shape
    size = TILE * pairs
    together = TILE // own_offsets

    def received(r):
        k = quotient(r, TILE)
        return remainder(r, TILE) * pairs + k + down * (pairs - 1 - 2 * k)

    swap = one_hot(size, size, received)
    for d in range(devices // together):
        block = data_ref[d * together : (d + 1) * together].reshape(size, lanes)
        if pairs > 1:
            block = jnp.dot(swap, block, preferred_element_type=jnp.float32).astype(jnp.bfloat16)
        plain[:, d * TILE : (d + 1) * TILE] = block.reshape(pairs, TILE, lanes)
    row = lax.broadcasted_iota(jnp.int32, (lanes, lanes), 0)
    column = lax.broadcasted_iota(jnp.int32, (lanes, lanes), 1)
    quarter = jnp.where(
        remainder(column, 2 * gathers) < gathers,
        jnp.where(row == column + gathers, -1.0, 0.0),
        jnp.where(row == column - gathers, 1.0, 0.0),
    ).astype(jnp.bfloat16)
    for k in range(pairs):
        turned[k] = jnp.dot(plain[k], quarter, preferred_element_type=jnp.float32).astype(
            jnp.bfloat16
        )


def sum_offsets(gathers, first, state_ref, plain, turned, turns, held):
    pairs, slows, lanes = held.shape
    offsets = plain.shape[1]

    def fill(t, carry):
        source = pl.ds(pl.multiple_of(first + t * TILE, TILE), TILE)
        own = pl.ds(pl.multiple_of(t * TILE, TILE), TILE)
        step_c = state_ref[4, source]
        step_s = state_ref[5, source]
        twice = 2.0 * step_c
        now = [state_ref[i, source] for i in range(4)]
        past = [now[a] * step_c + now[2 + a] * step_s for a in range(2)]
        past += [now[2 + a] * step_c - now[a] * step_s for a in range(2)]
        for k in range(pairs):
            for i in range(4):
                turns[k, i, own] = now[i].astype(jnp.bfloat16)
                now[i], past[i] = twice * now[i] - past[i], now[i]
        return carry

    lax.fori_loop(0, slows // TILE, fill, 0)
    first_half = lax.broadcasted_iota(jnp.int32, (1, lanes), 1) < 2 * gathers
    for k in range(pairs):
        cosine = turns[k, :2].reshape(2 * slows, offsets)
        sines = turns[k, 2:].reshape(2 * slows, offsets)
        both = jnp.dot(cosine, plain[k], preferred_element_type=jnp.float32) + jnp.dot(
            sines, turned[k], preferred_element_type=jnp.float32
        )
        held[k] = jnp.where(first_half, both[:slows], both[slows:]).astype(jnp.bfloat16)


def deal(held, first, out_ref):
    pairs, _, lanes = held.shape
    size = TILE * pairs
    swap = one_hot(size, size, lambda r: remainder(r, pairs) * TILE + quotient(r, pairs))
    for p in range(out_ref.shape[0] // size):
        start = first + p * TILE
        if not isinstance(start, int):
            start = pl.multiple_of(start, TILE)
        block = held[:, pl.ds(start, TILE)].reshape(size, lanes)
        if pairs > 1:
            block = jnp.dot(swap, block, preferred_element_type=jnp.float32)
        out_ref[p * size : (p + 1) * size] = block.astype(out_ref.dtype)


def radon_kernel(gathers, down_ref, state_ref, data_ref, out_ref, turns, plain, turned, held):
    prepare(gathers, down_ref[0], data_ref, plain, turned)
    sum_offsets(gathers, 0, state_ref, plain, turned, turns, held)
    deal(held, 0, out_ref)


def radon(down, state, data, gathers):
    _, count, offsets = state.shape
    pairs, lanes = data.shape[2:]
    vmem = pl.BlockSpec(memory_space=pltpu.VMEM)
    return pl.pallas_call(
        functools.partial(radon_kernel, gathers),
        in_specs=[pl.BlockSpec(memory_space=pltpu.SMEM), vmem, vmem],
        out_specs=vmem,
        out_shape=jax.ShapeDtypeStruct((count * pairs, lanes), jnp.bfloat16),
        scratch_shapes=[
            pltpu.VMEM((pairs, 4, count, offsets), jnp.bfloat16),
            pltpu.VMEM((pairs, offsets, lanes), jnp.bfloat16),
            pltpu.VMEM((pairs, offsets, lanes), jnp.bfloat16),
            pltpu.VMEM((pairs, count, lanes), jnp.bfloat16),
        ],
        compiler_params=pltpu.CompilerParams(vmem_limit_bytes=24 * MIB),
    )(down, state, data)


def deal_half(held, me, first, out_refs):
    half = len(out_refs)
    each = held.shape[1] // half
    for s, out_ref in enumerate(out_refs):
        deal(held, remainder(me ^ (first + s), half) * each, out_ref)


def far_kernel(gathers, half, place_ref, state_ref, data_ref, plain, turned, *refs):
    *out_refs, turns, held = refs
    me = place_ref[1]
    prepare(gathers, place_ref[0], data_ref, plain, turned)
    other = (1 - quotient(me, half)) * held.shape[1]
    sum_offsets(gathers, other, state_ref, plain, turned, turns, held)
    deal_half(held, me, half, out_refs)


def near_kernel(gathers, half, place_ref, state_ref, plain, turned, *refs):
    *out_refs, turns, held = refs
    me = place_ref[1]
    own = quotient(me, half) * held.shape[1]
    sum_offsets(gathers, own, state_ref, plain, turned, turns, held)
    deal_half(held, me, 0, out_refs)


def radon_swapped(place, state, data, gathers, offset_devices):
    _, count, offsets = state.shape
    pairs, lanes = data.shape[2:]
    half = offset_devices // 2
    vmem = pl.BlockSpec(memory_space=pltpu.VMEM)
    smem = pl.BlockSpec(memory_space=pltpu.SMEM)
    block = jax.ShapeDtypeStruct((count // offset_devices * pairs, lanes), jnp.bfloat16)
    spectra = jax.ShapeDtypeStruct((pairs, offsets, lanes), jnp.bfloat16)
    scratch = [
        pltpu.VMEM((pairs, 4, count // 2, offsets), jnp.bfloat16),
        pltpu.VMEM((pairs, count // 2, lanes), jnp.bfloat16),
    ]
    cost = pl.CostEstimate(
        flops=8 * count * offsets * pairs * lanes,
        bytes_accessed=8 * count * offsets,
        transcendentals=0,
    )
    plain, turned, *far = pl.pallas_call(
        functools.partial(far_kernel, gathers, half),
        in_specs=[smem, vmem, vmem],
        out_specs=[vmem] * (2 + half),
        out_shape=[spectra, spectra] + [block] * half,
        scratch_shapes=scratch,
        compiler_params=pltpu.CompilerParams(vmem_limit_bytes=20 * MIB),
        cost_estimate=cost,
    )(place, state, data)
    near = pl.pallas_call(
        functools.partial(near_kernel, gathers, half),
        in_specs=[smem, vmem, vmem, vmem],
        out_specs=[vmem] * half,
        out_shape=[block] * half,
        scratch_shapes=scratch,
        compiler_params=pltpu.CompilerParams(vmem_limit_bytes=20 * MIB),
        cost_estimate=cost,
    )(place, state, plain, turned)
    crossing = list(range(half, offset_devices))
    order = crossing[:-1] + list(range(2, half)) + crossing[-1:] + list(range(min(2, half)))[::-1]
    parts = list(near) + list(far)
    blocks = []
    for s in order:
        part = parts[s]
        swaps = [(o, o ^ s) for o in range(offset_devices)]
        blocks.append(lax.ppermute(part, "offset", swaps) if s else part)
    return order, blocks


def join_kernel(scale, order, place_ref, *refs):
    *parts, out_ref, wide, ready, sems = refs
    groups, step, half_lanes, _ = ready.shape
    rows = wide.shape[1]
    pairs = rows // len(parts)
    copies = []
    for g in range(groups):
        for s, part in zip(order, parts):
            own = pl.ds(pl.multiple_of((place_ref[1] ^ s) * pairs, pairs), pairs)
            for i in range(step):
                p = g * step + i
                wide[p, own] = part[p * pairs : (p + 1) * pairs].astype(jnp.float32) * scale
        for i in range(step):
            block = wide[g * step + i].T
            ready[g, i, :, :rows] = block[:half_lanes]
            ready[g, i, :, rows:] = block[half_lanes:]
        copies.append(
            pltpu.make_async_copy(ready.at[g], out_ref.at[pl.ds(g * step, step)], sems.at[g])
        )
        copies[-1].start()
    for copy in copies:
        copy.wait()


def join(place, order, parts, slows, scale):
    pairs = parts[0].shape[0] // slows
    lanes = parts[0].shape[1]
    rows = len(parts) * pairs
    step = 4
    vmem = pl.BlockSpec(memory_space=pltpu.VMEM)
    return pl.pallas_call(
        functools.partial(join_kernel, scale, order),
        in_specs=[pl.BlockSpec(memory_space=pltpu.SMEM)] + [vmem] * len(parts),
        out_specs=pl.BlockSpec(memory_space=pl.ANY),
        out_shape=jax.ShapeDtypeStruct((slows, lanes // 2, 2 * rows), jnp.float32),
        scratch_shapes=[
            pltpu.VMEM((slows, rows, lanes), jnp.float32),
            pltpu.VMEM((slows // step, step, lanes // 2, 2 * rows), jnp.float32),
            pltpu.SemaphoreType.DMA((slows // step,)),
        ],
        compiler_params=pltpu.CompilerParams(vmem_limit_bytes=16 * MIB),
    )(place, *parts)


def finish_kernel(scale, in_ref, out_ref):
    devices, slows, pairs, lanes = in_ref.shape
    rows = devices * pairs
    for p in range(slows):
        block = in_ref[:, p].reshape(rows, lanes).astype(jnp.float32) * scale
        turned = block.T
        out_ref[p, :, :rows] = turned[: lanes // 2]
        out_ref[p, :, rows:] = turned[lanes // 2 :]


def finish(parts, scale):
    devices, slows, pairs, lanes = parts.shape
    rows = devices * pairs
    step = 8
    return pl.pallas_call(
        functools.partial(finish_kernel, scale),
        grid=(slows // step,),
        in_specs=[pl.BlockSpec((devices, step, pairs, lanes), lambda i: (0, i, 0, 0))],
        out_specs=pl.BlockSpec((step, lanes // 2, 2 * rows), lambda i: (i, 0, 0)),
        out_shape=jax.ShapeDtypeStruct((slows, lanes // 2, 2 * rows), jnp.float32),
        compiler_params=pltpu.CompilerParams(vmem_limit_bytes=32 * MIB),
    )(parts)


def local(raw_traces, trace_slot, offset_index, slowness_index):
    gathers, local_offsets = trace_slot.shape
    local_times = raw_traces.shape[1]
    freq_devices = lax.axis_size("freq")
    offset_devices = lax.axis_size("offset")
    devices = freq_devices * offset_devices
    total_time = local_times * freq_devices
    offsets = local_offsets * offset_devices
    band = NF // freq_devices
    own_freqs = NF // devices
    halves = 2
    pairs = own_freqs // halves
    own_offsets = local_offsets // freq_devices

    picked = pick(trace_slot.astype(jnp.float32), raw_traces, freq_devices)
    series = lax.all_to_all(picked, "freq", 0, 0, tiled=True)
    table = jnp.asarray(table_rows(total_time, freq_devices, offset_devices, halves, pairs))
    spectrum = transform(table, series, pairs, gathers)
    data = lax.all_to_all(spectrum, ("freq", "offset"), 0, 0, tiled=True)

    offs = offset_index.reshape(offset_devices, freq_devices, own_offsets)
    offs = offs.transpose(1, 0, 2).reshape(1, offsets).astype(jnp.float32)
    slows = slowness_index.astype(jnp.float32)[:, None]
    first = lax.axis_index("freq") * band + lax.axis_index("offset") * pairs
    base = (2 * first + 1).astype(jnp.float32) * (math.pi / total_time)
    state = moveout(base.reshape(1), slows, offs, band // halves, total_time)
    down = (2 * lax.axis_index("freq") // freq_devices).astype(jnp.int32)
    place = jnp.stack([down, lax.axis_index("offset").astype(jnp.int32)])
    slows_each = NP // offset_devices
    scale = 1.0 / math.sqrt(offsets)
    if slows_each % TILE == 0:
        order, blocks = radon_swapped(place, state, data, gathers, offset_devices)
        result = join(place, order, blocks, slows_each, scale)
    else:
        panel = radon(place, state, data, gathers)
        panel = panel.reshape(offset_devices, slows_each, pairs, 2 * halves * gathers)
        result = finish(lax.all_to_all(panel, "offset", 0, 0, tiled=True), scale)
    return jnp.transpose(result, (0, 2, 1))


def solution(mesh):
    placed = (P("offset", "freq"), P(None, "offset"), P(), P())
    return jax.shard_map(
        local, mesh=mesh, in_specs=placed, out_specs=P("offset", "freq", None), check_vma=False
    )
```

```python
import functools
import math

import jax
import jax.numpy as jnp
import ml_dtypes
import numpy as np
from jax import lax
from jax.experimental import pallas as pl
from jax.experimental.pallas import tpu as pltpu
from jax.sharding import PartitionSpec as P

NF = 1024
NP = 256
APEX_TIME = 100.0
CURVATURE = 0.0003
MIB = 1 << 20


def table_rows(total_time, freq_devices, offset_devices, halves, pairs):
    band = NF // freq_devices
    f, o, a, k = np.meshgrid(
        np.arange(freq_devices // 2),
        np.arange(offset_devices),
        np.arange(halves),
        np.arange(pairs),
        indexing="ij",
    )
    freq_ids = (f * band + a * (band // halves) + o * pairs + k).reshape(-1, pairs)
    times = np.concatenate([np.arange(0, total_time, 2), np.arange(1, total_time, 2)])
    turns = (2 * freq_ids[..., None] + 1) * times % (2 * total_time)
    angles = turns.astype(np.float32) * np.float32(math.pi / total_time)
    both = np.stack([np.cos(angles), -np.sin(angles)], axis=1).reshape(-1, total_time)
    return (both / np.float32(math.sqrt(total_time))).astype(ml_dtypes.bfloat16)


def pick_kernel(me_ref, slot_ref, raw_ref, *out_refs):
    gathers, local_offsets = slot_ref.shape
    own_offsets = local_offsets // len(out_refs)
    times = raw_ref.shape[1]
    half = times // 2
    row = lax.broadcasted_iota(jnp.int32, (times, times), 0)
    column = lax.broadcasted_iota(jnp.int32, (times, times), 1)
    source = jnp.where(column < half, 2 * column, 2 * (column - half) + 1)
    split = jnp.where(row == source, 1.0, 0.0).astype(jnp.bfloat16)
    raw = jnp.dot(raw_ref[...], split, preferred_element_type=jnp.float32).astype(jnp.bfloat16)
    lane = lax.broadcasted_iota(jnp.int32, (gathers, raw_ref.shape[0]), 1)
    slot = slot_ref[...]
    place = lax.broadcasted_iota(jnp.int32, slot.shape, 1)
    for s, out_ref in enumerate(out_refs):
        first = (me_ref[0] ^ s) * own_offsets
        picks = []
        for h in range(own_offsets):
            wanted = jnp.sum(jnp.where(place == first + h, slot, 0.0), axis=1, keepdims=True)
            picks.append(
                jnp.where(lane == wanted.astype(jnp.int32), 1.0, 0.0).astype(jnp.bfloat16)
            )
        out_ref[...] = jnp.dot(
            jnp.concatenate(picks, axis=0), raw, preferred_element_type=jnp.float32
        ).astype(out_ref.dtype)


def pick(me, trace_slot, raw_traces, groups):
    gathers, local_offsets = trace_slot.shape
    rows = gathers * local_offsets // groups
    vmem = pl.BlockSpec(memory_space=pltpu.VMEM)
    block = jax.ShapeDtypeStruct((rows, raw_traces.shape[1]), raw_traces.dtype)
    return pl.pallas_call(
        pick_kernel,
        in_specs=[pl.BlockSpec(memory_space=pltpu.SMEM), vmem, vmem],
        out_specs=[vmem] * groups,
        out_shape=[block] * groups,
        compiler_params=pltpu.CompilerParams(vmem_limit_bytes=24 * MIB),
    )(me, trace_slot, raw_traces)


def regroup(parts, gathers):
    lanes = 4 * gathers
    lane = lax.broadcasted_iota(jnp.int32, (1, lanes), 1)
    low_half = lane < 2 * gathers
    low_part = lane % (2 * gathers) < gathers
    found = []
    for q in range(parts[0].shape[1] // lanes):
        x = [part[:, q * lanes : (q + 1) * lanes] for part in parts]
        for top in range(2):
            pair = []
            for part in range(2):
                a, b = x[part], x[2 + part]
                if top == 0:
                    pair.append(jnp.where(low_half, a, pltpu.roll(b, 2 * gathers, 1)))
                else:
                    pair.append(jnp.where(low_half, pltpu.roll(a, 2 * gathers, 1), b))
            found.append(jnp.where(low_part, pair[0], pltpu.roll(pair[1], gathers, 1)))
            found.append(jnp.where(low_part, pltpu.roll(pair[0], lanes - gathers, 1), pair[1]))
    return found


def time_sums(me, first, table_ref, series_refs, even, odd, own):
    half = even.shape[1] // 2
    depth = table_ref.shape[1] // 2
    evens = odds = None
    for r in range(len(series_refs) // 2):
        start = (quotient(me, 2) ^ (first + r)) * 2 * half
        even_part = jnp.dot(
            table_ref[own, pl.ds(pl.multiple_of(start, 2 * half), 2 * half)],
            even[r],
            preferred_element_type=jnp.float32,
        )
        odd_part = jnp.dot(
            table_ref[own, pl.ds(pl.multiple_of(depth + start, 2 * half), 2 * half)],
            odd[r],
            preferred_element_type=jnp.float32,
        )
        evens = even_part if evens is None else evens + even_part
        odds = odd_part if odds is None else odds + odd_part
    return evens, odds


def turn_series(me, series_refs, even, odd):
    half = even.shape[1] // 2
    for s, series_ref in enumerate(series_refs):
        turned = series_ref[...].T
        place = pl.ds(pl.multiple_of(((me ^ s) & 1) * half, half), half)
        even[s // 2, place] = turned[:half]
        odd[s // 2, place] = turned[half:]


def begin_kernel(chunks, me_ref, table_ref, *refs):
    *series_refs, out_ref, even, odd = refs
    me = me_ref[0]
    turn_series(me, series_refs, even, odd)
    step = table_ref.shape[0] // chunks
    for i in range(chunks):
        own = slice(i * step, (i + 1) * step)
        out_ref[0, own], out_ref[1, own] = time_sums(
            me, 0, table_ref, series_refs, even, odd, own
        )


def transform_kernel(pairs, gathers, chunks, me_ref, table_ref, begun_ref, *refs):
    *series_refs, out_ref, even, odd = refs
    me = me_ref[0]
    turn_series(me, series_refs, even, odd)
    step = table_ref.shape[0] // chunks
    for i in range(chunks):
        own = slice(i * step, (i + 1) * step)
        evens, odds = time_sums(me, 1, table_ref, series_refs, even, odd, own)
        evens = evens + begun_ref[0, own]
        odds = odds + begun_ref[1, own]
        low = evens + odds
        high = evens - odds
        if len(out_ref.shape) == 3:
            row = lax.broadcasted_iota(jnp.int32, (step, 1), 0)
            out_ref[0, own] = low.astype(out_ref.dtype)
            out_ref[1, own] = jnp.where(row // pairs % 2 == 0, high, -high).astype(out_ref.dtype)
            continue
        targets = step // (4 * pairs)
        devices = out_ref.shape[0]
        for d in range(targets):
            cuts = [slice((4 * d + c) * pairs, (4 * d + c + 1) * pairs) for c in range(4)]
            place = i * targets + d
            for h, value in enumerate(regroup([low[cut] for cut in cuts], gathers)):
                out_ref[place, h] = value.astype(out_ref.dtype)
            mirrored = [high[cuts[2]], -high[cuts[3]], high[cuts[0]], -high[cuts[1]]]
            for h, value in enumerate(regroup(mirrored, gathers)):
                out_ref[devices - 1 - place, h] = value.astype(out_ref.dtype)


def transform(me, table, series, pairs, gathers):
    columns, total_time = table.shape
    rows, local_times = series[0].shape
    own_offsets = rows // gathers
    devices = columns // (2 * pairs)
    final = (devices, own_offsets, pairs, 4 * gathers)
    chunks = 4
    aligned = rows % (4 * gathers) == 0 and pairs % 8 == 0 and devices % (2 * chunks) == 0
    vmem = pl.BlockSpec(memory_space=pltpu.VMEM)
    smem = pl.BlockSpec(memory_space=pltpu.SMEM)
    early, late = series[:2], series[2:]

    def scratch(blocks):
        return [pltpu.VMEM((len(blocks) // 2, local_times, rows), jnp.bfloat16)] * 2

    params = pltpu.CompilerParams(vmem_limit_bytes=24 * MIB)
    begun = pl.pallas_call(
        functools.partial(begin_kernel, chunks),
        in_specs=[smem] + [vmem] * (1 + len(early)),
        out_specs=vmem,
        out_shape=jax.ShapeDtypeStruct((2, columns, rows), jnp.float32),
        scratch_shapes=scratch(early),
        compiler_params=params,
        cost_estimate=pl.CostEstimate(
            flops=columns * total_time * rows,
            bytes_accessed=2 * columns * total_time,
            transcendentals=0,
        ),
    )(me, table, *early)
    out = pl.pallas_call(
        functools.partial(transform_kernel, pairs, gathers, chunks),
        in_specs=[smem] + [vmem] * (2 + len(late)),
        out_specs=vmem,
        out_shape=jax.ShapeDtypeStruct(final if aligned else (2, columns, rows), jnp.bfloat16),
        scratch_shapes=scratch(late),
        compiler_params=params,
    )(me, table, begun, *late)
    if aligned:
        return out
    out = out.reshape(2, devices // 2, 2, 2, pairs, own_offsets, gathers)
    out = jnp.concatenate([out[0], jnp.flip(out[1], (0, 1))], axis=0)
    return out.transpose(0, 4, 3, 1, 2, 5).reshape(final)


def moveout_kernel(shift, total_time, base_ref, slow_ref, offs_ref, out_ref):
    spread = CURVATURE * slow_ref[...] * offs_ref[...]
    delay = jnp.sqrt(APEX_TIME * APEX_TIME + spread * spread) - APEX_TIME
    phase = base_ref[0] * delay
    c = jnp.cos(phase)
    s = jnp.sin(phase)
    far = delay * (2.0 * shift * math.pi / total_time)
    far_c = jnp.cos(far)
    far_s = jnp.sin(far)
    turn = delay * (2.0 * math.pi / total_time)
    out_ref[0] = c
    out_ref[1] = c * far_c - s * far_s
    out_ref[2] = s
    out_ref[3] = s * far_c + c * far_s
    out_ref[4] = jnp.cos(turn)
    out_ref[5] = jnp.sin(turn)


def moveout(base, slows, offs, shift, total_time):
    count = slows.shape[0]
    offsets = offs.shape[1]
    rows = min(count, 64)
    return pl.pallas_call(
        functools.partial(moveout_kernel, shift, total_time),
        grid=(count // rows,),
        in_specs=[
            pl.BlockSpec(memory_space=pltpu.SMEM),
            pl.BlockSpec((rows, 1), lambda i: (i, 0)),
            pl.BlockSpec((1, offsets), lambda i: (0, 0)),
        ],
        out_specs=pl.BlockSpec((6, rows, offsets), lambda i: (0, i, 0)),
        out_shape=jax.ShapeDtypeStruct((6, count, offsets), jnp.float32),
        compiler_params=pltpu.CompilerParams(vmem_limit_bytes=24 * MIB),
        cost_estimate=pl.CostEstimate(
            flops=300 * count * offsets,
            bytes_accessed=24 * count * offsets,
            transcendentals=6 * count * offsets,
        ),
    )(base, slows, offs)


def quotient(value, divisor):
    if divisor & (divisor - 1):
        return value // divisor
    return lax.shift_right_logical(value, jnp.int32(divisor.bit_length() - 1))


def remainder(value, divisor):
    if divisor & (divisor - 1):
        return value % divisor
    return value & (divisor - 1)


def one_hot(rows, columns, source):
    row = lax.broadcasted_iota(jnp.int32, (rows, 1), 0)
    column = lax.broadcasted_iota(jnp.int32, (rows, columns), 1)
    return jnp.where(column == source(row), 1.0, 0.0).astype(jnp.bfloat16)


TILE = 16


def prepare(gathers, down, data_ref, plain, turned):
    devices, own_offsets, pairs, lanes = data_ref.shape
    size = TILE * pairs
    together = TILE // own_offsets

    def received(r):
        k = quotient(r, TILE)
        return remainder(r, TILE) * pairs + k + down * (pairs - 1 - 2 * k)

    swap = one_hot(size, size, received)
    for d in range(devices // together):
        block = data_ref[d * together : (d + 1) * together].reshape(size, lanes)
        if pairs > 1:
            block = jnp.dot(swap, block, preferred_element_type=jnp.float32).astype(jnp.bfloat16)
        plain[:, d * TILE : (d + 1) * TILE] = block.reshape(pairs, TILE, lanes)
    row = lax.broadcasted_iota(jnp.int32, (lanes, lanes), 0)
    column = lax.broadcasted_iota(jnp.int32, (lanes, lanes), 1)
    quarter = jnp.where(
        remainder(column, 2 * gathers) < gathers,
        jnp.where(row == column + gathers, -1.0, 0.0),
        jnp.where(row == column - gathers, 1.0, 0.0),
    ).astype(jnp.bfloat16)
    for k in range(pairs):
        turned[k] = jnp.dot(plain[k], quarter, preferred_element_type=jnp.float32).astype(
            jnp.bfloat16
        )


def sum_offsets(gathers, first, state_ref, plain, turned, turns, held):
    pairs, slows, lanes = held.shape
    offsets = plain.shape[1]

    def fill(t, carry):
        source = pl.ds(pl.multiple_of(first + t * TILE, TILE), TILE)
        own = pl.ds(pl.multiple_of(t * TILE, TILE), TILE)
        step_c = state_ref[4, source]
        step_s = state_ref[5, source]
        twice = 2.0 * step_c
        now = [state_ref[i, source] for i in range(4)]
        past = [now[a] * step_c + now[2 + a] * step_s for a in range(2)]
        past += [now[2 + a] * step_c - now[a] * step_s for a in range(2)]
        for k in range(pairs):
            for i in range(4):
                turns[k, i, own] = now[i].astype(jnp.bfloat16)
                now[i], past[i] = twice * now[i] - past[i], now[i]
        return carry

    lax.fori_loop(0, slows // TILE, fill, 0)
    first_half = lax.broadcasted_iota(jnp.int32, (1, lanes), 1) < 2 * gathers
    for k in range(pairs):
        cosine = turns[k, :2].reshape(2 * slows, offsets)
        sines = turns[k, 2:].reshape(2 * slows, offsets)
        both = jnp.dot(cosine, plain[k], preferred_element_type=jnp.float32) + jnp.dot(
            sines, turned[k], preferred_element_type=jnp.float32
        )
        held[k] = jnp.where(first_half, both[:slows], both[slows:]).astype(jnp.bfloat16)


def deal(held, first, out_ref):
    pairs, _, lanes = held.shape
    size = TILE * pairs
    swap = one_hot(size, size, lambda r: remainder(r, pairs) * TILE + quotient(r, pairs))
    for p in range(out_ref.shape[0] // size):
        start = first + p * TILE
        if not isinstance(start, int):
            start = pl.multiple_of(start, TILE)
        block = held[:, pl.ds(start, TILE)].reshape(size, lanes)
        if pairs > 1:
            block = jnp.dot(swap, block, preferred_element_type=jnp.float32)
        out_ref[p * size : (p + 1) * size] = block.astype(out_ref.dtype)


def radon_kernel(gathers, down_ref, state_ref, data_ref, out_ref, turns, plain, turned, held):
    prepare(gathers, down_ref[0], data_ref, plain, turned)
    sum_offsets(gathers, 0, state_ref, plain, turned, turns, held)
    deal(held, 0, out_ref)


def radon(down, state, data, gathers):
    _, count, offsets = state.shape
    pairs, lanes = data.shape[2:]
    vmem = pl.BlockSpec(memory_space=pltpu.VMEM)
    return pl.pallas_call(
        functools.partial(radon_kernel, gathers),
        in_specs=[pl.BlockSpec(memory_space=pltpu.SMEM), vmem, vmem],
        out_specs=vmem,
        out_shape=jax.ShapeDtypeStruct((count * pairs, lanes), jnp.bfloat16),
        scratch_shapes=[
            pltpu.VMEM((pairs, 4, count, offsets), jnp.bfloat16),
            pltpu.VMEM((pairs, offsets, lanes), jnp.bfloat16),
            pltpu.VMEM((pairs, offsets, lanes), jnp.bfloat16),
            pltpu.VMEM((pairs, count, lanes), jnp.bfloat16),
        ],
        compiler_params=pltpu.CompilerParams(vmem_limit_bytes=24 * MIB),
    )(down, state, data)


def deal_half(held, me, first, out_refs):
    half = len(out_refs)
    each = held.shape[1] // half
    for s, out_ref in enumerate(out_refs):
        deal(held, remainder(me ^ (first + s), half) * each, out_ref)


def far_kernel(gathers, half, place_ref, state_ref, data_ref, plain, turned, *refs):
    *out_refs, turns, held = refs
    me = place_ref[1]
    prepare(gathers, place_ref[0], data_ref, plain, turned)
    other = (1 - quotient(me, half)) * held.shape[1]
    sum_offsets(gathers, other, state_ref, plain, turned, turns, held)
    deal_half(held, me, half, out_refs)


def near_kernel(gathers, half, place_ref, state_ref, plain, turned, *refs):
    *out_refs, turns, held = refs
    me = place_ref[1]
    own = quotient(me, half) * held.shape[1]
    sum_offsets(gathers, own, state_ref, plain, turned, turns, held)
    deal_half(held, me, 0, out_refs)


def radon_swapped(place, state, data, gathers, offset_devices):
    _, count, offsets = state.shape
    pairs, lanes = data.shape[2:]
    half = offset_devices // 2
    vmem = pl.BlockSpec(memory_space=pltpu.VMEM)
    smem = pl.BlockSpec(memory_space=pltpu.SMEM)
    block = jax.ShapeDtypeStruct((count // offset_devices * pairs, lanes), jnp.bfloat16)
    spectra = jax.ShapeDtypeStruct((pairs, offsets, lanes), jnp.bfloat16)
    scratch = [
        pltpu.VMEM((pairs, 4, count // 2, offsets), jnp.bfloat16),
        pltpu.VMEM((pairs, count // 2, lanes), jnp.bfloat16),
    ]
    cost = pl.CostEstimate(
        flops=8 * count * offsets * pairs * lanes,
        bytes_accessed=8 * count * offsets,
        transcendentals=0,
    )
    plain, turned, *far = pl.pallas_call(
        functools.partial(far_kernel, gathers, half),
        in_specs=[smem, vmem, vmem],
        out_specs=[vmem] * (2 + half),
        out_shape=[spectra, spectra] + [block] * half,
        scratch_shapes=scratch,
        compiler_params=pltpu.CompilerParams(vmem_limit_bytes=20 * MIB),
        cost_estimate=cost,
    )(place, state, data)
    near = pl.pallas_call(
        functools.partial(near_kernel, gathers, half),
        in_specs=[smem, vmem, vmem, vmem],
        out_specs=[vmem] * half,
        out_shape=[block] * half,
        scratch_shapes=scratch,
        compiler_params=pltpu.CompilerParams(vmem_limit_bytes=20 * MIB),
        cost_estimate=cost,
    )(place, state, plain, turned)
    crossing = list(range(half, offset_devices))
    order = crossing[:-1] + list(range(2, half)) + crossing[-1:] + list(range(min(2, half)))[::-1]
    parts = list(near) + list(far)
    blocks = []
    for s in order:
        part = parts[s]
        swaps = [(o, o ^ s) for o in range(offset_devices)]
        blocks.append(lax.ppermute(part, "offset", swaps) if s else part)
    return order, blocks


def join_kernel(scale, order, place_ref, *refs):
    *parts, out_ref, wide, ready, sems = refs
    groups, step, half_lanes, _ = ready.shape
    rows = wide.shape[1]
    pairs = rows // len(parts)
    copies = []
    for g in range(groups):
        for s, part in zip(order, parts):
            own = pl.ds(pl.multiple_of((place_ref[1] ^ s) * pairs, pairs), pairs)
            for i in range(step):
                p = g * step + i
                wide[p, own] = part[p * pairs : (p + 1) * pairs].astype(jnp.float32) * scale
        for i in range(step):
            block = wide[g * step + i].T
            ready[g, i, :, :rows] = block[:half_lanes]
            ready[g, i, :, rows:] = block[half_lanes:]
        copies.append(
            pltpu.make_async_copy(ready.at[g], out_ref.at[pl.ds(g * step, step)], sems.at[g])
        )
        copies[-1].start()
    for copy in copies:
        copy.wait()


def join(place, order, parts, slows, scale):
    pairs = parts[0].shape[0] // slows
    lanes = parts[0].shape[1]
    rows = len(parts) * pairs
    step = 4
    vmem = pl.BlockSpec(memory_space=pltpu.VMEM)
    return pl.pallas_call(
        functools.partial(join_kernel, scale, order),
        in_specs=[pl.BlockSpec(memory_space=pltpu.SMEM)] + [vmem] * len(parts),
        out_specs=pl.BlockSpec(memory_space=pl.ANY),
        out_shape=jax.ShapeDtypeStruct((slows, lanes // 2, 2 * rows), jnp.float32),
        scratch_shapes=[
            pltpu.VMEM((slows, rows, lanes), jnp.float32),
            pltpu.VMEM((slows // step, step, lanes // 2, 2 * rows), jnp.float32),
            pltpu.SemaphoreType.DMA((slows // step,)),
        ],
        compiler_params=pltpu.CompilerParams(vmem_limit_bytes=16 * MIB),
    )(place, *parts)


def finish_kernel(scale, in_ref, out_ref):
    devices, slows, pairs, lanes = in_ref.shape
    rows = devices * pairs
    for p in range(slows):
        block = in_ref[:, p].reshape(rows, lanes).astype(jnp.float32) * scale
        turned = block.T
        out_ref[p, :, :rows] = turned[: lanes // 2]
        out_ref[p, :, rows:] = turned[lanes // 2 :]


def finish(parts, scale):
    devices, slows, pairs, lanes = parts.shape
    rows = devices * pairs
    step = 8
    return pl.pallas_call(
        functools.partial(finish_kernel, scale),
        grid=(slows // step,),
        in_specs=[pl.BlockSpec((devices, step, pairs, lanes), lambda i: (0, i, 0, 0))],
        out_specs=pl.BlockSpec((step, lanes // 2, 2 * rows), lambda i: (i, 0, 0)),
        out_shape=jax.ShapeDtypeStruct((slows, lanes // 2, 2 * rows), jnp.float32),
        compiler_params=pltpu.CompilerParams(vmem_limit_bytes=32 * MIB),
    )(parts)


def local(raw_traces, trace_slot, offset_index, slowness_index):
    gathers, local_offsets = trace_slot.shape
    local_times = raw_traces.shape[1]
    freq_devices = lax.axis_size("freq")
    offset_devices = lax.axis_size("offset")
    devices = freq_devices * offset_devices
    total_time = local_times * freq_devices
    offsets = local_offsets * offset_devices
    band = NF // freq_devices
    own_freqs = NF // devices
    halves = 2
    pairs = own_freqs // halves
    own_offsets = local_offsets // freq_devices

    me = lax.axis_index("freq").astype(jnp.int32).reshape(1)
    series = list(pick(me, trace_slot.astype(jnp.float32), raw_traces, freq_devices))
    for s in list(range(2, freq_devices)) + [1]:
        swaps = [(f, f ^ s) for f in range(freq_devices)]
        series[s] = lax.ppermute(series[s], "freq", swaps)
    table = jnp.asarray(table_rows(total_time, freq_devices, offset_devices, halves, pairs))
    spectrum = transform(me, table, series, pairs, gathers)
    data = lax.all_to_all(spectrum, ("freq", "offset"), 0, 0, tiled=True)

    offs = offset_index.reshape(offset_devices, freq_devices, own_offsets)
    offs = offs.transpose(1, 0, 2).reshape(1, offsets).astype(jnp.float32)
    slows = slowness_index.astype(jnp.float32)[:, None]
    first = lax.axis_index("freq") * band + lax.axis_index("offset") * pairs
    base = (2 * first + 1).astype(jnp.float32) * (math.pi / total_time)
    state = moveout(base.reshape(1), slows, offs, band // halves, total_time)
    down = (2 * lax.axis_index("freq") // freq_devices).astype(jnp.int32)
    place = jnp.stack([down, lax.axis_index("offset").astype(jnp.int32)])
    slows_each = NP // offset_devices
    scale = 1.0 / math.sqrt(offsets)
    if slows_each % TILE == 0:
        order, blocks = radon_swapped(place, state, data, gathers, offset_devices)
        result = join(place, order, blocks, slows_each, scale)
    else:
        panel = radon(place, state, data, gathers)
        panel = panel.reshape(offset_devices, slows_each, pairs, 2 * halves * gathers)
        result = finish(lax.all_to_all(panel, "offset", 0, 0, tiled=True), scale)
    return jnp.transpose(result, (0, 2, 1))


def solution(mesh):
    placed = (P("offset", "freq"), P(None, "offset"), P(), P())
    return jax.shard_map(
        local, mesh=mesh, in_specs=placed, out_specs=P("offset", "freq", None), check_vma=False
    )
```

```python
import functools
import math

import jax
import jax.numpy as jnp
import ml_dtypes
import numpy as np
from jax import lax
from jax.experimental import pallas as pl
from jax.experimental.pallas import tpu as pltpu
from jax.sharding import PartitionSpec as P

NF = 1024
NP = 256
APEX_TIME = 100.0
CURVATURE = 0.0003
MIB = 1 << 20


def table_rows(total_time, freq_devices, offset_devices, halves, pairs):
    band = NF // freq_devices
    f, o, a, k = np.meshgrid(
        np.arange(freq_devices // 2),
        np.arange(offset_devices),
        np.arange(halves),
        np.arange(pairs),
        indexing="ij",
    )
    freq_ids = (f * band + a * (band // halves) + o * pairs + k).reshape(-1, pairs)
    times = np.concatenate([np.arange(0, total_time, 2), np.arange(1, total_time, 2)])
    turns = (2 * freq_ids[..., None] + 1) * times % (2 * total_time)
    angles = turns.astype(np.float32) * np.float32(math.pi / total_time)
    both = np.stack([np.cos(angles), -np.sin(angles)], axis=1).reshape(-1, total_time)
    return (both / np.float32(math.sqrt(total_time))).astype(ml_dtypes.bfloat16)


def pick_kernel(me_ref, slot_ref, raw_ref, *out_refs):
    gathers, local_offsets = slot_ref.shape
    own_offsets = local_offsets // len(out_refs)
    times = raw_ref.shape[1]
    half = times // 2
    row = lax.broadcasted_iota(jnp.int32, (times, times), 0)
    column = lax.broadcasted_iota(jnp.int32, (times, times), 1)
    source = jnp.where(column < half, 2 * column, 2 * (column - half) + 1)
    split = jnp.where(row == source, 1.0, 0.0).astype(jnp.bfloat16)
    raw = jnp.dot(raw_ref[...], split, preferred_element_type=jnp.float32).astype(jnp.bfloat16)
    lane = lax.broadcasted_iota(jnp.int32, (gathers, raw_ref.shape[0]), 1)
    slot = slot_ref[...]
    place = lax.broadcasted_iota(jnp.int32, slot.shape, 1)
    for s, out_ref in enumerate(out_refs):
        first = (me_ref[0] ^ s) * own_offsets
        picks = []
        for h in range(own_offsets):
            wanted = jnp.sum(jnp.where(place == first + h, slot, 0.0), axis=1, keepdims=True)
            picks.append(
                jnp.where(lane == wanted.astype(jnp.int32), 1.0, 0.0).astype(jnp.bfloat16)
            )
        out_ref[...] = jnp.dot(
            jnp.concatenate(picks, axis=0), raw, preferred_element_type=jnp.float32
        ).astype(out_ref.dtype)


def pick(me, trace_slot, raw_traces, groups):
    gathers, local_offsets = trace_slot.shape
    rows = gathers * local_offsets // groups
    vmem = pl.BlockSpec(memory_space=pltpu.VMEM)
    block = jax.ShapeDtypeStruct((rows, raw_traces.shape[1]), raw_traces.dtype)
    return pl.pallas_call(
        pick_kernel,
        in_specs=[pl.BlockSpec(memory_space=pltpu.SMEM), vmem, vmem],
        out_specs=[vmem] * groups,
        out_shape=[block] * groups,
        compiler_params=pltpu.CompilerParams(vmem_limit_bytes=24 * MIB),
    )(me, trace_slot, raw_traces)


def regroup(parts, gathers):
    lanes = 4 * gathers
    lane = lax.broadcasted_iota(jnp.int32, (1, lanes), 1)
    low_half = lane < 2 * gathers
    low_part = lane % (2 * gathers) < gathers
    found = []
    for q in range(parts[0].shape[1] // lanes):
        x = [part[:, q * lanes : (q + 1) * lanes] for part in parts]
        for top in range(2):
            pair = []
            for part in range(2):
                a, b = x[part], x[2 + part]
                if top == 0:
                    pair.append(jnp.where(low_half, a, pltpu.roll(b, 2 * gathers, 1)))
                else:
                    pair.append(jnp.where(low_half, pltpu.roll(a, 2 * gathers, 1), b))
            found.append(jnp.where(low_part, pair[0], pltpu.roll(pair[1], gathers, 1)))
            found.append(jnp.where(low_part, pltpu.roll(pair[0], lanes - gathers, 1), pair[1]))
    return found


def time_sums(me, first, table_ref, series_refs, even, odd, own):
    half = even.shape[1] // 2
    depth = table_ref.shape[1] // 2
    evens = odds = None
    for r in range(len(series_refs) // 2):
        start = (quotient(me, 2) ^ (first + r)) * 2 * half
        even_part = jnp.dot(
            table_ref[own, pl.ds(pl.multiple_of(start, 2 * half), 2 * half)],
            even[r],
            preferred_element_type=jnp.float32,
        )
        odd_part = jnp.dot(
            table_ref[own, pl.ds(pl.multiple_of(depth + start, 2 * half), 2 * half)],
            odd[r],
            preferred_element_type=jnp.float32,
        )
        evens = even_part if evens is None else evens + even_part
        odds = odd_part if odds is None else odds + odd_part
    return evens, odds


def turn_series(me, series_refs, even, odd):
    half = even.shape[1] // 2
    for s, series_ref in enumerate(series_refs):
        turned = series_ref[...].T
        place = pl.ds(pl.multiple_of(((me ^ s) & 1) * half, half), half)
        even[s // 2, place] = turned[:half]
        odd[s // 2, place] = turned[half:]


def begin_kernel(chunks, me_ref, table_ref, *refs):
    *series_refs, out_ref, even, odd = refs
    me = me_ref[0]
    turn_series(me, series_refs, even, odd)
    step = table_ref.shape[0] // chunks
    for i in range(chunks):
        own = slice(i * step, (i + 1) * step)
        out_ref[0, own], out_ref[1, own] = time_sums(
            me, 0, table_ref, series_refs, even, odd, own
        )


def transform_kernel(pairs, gathers, chunks, me_ref, table_ref, begun_ref, *refs):
    *series_refs, out_ref, even, odd = refs
    me = me_ref[0]
    turn_series(me, series_refs, even, odd)
    step = table_ref.shape[0] // chunks
    for i in range(chunks):
        own = slice(i * step, (i + 1) * step)
        evens, odds = time_sums(me, 1, table_ref, series_refs, even, odd, own)
        evens = evens + begun_ref[0, own]
        odds = odds + begun_ref[1, own]
        low = evens + odds
        high = evens - odds
        if len(out_ref.shape) == 3:
            row = lax.broadcasted_iota(jnp.int32, (step, 1), 0)
            out_ref[0, own] = low.astype(out_ref.dtype)
            out_ref[1, own] = jnp.where(row // pairs % 2 == 0, high, -high).astype(out_ref.dtype)
            continue
        targets = step // (4 * pairs)
        devices = out_ref.shape[0]
        for d in range(targets):
            cuts = [slice((4 * d + c) * pairs, (4 * d + c + 1) * pairs) for c in range(4)]
            place = i * targets + d
            for h, value in enumerate(regroup([low[cut] for cut in cuts], gathers)):
                out_ref[place, h] = value.astype(out_ref.dtype)
            mirrored = [high[cuts[2]], -high[cuts[3]], high[cuts[0]], -high[cuts[1]]]
            for h, value in enumerate(regroup(mirrored, gathers)):
                out_ref[devices - 1 - place, h] = value.astype(out_ref.dtype)


def transform(me, table, series, pairs, gathers):
    columns, total_time = table.shape
    rows, local_times = series[0].shape
    own_offsets = rows // gathers
    devices = columns // (2 * pairs)
    final = (devices, own_offsets, pairs, 4 * gathers)
    chunks = 4
    aligned = rows % (4 * gathers) == 0 and pairs % 8 == 0 and devices % (2 * chunks) == 0
    vmem = pl.BlockSpec(memory_space=pltpu.VMEM)
    smem = pl.BlockSpec(memory_space=pltpu.SMEM)
    early, late = series[:2], series[2:]

    def scratch(blocks):
        return [pltpu.VMEM((len(blocks) // 2, local_times, rows), jnp.bfloat16)] * 2

    params = pltpu.CompilerParams(vmem_limit_bytes=24 * MIB)
    begun = pl.pallas_call(
        functools.partial(begin_kernel, chunks),
        in_specs=[smem] + [vmem] * (1 + len(early)),
        out_specs=vmem,
        out_shape=jax.ShapeDtypeStruct((2, columns, rows), jnp.float32),
        scratch_shapes=scratch(early),
        compiler_params=params,
        cost_estimate=pl.CostEstimate(
            flops=columns * total_time * rows,
            bytes_accessed=2 * columns * total_time,
            transcendentals=0,
        ),
    )(me, table, *early)
    out = pl.pallas_call(
        functools.partial(transform_kernel, pairs, gathers, chunks),
        in_specs=[smem] + [vmem] * (2 + len(late)),
        out_specs=vmem,
        out_shape=jax.ShapeDtypeStruct(final if aligned else (2, columns, rows), jnp.bfloat16),
        scratch_shapes=scratch(late),
        compiler_params=params,
    )(me, table, begun, *late)
    if aligned:
        return out
    out = out.reshape(2, devices // 2, 2, 2, pairs, own_offsets, gathers)
    out = jnp.concatenate([out[0], jnp.flip(out[1], (0, 1))], axis=0)
    return out.transpose(0, 4, 3, 1, 2, 5).reshape(final)


def moveout_kernel(shift, total_time, base_ref, slow_ref, offs_ref, out_ref):
    spread = CURVATURE * slow_ref[...] * offs_ref[...]
    delay = jnp.sqrt(APEX_TIME * APEX_TIME + spread * spread) - APEX_TIME
    phase = base_ref[0] * delay
    c = jnp.cos(phase)
    s = jnp.sin(phase)
    far = delay * (2.0 * shift * math.pi / total_time)
    far_c = jnp.cos(far)
    far_s = jnp.sin(far)
    turn = delay * (2.0 * math.pi / total_time)
    out_ref[0] = c
    out_ref[1] = c * far_c - s * far_s
    out_ref[2] = s
    out_ref[3] = s * far_c + c * far_s
    out_ref[4] = jnp.cos(turn)
    out_ref[5] = jnp.sin(turn)


def moveout(base, slows, offs, shift, total_time):
    count = slows.shape[0]
    offsets = offs.shape[1]
    rows = min(count, 64)
    return pl.pallas_call(
        functools.partial(moveout_kernel, shift, total_time),
        grid=(count // rows,),
        in_specs=[
            pl.BlockSpec(memory_space=pltpu.SMEM),
            pl.BlockSpec((rows, 1), lambda i: (i, 0)),
            pl.BlockSpec((1, offsets), lambda i: (0, 0)),
        ],
        out_specs=pl.BlockSpec((6, rows, offsets), lambda i: (0, i, 0)),
        out_shape=jax.ShapeDtypeStruct((6, count, offsets), jnp.float32),
        compiler_params=pltpu.CompilerParams(vmem_limit_bytes=24 * MIB),
        cost_estimate=pl.CostEstimate(
            flops=300 * count * offsets,
            bytes_accessed=24 * count * offsets,
            transcendentals=6 * count * offsets,
        ),
    )(base, slows, offs)


def quotient(value, divisor):
    if divisor & (divisor - 1):
        return value // divisor
    return lax.shift_right_logical(value, jnp.int32(divisor.bit_length() - 1))


def remainder(value, divisor):
    if divisor & (divisor - 1):
        return value % divisor
    return value & (divisor - 1)


def one_hot(rows, columns, source):
    row = lax.broadcasted_iota(jnp.int32, (rows, 1), 0)
    column = lax.broadcasted_iota(jnp.int32, (rows, columns), 1)
    return jnp.where(column == source(row), 1.0, 0.0).astype(jnp.bfloat16)


TILE = 16


def prepare(gathers, down, data_ref, plain, turned):
    devices, own_offsets, pairs, lanes = data_ref.shape
    size = TILE * pairs
    together = TILE // own_offsets

    def received(r):
        k = quotient(r, TILE)
        return remainder(r, TILE) * pairs + k + down * (pairs - 1 - 2 * k)

    swap = one_hot(size, size, received)
    for d in range(devices // together):
        block = data_ref[d * together : (d + 1) * together].reshape(size, lanes)
        if pairs > 1:
            block = jnp.dot(swap, block, preferred_element_type=jnp.float32).astype(jnp.bfloat16)
        plain[:, d * TILE : (d + 1) * TILE] = block.reshape(pairs, TILE, lanes)
    row = lax.broadcasted_iota(jnp.int32, (lanes, lanes), 0)
    column = lax.broadcasted_iota(jnp.int32, (lanes, lanes), 1)
    quarter = jnp.where(
        remainder(column, 2 * gathers) < gathers,
        jnp.where(row == column + gathers, -1.0, 0.0),
        jnp.where(row == column - gathers, 1.0, 0.0),
    ).astype(jnp.bfloat16)
    for k in range(pairs):
        turned[k] = jnp.dot(plain[k], quarter, preferred_element_type=jnp.float32).astype(
            jnp.bfloat16
        )


def sum_offsets(gathers, first, state_ref, plain, turned, turns, held):
    pairs, slows, lanes = held.shape
    offsets = plain.shape[1]

    def fill(t, carry):
        source = pl.ds(pl.multiple_of(first + t * TILE, TILE), TILE)
        own = pl.ds(pl.multiple_of(t * TILE, TILE), TILE)
        step_c = state_ref[4, source]
        step_s = state_ref[5, source]
        twice = 2.0 * step_c
        now = [state_ref[i, source] for i in range(4)]
        past = [now[a] * step_c + now[2 + a] * step_s for a in range(2)]
        past += [now[2 + a] * step_c - now[a] * step_s for a in range(2)]
        for k in range(pairs):
            for i in range(4):
                turns[k, i, own] = now[i].astype(jnp.bfloat16)
                now[i], past[i] = twice * now[i] - past[i], now[i]
        return carry

    lax.fori_loop(0, slows // TILE, fill, 0)
    first_half = lax.broadcasted_iota(jnp.int32, (1, lanes), 1) < 2 * gathers
    for k in range(pairs):
        cosine = turns[k, :2].reshape(2 * slows, offsets)
        sines = turns[k, 2:].reshape(2 * slows, offsets)
        both = jnp.dot(cosine, plain[k], preferred_element_type=jnp.float32) + jnp.dot(
            sines, turned[k], preferred_element_type=jnp.float32
        )
        held[k] = jnp.where(first_half, both[:slows], both[slows:]).astype(jnp.bfloat16)


def deal(held, first, out_ref):
    pairs, _, lanes = held.shape
    size = TILE * pairs
    swap = one_hot(size, size, lambda r: remainder(r, pairs) * TILE + quotient(r, pairs))
    for p in range(out_ref.shape[0] // size):
        start = first + p * TILE
        if not isinstance(start, int):
            start = pl.multiple_of(start, TILE)
        block = held[:, pl.ds(start, TILE)].reshape(size, lanes)
        if pairs > 1:
            block = jnp.dot(swap, block, preferred_element_type=jnp.float32)
        out_ref[p * size : (p + 1) * size] = block.astype(out_ref.dtype)


def radon_kernel(gathers, down_ref, state_ref, data_ref, out_ref, turns, plain, turned, held):
    prepare(gathers, down_ref[0], data_ref, plain, turned)
    sum_offsets(gathers, 0, state_ref, plain, turned, turns, held)
    deal(held, 0, out_ref)


def radon(down, state, data, gathers):
    _, count, offsets = state.shape
    pairs, lanes = data.shape[2:]
    vmem = pl.BlockSpec(memory_space=pltpu.VMEM)
    return pl.pallas_call(
        functools.partial(radon_kernel, gathers),
        in_specs=[pl.BlockSpec(memory_space=pltpu.SMEM), vmem, vmem],
        out_specs=vmem,
        out_shape=jax.ShapeDtypeStruct((count * pairs, lanes), jnp.bfloat16),
        scratch_shapes=[
            pltpu.VMEM((pairs, 4, count, offsets), jnp.bfloat16),
            pltpu.VMEM((pairs, offsets, lanes), jnp.bfloat16),
            pltpu.VMEM((pairs, offsets, lanes), jnp.bfloat16),
            pltpu.VMEM((pairs, count, lanes), jnp.bfloat16),
        ],
        compiler_params=pltpu.CompilerParams(vmem_limit_bytes=24 * MIB),
    )(down, state, data)


def deal_half(held, me, first, out_refs):
    half = len(out_refs)
    each = held.shape[1] // half
    for s, out_ref in enumerate(out_refs):
        deal(held, remainder(me ^ (first + s), half) * each, out_ref)


def far_kernel(gathers, half, place_ref, state_ref, data_ref, plain, turned, sign_ref, *refs):
    *out_refs, turns, held = refs
    me = place_ref[1]
    prepare(gathers, place_ref[0], data_ref, plain, turned)
    sign_ref[...] = plain[0, :TILE]
    other = (1 - quotient(me, half)) * held.shape[1]
    sum_offsets(gathers, other, state_ref, plain, turned, turns, held)
    deal_half(held, me, half, out_refs)


def near_kernel(gathers, half, place_ref, state_ref, plain, turned, _, *refs):
    *out_refs, turns, held = refs
    me = place_ref[1]
    own = quotient(me, half) * held.shape[1]
    sum_offsets(gathers, own, state_ref, plain, turned, turns, held)
    deal_half(held, me, 0, out_refs)


def radon_swapped(place, state, data, gathers, offset_devices):
    _, count, offsets = state.shape
    pairs, lanes = data.shape[2:]
    half = offset_devices // 2
    vmem = pl.BlockSpec(memory_space=pltpu.VMEM)
    smem = pl.BlockSpec(memory_space=pltpu.SMEM)
    block = jax.ShapeDtypeStruct((count // offset_devices * pairs, lanes), jnp.bfloat16)
    spectra = jax.ShapeDtypeStruct((pairs, offsets, lanes), jnp.bfloat16)
    scratch = [
        pltpu.VMEM((pairs, 4, count // 2, offsets), jnp.bfloat16),
        pltpu.VMEM((pairs, count // 2, lanes), jnp.bfloat16),
    ]
    cost = pl.CostEstimate(
        flops=8 * count * offsets * pairs * lanes,
        bytes_accessed=8 * count * offsets,
        transcendentals=0,
    )
    sign = jax.ShapeDtypeStruct((TILE, lanes), jnp.bfloat16)
    plain, turned, sign, *far = pl.pallas_call(
        functools.partial(far_kernel, gathers, half),
        in_specs=[smem, vmem, vmem],
        out_specs=[vmem] * (3 + half),
        out_shape=[spectra, spectra, sign] + [block] * half,
        scratch_shapes=scratch,
        compiler_params=pltpu.CompilerParams(vmem_limit_bytes=20 * MIB),
        cost_estimate=cost,
    )(place, state, data)
    def swapped(part, s):
        swaps = [(o, o ^ s) for o in range(offset_devices)]
        return lax.ppermute(part, "offset", swaps)

    far = [swapped(part, half + s) for s, part in enumerate(far)]
    sign = swapped(sign, 1)
    near = pl.pallas_call(
        functools.partial(near_kernel, gathers, half),
        in_specs=[smem, vmem, vmem, vmem, vmem],
        out_specs=[vmem] * half,
        out_shape=[block] * half,
        scratch_shapes=scratch,
        compiler_params=pltpu.CompilerParams(vmem_limit_bytes=20 * MIB),
        cost_estimate=cost,
    )(place, state, plain, turned, sign)
    near = [swapped(part, s) if s else part for s, part in enumerate(near)]
    return list(range(half, offset_devices)) + list(range(half)), far + near


def join_kernel(scale, order, place_ref, *refs):
    *parts, out_ref, wide, ready, sems = refs
    groups, step, half_lanes, _ = ready.shape
    rows = wide.shape[1]
    pairs = rows // len(parts)
    copies = []
    for g in range(groups):
        for s, part in zip(order, parts):
            own = pl.ds(pl.multiple_of((place_ref[1] ^ s) * pairs, pairs), pairs)
            for i in range(step):
                p = g * step + i
                wide[p, own] = part[p * pairs : (p + 1) * pairs].astype(jnp.float32) * scale
        for i in range(step):
            block = wide[g * step + i].T
            ready[g, i, :, :rows] = block[:half_lanes]
            ready[g, i, :, rows:] = block[half_lanes:]
        copies.append(
            pltpu.make_async_copy(ready.at[g], out_ref.at[pl.ds(g * step, step)], sems.at[g])
        )
        copies[-1].start()
    for copy in copies:
        copy.wait()


def join(place, order, parts, slows, scale):
    pairs = parts[0].shape[0] // slows
    lanes = parts[0].shape[1]
    rows = len(parts) * pairs
    step = 4
    vmem = pl.BlockSpec(memory_space=pltpu.VMEM)
    return pl.pallas_call(
        functools.partial(join_kernel, scale, order),
        in_specs=[pl.BlockSpec(memory_space=pltpu.SMEM)] + [vmem] * len(parts),
        out_specs=pl.BlockSpec(memory_space=pl.ANY),
        out_shape=jax.ShapeDtypeStruct((slows, lanes // 2, 2 * rows), jnp.float32),
        scratch_shapes=[
            pltpu.VMEM((slows, rows, lanes), jnp.float32),
            pltpu.VMEM((slows // step, step, lanes // 2, 2 * rows), jnp.float32),
            pltpu.SemaphoreType.DMA((slows // step,)),
        ],
        compiler_params=pltpu.CompilerParams(vmem_limit_bytes=16 * MIB),
    )(place, *parts)


def finish_kernel(scale, in_ref, out_ref):
    devices, slows, pairs, lanes = in_ref.shape
    rows = devices * pairs
    for p in range(slows):
        block = in_ref[:, p].reshape(rows, lanes).astype(jnp.float32) * scale
        turned = block.T
        out_ref[p, :, :rows] = turned[: lanes // 2]
        out_ref[p, :, rows:] = turned[lanes // 2 :]


def finish(parts, scale):
    devices, slows, pairs, lanes = parts.shape
    rows = devices * pairs
    step = 8
    return pl.pallas_call(
        functools.partial(finish_kernel, scale),
        grid=(slows // step,),
        in_specs=[pl.BlockSpec((devices, step, pairs, lanes), lambda i: (0, i, 0, 0))],
        out_specs=pl.BlockSpec((step, lanes // 2, 2 * rows), lambda i: (i, 0, 0)),
        out_shape=jax.ShapeDtypeStruct((slows, lanes // 2, 2 * rows), jnp.float32),
        compiler_params=pltpu.CompilerParams(vmem_limit_bytes=32 * MIB),
    )(parts)


def local(raw_traces, trace_slot, offset_index, slowness_index):
    gathers, local_offsets = trace_slot.shape
    local_times = raw_traces.shape[1]
    freq_devices = lax.axis_size("freq")
    offset_devices = lax.axis_size("offset")
    devices = freq_devices * offset_devices
    total_time = local_times * freq_devices
    offsets = local_offsets * offset_devices
    band = NF // freq_devices
    own_freqs = NF // devices
    halves = 2
    pairs = own_freqs // halves
    own_offsets = local_offsets // freq_devices

    me = lax.axis_index("freq").astype(jnp.int32).reshape(1)
    series = list(pick(me, trace_slot.astype(jnp.float32), raw_traces, freq_devices))
    for s in list(range(2, freq_devices)) + [1]:
        swaps = [(f, f ^ s) for f in range(freq_devices)]
        series[s] = lax.ppermute(series[s], "freq", swaps)
    table = jnp.asarray(table_rows(total_time, freq_devices, offset_devices, halves, pairs))
    spectrum = transform(me, table, series, pairs, gathers)
    data = lax.all_to_all(spectrum, ("freq", "offset"), 0, 0, tiled=True)

    offs = offset_index.reshape(offset_devices, freq_devices, own_offsets)
    offs = offs.transpose(1, 0, 2).reshape(1, offsets).astype(jnp.float32)
    slows = slowness_index.astype(jnp.float32)[:, None]
    first = lax.axis_index("freq") * band + lax.axis_index("offset") * pairs
    base = (2 * first + 1).astype(jnp.float32) * (math.pi / total_time)
    state = moveout(base.reshape(1), slows, offs, band // halves, total_time)
    down = (2 * lax.axis_index("freq") // freq_devices).astype(jnp.int32)
    place = jnp.stack([down, lax.axis_index("offset").astype(jnp.int32)])
    slows_each = NP // offset_devices
    scale = 1.0 / math.sqrt(offsets)
    if slows_each % TILE == 0:
        order, blocks = radon_swapped(place, state, data, gathers, offset_devices)
        result = join(place, order, blocks, slows_each, scale)
    else:
        panel = radon(place, state, data, gathers)
        panel = panel.reshape(offset_devices, slows_each, pairs, 2 * halves * gathers)
        result = finish(lax.all_to_all(panel, "offset", 0, 0, tiled=True), scale)
    return jnp.transpose(result, (0, 2, 1))


def solution(mesh):
    placed = (P("offset", "freq"), P(None, "offset"), P(), P())
    return jax.shard_map(
        local, mesh=mesh, in_specs=placed, out_specs=P("offset", "freq", None), check_vma=False
    )
```

```python
import functools
import math

import jax
import jax.numpy as jnp
import ml_dtypes
import numpy as np
from jax import lax
from jax.experimental import pallas as pl
from jax.experimental.pallas import tpu as pltpu
from jax.sharding import PartitionSpec as P

NF = 1024
NP = 256
APEX_TIME = 100.0
CURVATURE = 0.0003
MIB = 1 << 20


def table_rows(total_time, freq_devices, offset_devices, halves, pairs):
    band = NF // freq_devices
    f, o, a, k = np.meshgrid(
        np.arange(freq_devices // 2),
        np.arange(offset_devices),
        np.arange(halves),
        np.arange(pairs),
        indexing="ij",
    )
    freq_ids = (f * band + a * (band // halves) + o * pairs + k).reshape(-1, pairs)
    times = np.concatenate([np.arange(0, total_time, 2), np.arange(1, total_time, 2)])
    turns = (2 * freq_ids[..., None] + 1) * times % (2 * total_time)
    angles = turns.astype(np.float32) * np.float32(math.pi / total_time)
    both = np.stack([np.cos(angles), -np.sin(angles)], axis=1).reshape(-1, total_time)
    return (both / np.float32(math.sqrt(total_time))).astype(ml_dtypes.bfloat16)


def pick_kernel(me_ref, slot_ref, raw_ref, *out_refs):
    gathers, local_offsets = slot_ref.shape
    own_offsets = local_offsets // len(out_refs)
    times = raw_ref.shape[1]
    half = times // 2
    row = lax.broadcasted_iota(jnp.int32, (times, times), 0)
    column = lax.broadcasted_iota(jnp.int32, (times, times), 1)
    source = jnp.where(column < half, 2 * column, 2 * (column - half) + 1)
    split = jnp.where(row == source, 1.0, 0.0).astype(jnp.bfloat16)
    raw = jnp.dot(raw_ref[...], split, preferred_element_type=jnp.float32).astype(jnp.bfloat16)
    lane = lax.broadcasted_iota(jnp.int32, (gathers, raw_ref.shape[0]), 1)
    slot = slot_ref[...]
    place = lax.broadcasted_iota(jnp.int32, slot.shape, 1)
    for s, out_ref in enumerate(out_refs):
        first = (me_ref[0] ^ s) * own_offsets
        picks = []
        for h in range(own_offsets):
            wanted = jnp.sum(jnp.where(place == first + h, slot, 0.0), axis=1, keepdims=True)
            picks.append(
                jnp.where(lane == wanted.astype(jnp.int32), 1.0, 0.0).astype(jnp.bfloat16)
            )
        out_ref[...] = jnp.dot(
            jnp.concatenate(picks, axis=0), raw, preferred_element_type=jnp.float32
        ).astype(out_ref.dtype)


def pick(me, trace_slot, raw_traces, groups):
    gathers, local_offsets = trace_slot.shape
    rows = gathers * local_offsets // groups
    vmem = pl.BlockSpec(memory_space=pltpu.VMEM)
    block = jax.ShapeDtypeStruct((rows, raw_traces.shape[1]), raw_traces.dtype)
    return pl.pallas_call(
        pick_kernel,
        in_specs=[pl.BlockSpec(memory_space=pltpu.SMEM), vmem, vmem],
        out_specs=[vmem] * groups,
        out_shape=[block] * groups,
        compiler_params=pltpu.CompilerParams(vmem_limit_bytes=24 * MIB),
    )(me, trace_slot, raw_traces)


def regroup(parts, gathers):
    lanes = 4 * gathers
    lane = lax.broadcasted_iota(jnp.int32, (1, lanes), 1)
    low_half = lane < 2 * gathers
    low_part = lane % (2 * gathers) < gathers
    found = []
    for q in range(parts[0].shape[1] // lanes):
        x = [part[:, q * lanes : (q + 1) * lanes] for part in parts]
        for top in range(2):
            pair = []
            for part in range(2):
                a, b = x[part], x[2 + part]
                if top == 0:
                    pair.append(jnp.where(low_half, a, pltpu.roll(b, 2 * gathers, 1)))
                else:
                    pair.append(jnp.where(low_half, pltpu.roll(a, 2 * gathers, 1), b))
            found.append(jnp.where(low_part, pair[0], pltpu.roll(pair[1], gathers, 1)))
            found.append(jnp.where(low_part, pltpu.roll(pair[0], lanes - gathers, 1), pair[1]))
    return found


def time_sums(me, first, table_ref, series_refs, even, odd, own):
    half = even.shape[1] // 2
    depth = table_ref.shape[1] // 2
    evens = odds = None
    for r in range(len(series_refs) // 2):
        start = (quotient(me, 2) ^ (first + r)) * 2 * half
        even_part = jnp.dot(
            table_ref[own, pl.ds(pl.multiple_of(start, 2 * half), 2 * half)],
            even[r],
            preferred_element_type=jnp.float32,
        )
        odd_part = jnp.dot(
            table_ref[own, pl.ds(pl.multiple_of(depth + start, 2 * half), 2 * half)],
            odd[r],
            preferred_element_type=jnp.float32,
        )
        evens = even_part if evens is None else evens + even_part
        odds = odd_part if odds is None else odds + odd_part
    return evens, odds


def turn_series(me, series_refs, even, odd):
    half = even.shape[1] // 2
    for s, series_ref in enumerate(series_refs):
        turned = series_ref[...].T
        place = pl.ds(pl.multiple_of(((me ^ s) & 1) * half, half), half)
        even[s // 2, place] = turned[:half]
        odd[s // 2, place] = turned[half:]


def begin_kernel(chunks, me_ref, table_ref, *refs):
    *series_refs, out_ref, even, odd = refs
    me = me_ref[0]
    turn_series(me, series_refs, even, odd)
    step = table_ref.shape[0] // chunks
    for i in range(chunks):
        own = slice(i * step, (i + 1) * step)
        out_ref[0, own], out_ref[1, own] = time_sums(
            me, 0, table_ref, series_refs, even, odd, own
        )


def transform_kernel(pairs, gathers, chunks, me_ref, table_ref, begun_ref, *refs):
    *series_refs, out_ref, even, odd = refs
    me = me_ref[0]
    turn_series(me, series_refs, even, odd)
    step = table_ref.shape[0] // chunks
    for i in range(chunks):
        own = slice(i * step, (i + 1) * step)
        evens, odds = time_sums(me, 1, table_ref, series_refs, even, odd, own)
        evens = evens + begun_ref[0, own]
        odds = odds + begun_ref[1, own]
        low = evens + odds
        high = evens - odds
        if len(out_ref.shape) == 3:
            row = lax.broadcasted_iota(jnp.int32, (step, 1), 0)
            out_ref[0, own] = low.astype(out_ref.dtype)
            out_ref[1, own] = jnp.where(row // pairs % 2 == 0, high, -high).astype(out_ref.dtype)
            continue
        targets = step // (4 * pairs)
        devices = out_ref.shape[0]
        for d in range(targets):
            cuts = [slice((4 * d + c) * pairs, (4 * d + c + 1) * pairs) for c in range(4)]
            place = i * targets + d
            for h, value in enumerate(regroup([low[cut] for cut in cuts], gathers)):
                out_ref[place, h] = value.astype(out_ref.dtype)
            mirrored = [high[cuts[2]], -high[cuts[3]], high[cuts[0]], -high[cuts[1]]]
            for h, value in enumerate(regroup(mirrored, gathers)):
                out_ref[devices - 1 - place, h] = value.astype(out_ref.dtype)


def transform(me, table, series, pairs, gathers):
    columns, total_time = table.shape
    rows, local_times = series[0].shape
    own_offsets = rows // gathers
    devices = columns // (2 * pairs)
    final = (devices, own_offsets, pairs, 4 * gathers)
    chunks = 4
    aligned = rows % (4 * gathers) == 0 and pairs % 8 == 0 and devices % (2 * chunks) == 0
    vmem = pl.BlockSpec(memory_space=pltpu.VMEM)
    smem = pl.BlockSpec(memory_space=pltpu.SMEM)
    early, late = series[:2], series[2:]

    def scratch(blocks):
        return [pltpu.VMEM((len(blocks) // 2, local_times, rows), jnp.bfloat16)] * 2

    params = pltpu.CompilerParams(vmem_limit_bytes=24 * MIB)
    begun = pl.pallas_call(
        functools.partial(begin_kernel, chunks),
        in_specs=[smem] + [vmem] * (1 + len(early)),
        out_specs=vmem,
        out_shape=jax.ShapeDtypeStruct((2, columns, rows), jnp.float32),
        scratch_shapes=scratch(early),
        compiler_params=params,
        cost_estimate=pl.CostEstimate(
            flops=columns * total_time * rows,
            bytes_accessed=2 * columns * total_time,
            transcendentals=0,
        ),
    )(me, table, *early)
    out = pl.pallas_call(
        functools.partial(transform_kernel, pairs, gathers, chunks),
        in_specs=[smem] + [vmem] * (2 + len(late)),
        out_specs=vmem,
        out_shape=jax.ShapeDtypeStruct(final if aligned else (2, columns, rows), jnp.bfloat16),
        scratch_shapes=scratch(late),
        compiler_params=params,
    )(me, table, begun, *late)
    if aligned:
        return out
    out = out.reshape(2, devices // 2, 2, 2, pairs, own_offsets, gathers)
    out = jnp.concatenate([out[0], jnp.flip(out[1], (0, 1))], axis=0)
    return out.transpose(0, 4, 3, 1, 2, 5).reshape(final)


def moveout_kernel(shift, total_time, base_ref, slow_ref, offs_ref, out_ref):
    spread = CURVATURE * slow_ref[...] * offs_ref[...]
    delay = jnp.sqrt(APEX_TIME * APEX_TIME + spread * spread) - APEX_TIME
    phase = base_ref[0] * delay
    c = jnp.cos(phase)
    s = jnp.sin(phase)
    far = delay * (2.0 * shift * math.pi / total_time)
    far_c = jnp.cos(far)
    far_s = jnp.sin(far)
    turn = delay * (2.0 * math.pi / total_time)
    out_ref[0] = c
    out_ref[1] = c * far_c - s * far_s
    out_ref[2] = s
    out_ref[3] = s * far_c + c * far_s
    out_ref[4] = jnp.cos(turn)
    out_ref[5] = jnp.sin(turn)


def moveout(base, slows, offs, shift, total_time):
    count = slows.shape[0]
    offsets = offs.shape[1]
    rows = min(count, 64)
    return pl.pallas_call(
        functools.partial(moveout_kernel, shift, total_time),
        grid=(count // rows,),
        in_specs=[
            pl.BlockSpec(memory_space=pltpu.SMEM),
            pl.BlockSpec((rows, 1), lambda i: (i, 0)),
            pl.BlockSpec((1, offsets), lambda i: (0, 0)),
        ],
        out_specs=pl.BlockSpec((6, rows, offsets), lambda i: (0, i, 0)),
        out_shape=jax.ShapeDtypeStruct((6, count, offsets), jnp.float32),
        compiler_params=pltpu.CompilerParams(vmem_limit_bytes=24 * MIB),
        cost_estimate=pl.CostEstimate(
            flops=300 * count * offsets,
            bytes_accessed=24 * count * offsets,
            transcendentals=6 * count * offsets,
        ),
    )(base, slows, offs)


def quotient(value, divisor):
    if divisor & (divisor - 1):
        return value // divisor
    return lax.shift_right_logical(value, jnp.int32(divisor.bit_length() - 1))


def remainder(value, divisor):
    if divisor & (divisor - 1):
        return value % divisor
    return value & (divisor - 1)


def one_hot(rows, columns, source):
    row = lax.broadcasted_iota(jnp.int32, (rows, 1), 0)
    column = lax.broadcasted_iota(jnp.int32, (rows, columns), 1)
    return jnp.where(column == source(row), 1.0, 0.0).astype(jnp.bfloat16)


TILE = 16


def prepare(gathers, down, data_ref, plain, turned):
    devices, own_offsets, pairs, lanes = data_ref.shape
    size = TILE * pairs
    together = TILE // own_offsets

    def received(r):
        k = quotient(r, TILE)
        return remainder(r, TILE) * pairs + k + down * (pairs - 1 - 2 * k)

    swap = one_hot(size, size, received)
    for d in range(devices // together):
        block = data_ref[d * together : (d + 1) * together].reshape(size, lanes)
        if pairs > 1:
            block = jnp.dot(swap, block, preferred_element_type=jnp.float32).astype(jnp.bfloat16)
        plain[:, d * TILE : (d + 1) * TILE] = block.reshape(pairs, TILE, lanes)
    row = lax.broadcasted_iota(jnp.int32, (lanes, lanes), 0)
    column = lax.broadcasted_iota(jnp.int32, (lanes, lanes), 1)
    quarter = jnp.where(
        remainder(column, 2 * gathers) < gathers,
        jnp.where(row == column + gathers, -1.0, 0.0),
        jnp.where(row == column - gathers, 1.0, 0.0),
    ).astype(jnp.bfloat16)
    for k in range(pairs):
        turned[k] = jnp.dot(plain[k], quarter, preferred_element_type=jnp.float32).astype(
            jnp.bfloat16
        )


def sum_offsets(gathers, first, state_ref, plain, turned, turns, held):
    pairs, slows, lanes = held.shape
    offsets = plain.shape[1]

    def fill(t, carry):
        source = pl.ds(pl.multiple_of(first + t * TILE, TILE), TILE)
        own = pl.ds(pl.multiple_of(t * TILE, TILE), TILE)
        step_c = state_ref[4, source]
        step_s = state_ref[5, source]
        twice = 2.0 * step_c
        now = [state_ref[i, source] for i in range(4)]
        past = [now[a] * step_c + now[2 + a] * step_s for a in range(2)]
        past += [now[2 + a] * step_c - now[a] * step_s for a in range(2)]
        for k in range(pairs):
            for i in range(4):
                turns[k, i, own] = now[i].astype(jnp.bfloat16)
                now[i], past[i] = twice * now[i] - past[i], now[i]
        return carry

    lax.fori_loop(0, slows // TILE, fill, 0)
    first_half = lax.broadcasted_iota(jnp.int32, (1, lanes), 1) < 2 * gathers
    for k in range(pairs):
        cosine = turns[k, :2].reshape(2 * slows, offsets)
        sines = turns[k, 2:].reshape(2 * slows, offsets)
        both = jnp.dot(cosine, plain[k], preferred_element_type=jnp.float32) + jnp.dot(
            sines, turned[k], preferred_element_type=jnp.float32
        )
        held[k] = jnp.where(first_half, both[:slows], both[slows:]).astype(jnp.bfloat16)


def deal(held, first, out_ref):
    pairs, _, lanes = held.shape
    size = TILE * pairs
    swap = one_hot(size, size, lambda r: remainder(r, pairs) * TILE + quotient(r, pairs))
    for p in range(out_ref.shape[0] // size):
        start = first + p * TILE
        if not isinstance(start, int):
            start = pl.multiple_of(start, TILE)
        block = held[:, pl.ds(start, TILE)].reshape(size, lanes)
        if pairs > 1:
            block = jnp.dot(swap, block, preferred_element_type=jnp.float32)
        out_ref[p * size : (p + 1) * size] = block.astype(out_ref.dtype)


def radon_kernel(gathers, down_ref, state_ref, data_ref, out_ref, turns, plain, turned, held):
    prepare(gathers, down_ref[0], data_ref, plain, turned)
    sum_offsets(gathers, 0, state_ref, plain, turned, turns, held)
    deal(held, 0, out_ref)


def radon(down, state, data, gathers):
    _, count, offsets = state.shape
    pairs, lanes = data.shape[2:]
    vmem = pl.BlockSpec(memory_space=pltpu.VMEM)
    return pl.pallas_call(
        functools.partial(radon_kernel, gathers),
        in_specs=[pl.BlockSpec(memory_space=pltpu.SMEM), vmem, vmem],
        out_specs=vmem,
        out_shape=jax.ShapeDtypeStruct((count * pairs, lanes), jnp.bfloat16),
        scratch_shapes=[
            pltpu.VMEM((pairs, 4, count, offsets), jnp.bfloat16),
            pltpu.VMEM((pairs, offsets, lanes), jnp.bfloat16),
            pltpu.VMEM((pairs, offsets, lanes), jnp.bfloat16),
            pltpu.VMEM((pairs, count, lanes), jnp.bfloat16),
        ],
        compiler_params=pltpu.CompilerParams(vmem_limit_bytes=24 * MIB),
    )(down, state, data)


def deal_half(held, me, first, out_refs):
    half = len(out_refs)
    each = held.shape[1] // half
    for s, out_ref in enumerate(out_refs):
        deal(held, remainder(me ^ (first + s), half) * each, out_ref)


def far_kernel(gathers, half, place_ref, state_ref, data_ref, plain, turned, sign_ref, *refs):
    *out_refs, turns, held = refs
    me = place_ref[1]
    prepare(gathers, place_ref[0], data_ref, plain, turned)
    sign_ref[...] = plain[0, :TILE]
    other = (1 - quotient(me, half)) * held.shape[1]
    sum_offsets(gathers, other, state_ref, plain, turned, turns, held)
    deal_half(held, me, half, out_refs)


def near_kernel(gathers, half, place_ref, state_ref, plain, turned, _, *refs):
    *out_refs, turns, held = refs
    me = place_ref[1]
    own = quotient(me, half) * held.shape[1]
    sum_offsets(gathers, own, state_ref, plain, turned, turns, held)
    deal_half(held, me, 0, out_refs)


def radon_swapped(place, state, data, gathers, offset_devices):
    _, count, offsets = state.shape
    pairs, lanes = data.shape[2:]
    half = offset_devices // 2
    vmem = pl.BlockSpec(memory_space=pltpu.VMEM)
    smem = pl.BlockSpec(memory_space=pltpu.SMEM)
    block = jax.ShapeDtypeStruct((count // offset_devices * pairs, lanes), jnp.bfloat16)
    spectra = jax.ShapeDtypeStruct((pairs, offsets, lanes), jnp.bfloat16)
    scratch = [
        pltpu.VMEM((pairs, 4, count // 2, offsets), jnp.bfloat16),
        pltpu.VMEM((pairs, count // 2, lanes), jnp.bfloat16),
    ]
    cost = pl.CostEstimate(
        flops=8 * count * offsets * pairs * lanes,
        bytes_accessed=8 * count * offsets,
        transcendentals=0,
    )
    sign = jax.ShapeDtypeStruct((TILE, lanes), jnp.bfloat16)
    plain, turned, sign, *far = pl.pallas_call(
        functools.partial(far_kernel, gathers, half),
        in_specs=[smem, vmem, vmem],
        out_specs=[vmem] * (3 + half),
        out_shape=[spectra, spectra, sign] + [block] * half,
        scratch_shapes=scratch,
        compiler_params=pltpu.CompilerParams(vmem_limit_bytes=20 * MIB),
        cost_estimate=cost,
    )(place, state, data)
    def swapped(part, s):
        swaps = [(o, o ^ s) for o in range(offset_devices)]
        return lax.ppermute(part, "offset", swaps)

    far[:-1] = [swapped(part, half + s) for s, part in enumerate(far[:-1])]
    sign = swapped(sign, 1)
    near = pl.pallas_call(
        functools.partial(near_kernel, gathers, half),
        in_specs=[smem, vmem, vmem, vmem, vmem],
        out_specs=[vmem] * half,
        out_shape=[block] * half,
        scratch_shapes=scratch,
        compiler_params=pltpu.CompilerParams(vmem_limit_bytes=20 * MIB),
        cost_estimate=cost,
    )(place, state, plain, turned, sign)
    near = list(near)
    last, far[0] = lax.optimization_barrier((far[-1], far[0]))
    near = [swapped(part, s) if s else part for s, part in enumerate(near)]
    far[-1] = swapped(last, offset_devices - 1)
    parts = near + far
    return list(range(half, offset_devices - 1)) + list(range(half))[::-1] + [offset_devices - 1], [parts[s] for s in list(range(half, offset_devices - 1)) + list(range(half))[::-1] + [offset_devices - 1]]


def join_kernel(scale, order, place_ref, *refs):
    *parts, out_ref, wide, ready, sems = refs
    groups, step, half_lanes, _ = ready.shape
    rows = wide.shape[1]
    pairs = rows // len(parts)
    copies = []
    for g in range(groups):
        for s, part in zip(order, parts):
            own = pl.ds(pl.multiple_of((place_ref[1] ^ s) * pairs, pairs), pairs)
            for i in range(step):
                p = g * step + i
                wide[p, own] = part[p * pairs : (p + 1) * pairs].astype(jnp.float32) * scale
        for i in range(step):
            block = wide[g * step + i].T
            ready[g, i, :, :rows] = block[:half_lanes]
            ready[g, i, :, rows:] = block[half_lanes:]
        copies.append(
            pltpu.make_async_copy(ready.at[g], out_ref.at[pl.ds(g * step, step)], sems.at[g])
        )
        copies[-1].start()
    for copy in copies:
        copy.wait()


def join(place, order, parts, slows, scale):
    pairs = parts[0].shape[0] // slows
    lanes = parts[0].shape[1]
    rows = len(parts) * pairs
    step = 4
    vmem = pl.BlockSpec(memory_space=pltpu.VMEM)
    return pl.pallas_call(
        functools.partial(join_kernel, scale, order),
        in_specs=[pl.BlockSpec(memory_space=pltpu.SMEM)] + [vmem] * len(parts),
        out_specs=pl.BlockSpec(memory_space=pl.ANY),
        out_shape=jax.ShapeDtypeStruct((slows, lanes // 2, 2 * rows), jnp.float32),
        scratch_shapes=[
            pltpu.VMEM((slows, rows, lanes), jnp.float32),
            pltpu.VMEM((slows // step, step, lanes // 2, 2 * rows), jnp.float32),
            pltpu.SemaphoreType.DMA((slows // step,)),
        ],
        compiler_params=pltpu.CompilerParams(vmem_limit_bytes=16 * MIB),
    )(place, *parts)


def finish_kernel(scale, in_ref, out_ref):
    devices, slows, pairs, lanes = in_ref.shape
    rows = devices * pairs
    for p in range(slows):
        block = in_ref[:, p].reshape(rows, lanes).astype(jnp.float32) * scale
        turned = block.T
        out_ref[p, :, :rows] = turned[: lanes // 2]
        out_ref[p, :, rows:] = turned[lanes // 2 :]


def finish(parts, scale):
    devices, slows, pairs, lanes = parts.shape
    rows = devices * pairs
    step = 8
    return pl.pallas_call(
        functools.partial(finish_kernel, scale),
        grid=(slows // step,),
        in_specs=[pl.BlockSpec((devices, step, pairs, lanes), lambda i: (0, i, 0, 0))],
        out_specs=pl.BlockSpec((step, lanes // 2, 2 * rows), lambda i: (i, 0, 0)),
        out_shape=jax.ShapeDtypeStruct((slows, lanes // 2, 2 * rows), jnp.float32),
        compiler_params=pltpu.CompilerParams(vmem_limit_bytes=32 * MIB),
    )(parts)


def local(raw_traces, trace_slot, offset_index, slowness_index):
    gathers, local_offsets = trace_slot.shape
    local_times = raw_traces.shape[1]
    freq_devices = lax.axis_size("freq")
    offset_devices = lax.axis_size("offset")
    devices = freq_devices * offset_devices
    total_time = local_times * freq_devices
    offsets = local_offsets * offset_devices
    band = NF // freq_devices
    own_freqs = NF // devices
    halves = 2
    pairs = own_freqs // halves
    own_offsets = local_offsets // freq_devices

    me = lax.axis_index("freq").astype(jnp.int32).reshape(1)
    series = list(pick(me, trace_slot.astype(jnp.float32), raw_traces, freq_devices))
    for s in list(range(2, freq_devices)) + [1]:
        swaps = [(f, f ^ s) for f in range(freq_devices)]
        series[s] = lax.ppermute(series[s], "freq", swaps)
    table = jnp.asarray(table_rows(total_time, freq_devices, offset_devices, halves, pairs))
    spectrum = transform(me, table, series, pairs, gathers)
    data = lax.all_to_all(spectrum, ("freq", "offset"), 0, 0, tiled=True)

    offs = offset_index.reshape(offset_devices, freq_devices, own_offsets)
    offs = offs.transpose(1, 0, 2).reshape(1, offsets).astype(jnp.float32)
    slows = slowness_index.astype(jnp.float32)[:, None]
    first = lax.axis_index("freq") * band + lax.axis_index("offset") * pairs
    base = (2 * first + 1).astype(jnp.float32) * (math.pi / total_time)
    state = moveout(base.reshape(1), slows, offs, band // halves, total_time)
    down = (2 * lax.axis_index("freq") // freq_devices).astype(jnp.int32)
    place = jnp.stack([down, lax.axis_index("offset").astype(jnp.int32)])
    slows_each = NP // offset_devices
    scale = 1.0 / math.sqrt(offsets)
    if slows_each % TILE == 0:
        order, blocks = radon_swapped(place, state, data, gathers, offset_devices)
        result = join(place, order, blocks, slows_each, scale)
    else:
        panel = radon(place, state, data, gathers)
        panel = panel.reshape(offset_devices, slows_each, pairs, 2 * halves * gathers)
        result = finish(lax.all_to_all(panel, "offset", 0, 0, tiled=True), scale)
    return jnp.transpose(result, (0, 2, 1))


def solution(mesh):
    placed = (P("offset", "freq"), P(None, "offset"), P(), P())
    return jax.shard_map(
        local, mesh=mesh, in_specs=placed, out_specs=P("offset", "freq", None), check_vma=False
    )
```

```python
import functools
import math

import jax
import jax.numpy as jnp
import ml_dtypes
import numpy as np
from jax import lax
from jax.experimental import pallas as pl
from jax.experimental.pallas import tpu as pltpu
from jax.sharding import PartitionSpec as P

NF = 1024
NP = 256
APEX_TIME = 100.0
CURVATURE = 0.0003
MIB = 1 << 20


def table_rows(total_time, freq_devices, offset_devices, halves, pairs):
    band = NF // freq_devices
    o, f, a, k = np.meshgrid(
        np.arange(offset_devices // 2),
        np.arange(freq_devices),
        np.arange(halves),
        np.arange(pairs),
        indexing="ij",
    )
    freq_ids = (f * band + a * (band // halves) + o * pairs + k).reshape(-1, pairs)
    times = np.concatenate([np.arange(0, total_time, 2), np.arange(1, total_time, 2)])
    turns = (2 * freq_ids[..., None] + 1) * times % (2 * total_time)
    angles = turns.astype(np.float32) * np.float32(math.pi / total_time)
    both = np.stack([np.cos(angles), -np.sin(angles)], axis=1).reshape(-1, total_time)
    return (both / np.float32(math.sqrt(total_time))).astype(ml_dtypes.bfloat16)


def pick_kernel(me_ref, slot_ref, raw_ref, *out_refs):
    gathers, local_offsets = slot_ref.shape
    own_offsets = local_offsets // len(out_refs)
    times = raw_ref.shape[1]
    half = times // 2
    row = lax.broadcasted_iota(jnp.int32, (times, times), 0)
    column = lax.broadcasted_iota(jnp.int32, (times, times), 1)
    source = jnp.where(column < half, 2 * column, 2 * (column - half) + 1)
    split = jnp.where(row == source, 1.0, 0.0).astype(jnp.bfloat16)
    raw = jnp.dot(raw_ref[...], split, preferred_element_type=jnp.float32).astype(jnp.bfloat16)
    lane = lax.broadcasted_iota(jnp.int32, (gathers, raw_ref.shape[0]), 1)
    slot = slot_ref[...]
    place = lax.broadcasted_iota(jnp.int32, slot.shape, 1)
    for s, out_ref in enumerate(out_refs):
        first = (me_ref[0] ^ s) * own_offsets
        picks = []
        for h in range(own_offsets):
            wanted = jnp.sum(jnp.where(place == first + h, slot, 0.0), axis=1, keepdims=True)
            picks.append(
                jnp.where(lane == wanted.astype(jnp.int32), 1.0, 0.0).astype(jnp.bfloat16)
            )
        out_ref[...] = jnp.dot(
            jnp.concatenate(picks, axis=0), raw, preferred_element_type=jnp.float32
        ).astype(out_ref.dtype)


def pick(me, trace_slot, raw_traces, groups):
    gathers, local_offsets = trace_slot.shape
    rows = gathers * local_offsets // groups
    vmem = pl.BlockSpec(memory_space=pltpu.VMEM)
    block = jax.ShapeDtypeStruct((rows, raw_traces.shape[1]), raw_traces.dtype)
    return pl.pallas_call(
        pick_kernel,
        in_specs=[pl.BlockSpec(memory_space=pltpu.SMEM), vmem, vmem],
        out_specs=[vmem] * groups,
        out_shape=[block] * groups,
        compiler_params=pltpu.CompilerParams(vmem_limit_bytes=24 * MIB),
    )(me, trace_slot, raw_traces)


def regroup(parts, gathers):
    lanes = 4 * gathers
    lane = lax.broadcasted_iota(jnp.int32, (1, lanes), 1)
    low_half = lane < 2 * gathers
    low_part = lane % (2 * gathers) < gathers
    found = []
    for q in range(parts[0].shape[1] // lanes):
        x = [part[:, q * lanes : (q + 1) * lanes] for part in parts]
        for top in range(2):
            pair = []
            for part in range(2):
                a, b = x[part], x[2 + part]
                if top == 0:
                    pair.append(jnp.where(low_half, a, pltpu.roll(b, 2 * gathers, 1)))
                else:
                    pair.append(jnp.where(low_half, pltpu.roll(a, 2 * gathers, 1), b))
            found.append(jnp.where(low_part, pair[0], pltpu.roll(pair[1], gathers, 1)))
            found.append(jnp.where(low_part, pltpu.roll(pair[0], lanes - gathers, 1), pair[1]))
    return found


def time_sums(me, first, table_ref, series_refs, even, odd, own):
    half = even.shape[1] // 2
    depth = table_ref.shape[1] // 2
    evens = odds = None
    for r in range(len(series_refs) // 2):
        start = (quotient(me, 2) ^ (first + r)) * 2 * half
        even_part = jnp.dot(
            table_ref[own, pl.ds(pl.multiple_of(start, 2 * half), 2 * half)],
            even[r],
            preferred_element_type=jnp.float32,
        )
        odd_part = jnp.dot(
            table_ref[own, pl.ds(pl.multiple_of(depth + start, 2 * half), 2 * half)],
            odd[r],
            preferred_element_type=jnp.float32,
        )
        evens = even_part if evens is None else evens + even_part
        odds = odd_part if odds is None else odds + odd_part
    return evens, odds


def turn_series(me, series_refs, even, odd):
    half = even.shape[1] // 2
    for s, series_ref in enumerate(series_refs):
        turned = series_ref[...].T
        place = pl.ds(pl.multiple_of(((me ^ s) & 1) * half, half), half)
        even[s // 2, place] = turned[:half]
        odd[s // 2, place] = turned[half:]


def begin_kernel(chunks, me_ref, table_ref, *refs):
    *series_refs, out_ref, even, odd = refs
    me = me_ref[0]
    turn_series(me, series_refs, even, odd)
    step = table_ref.shape[0] // chunks
    for i in range(chunks):
        own = slice(i * step, (i + 1) * step)
        out_ref[0, own], out_ref[1, own] = time_sums(
            me, 0, table_ref, series_refs, even, odd, own
        )


def transform_kernel(pairs, gathers, chunks, me_ref, table_ref, begun_ref, *refs):
    *series_refs, out_ref, even, odd = refs
    me = me_ref[0]
    turn_series(me, series_refs, even, odd)
    step = table_ref.shape[0] // chunks
    for i in range(chunks):
        own = slice(i * step, (i + 1) * step)
        evens, odds = time_sums(me, 1, table_ref, series_refs, even, odd, own)
        evens = evens + begun_ref[0, own]
        odds = odds + begun_ref[1, own]
        low = evens + odds
        high = evens - odds
        if len(out_ref.shape) == 3:
            row = lax.broadcasted_iota(jnp.int32, (step, 1), 0)
            out_ref[0, own] = low.astype(out_ref.dtype)
            out_ref[1, own] = jnp.where(row // pairs % 2 == 0, high, -high).astype(out_ref.dtype)
            continue
        targets = step // (4 * pairs)
        devices = out_ref.shape[0]
        for d in range(targets):
            cuts = [slice((4 * d + c) * pairs, (4 * d + c + 1) * pairs) for c in range(4)]
            place = i * targets + d
            for h, value in enumerate(regroup([low[cut] for cut in cuts], gathers)):
                out_ref[place, h] = value.astype(out_ref.dtype)
            mirrored = [high[cuts[2]], -high[cuts[3]], high[cuts[0]], -high[cuts[1]]]
            for h, value in enumerate(regroup(mirrored, gathers)):
                out_ref[devices - 1 - place, h] = value.astype(out_ref.dtype)


def transform(me, table, series, pairs, gathers):
    columns, total_time = table.shape
    rows, local_times = series[0].shape
    own_offsets = rows // gathers
    devices = columns // (2 * pairs)
    final = (devices, own_offsets, pairs, 4 * gathers)
    chunks = 4
    aligned = rows % (4 * gathers) == 0 and pairs % 8 == 0 and devices % (2 * chunks) == 0
    vmem = pl.BlockSpec(memory_space=pltpu.VMEM)
    smem = pl.BlockSpec(memory_space=pltpu.SMEM)
    early, late = series[:2], series[2:]

    def scratch(blocks):
        return [pltpu.VMEM((len(blocks) // 2, local_times, rows), jnp.bfloat16)] * 2

    params = pltpu.CompilerParams(vmem_limit_bytes=24 * MIB)
    begun = pl.pallas_call(
        functools.partial(begin_kernel, chunks),
        in_specs=[smem] + [vmem] * (1 + len(early)),
        out_specs=vmem,
        out_shape=jax.ShapeDtypeStruct((2, columns, rows), jnp.float32),
        scratch_shapes=scratch(early),
        compiler_params=params,
        cost_estimate=pl.CostEstimate(
            flops=columns * total_time * rows,
            bytes_accessed=2 * columns * total_time,
            transcendentals=0,
        ),
    )(me, table, *early)
    out = pl.pallas_call(
        functools.partial(transform_kernel, pairs, gathers, chunks),
        in_specs=[smem] + [vmem] * (2 + len(late)),
        out_specs=vmem,
        out_shape=jax.ShapeDtypeStruct(final if aligned else (2, columns, rows), jnp.bfloat16),
        scratch_shapes=scratch(late),
        compiler_params=params,
    )(me, table, begun, *late)
    if aligned:
        return out
    out = out.reshape(2, devices // 2, 2, 2, pairs, own_offsets, gathers)
    out = jnp.concatenate([out[0], jnp.flip(out[1], (0, 1))], axis=0)
    return out.transpose(0, 4, 3, 1, 2, 5).reshape(final)


def moveout_kernel(shift, total_time, base_ref, slow_ref, offs_ref, out_ref):
    spread = CURVATURE * slow_ref[...] * offs_ref[...]
    delay = jnp.sqrt(APEX_TIME * APEX_TIME + spread * spread) - APEX_TIME
    phase = base_ref[0] * delay
    c = jnp.cos(phase)
    s = jnp.sin(phase)
    far = delay * (2.0 * shift * math.pi / total_time)
    far_c = jnp.cos(far)
    far_s = jnp.sin(far)
    turn = delay * (2.0 * math.pi / total_time)
    out_ref[0] = c
    out_ref[1] = c * far_c - s * far_s
    out_ref[2] = s
    out_ref[3] = s * far_c + c * far_s
    out_ref[4] = jnp.cos(turn)
    out_ref[5] = jnp.sin(turn)


def moveout(base, slows, offs, shift, total_time):
    count = slows.shape[0]
    offsets = offs.shape[1]
    rows = min(count, 64)
    return pl.pallas_call(
        functools.partial(moveout_kernel, shift, total_time),
        grid=(count // rows,),
        in_specs=[
            pl.BlockSpec(memory_space=pltpu.SMEM),
            pl.BlockSpec((rows, 1), lambda i: (i, 0)),
            pl.BlockSpec((1, offsets), lambda i: (0, 0)),
        ],
        out_specs=pl.BlockSpec((6, rows, offsets), lambda i: (0, i, 0)),
        out_shape=jax.ShapeDtypeStruct((6, count, offsets), jnp.float32),
        compiler_params=pltpu.CompilerParams(vmem_limit_bytes=24 * MIB),
        cost_estimate=pl.CostEstimate(
            flops=300 * count * offsets,
            bytes_accessed=24 * count * offsets,
            transcendentals=6 * count * offsets,
        ),
    )(base, slows, offs)


def quotient(value, divisor):
    if divisor & (divisor - 1):
        return value // divisor
    return lax.shift_right_logical(value, jnp.int32(divisor.bit_length() - 1))


def remainder(value, divisor):
    if divisor & (divisor - 1):
        return value % divisor
    return value & (divisor - 1)


def one_hot(rows, columns, source):
    row = lax.broadcasted_iota(jnp.int32, (rows, 1), 0)
    column = lax.broadcasted_iota(jnp.int32, (rows, columns), 1)
    return jnp.where(column == source(row), 1.0, 0.0).astype(jnp.bfloat16)


TILE = 16


def prepare(gathers, down, data_ref, plain, turned):
    devices, own_offsets, pairs, lanes = data_ref.shape
    size = TILE * pairs
    together = TILE // own_offsets

    def received(r):
        k = quotient(r, TILE)
        return remainder(r, TILE) * pairs + k + down * (pairs - 1 - 2 * k)

    swap = one_hot(size, size, received)
    for d in range(devices // together):
        block = data_ref[d * together : (d + 1) * together].reshape(size, lanes)
        if pairs > 1:
            block = jnp.dot(swap, block, preferred_element_type=jnp.float32).astype(jnp.bfloat16)
        plain[:, d * TILE : (d + 1) * TILE] = block.reshape(pairs, TILE, lanes)
    row = lax.broadcasted_iota(jnp.int32, (lanes, lanes), 0)
    column = lax.broadcasted_iota(jnp.int32, (lanes, lanes), 1)
    quarter = jnp.where(
        remainder(column, 2 * gathers) < gathers,
        jnp.where(row == column + gathers, -1.0, 0.0),
        jnp.where(row == column - gathers, 1.0, 0.0),
    ).astype(jnp.bfloat16)
    for k in range(pairs):
        turned[k] = jnp.dot(plain[k], quarter, preferred_element_type=jnp.float32).astype(
            jnp.bfloat16
        )


def sum_offsets(gathers, first, state_ref, plain, turned, turns, held):
    pairs, slows, lanes = held.shape
    offsets = plain.shape[1]

    def fill(t, carry):
        source = pl.ds(pl.multiple_of(first + t * TILE, TILE), TILE)
        own = pl.ds(pl.multiple_of(t * TILE, TILE), TILE)
        step_c = state_ref[4, source]
        step_s = state_ref[5, source]
        twice = 2.0 * step_c
        now = [state_ref[i, source] for i in range(4)]
        past = [now[a] * step_c + now[2 + a] * step_s for a in range(2)]
        past += [now[2 + a] * step_c - now[a] * step_s for a in range(2)]
        for k in range(pairs):
            for i in range(4):
                turns[k, i, own] = now[i].astype(jnp.bfloat16)
                now[i], past[i] = twice * now[i] - past[i], now[i]
        return carry

    lax.fori_loop(0, slows // TILE, fill, 0)
    first_half = lax.broadcasted_iota(jnp.int32, (1, lanes), 1) < 2 * gathers
    for k in range(pairs):
        cosine = turns[k, :2].reshape(2 * slows, offsets)
        sines = turns[k, 2:].reshape(2 * slows, offsets)
        both = jnp.dot(cosine, plain[k], preferred_element_type=jnp.float32) + jnp.dot(
            sines, turned[k], preferred_element_type=jnp.float32
        )
        held[k] = jnp.where(first_half, both[:slows], both[slows:]).astype(jnp.bfloat16)


def deal(held, first, out_ref):
    pairs, _, lanes = held.shape
    size = TILE * pairs
    swap = one_hot(size, size, lambda r: remainder(r, pairs) * TILE + quotient(r, pairs))
    for p in range(out_ref.shape[0] // size):
        start = first + p * TILE
        if not isinstance(start, int):
            start = pl.multiple_of(start, TILE)
        block = held[:, pl.ds(start, TILE)].reshape(size, lanes)
        if pairs > 1:
            block = jnp.dot(swap, block, preferred_element_type=jnp.float32)
        out_ref[p * size : (p + 1) * size] = block.astype(out_ref.dtype)


def radon_kernel(gathers, down_ref, state_ref, data_ref, out_ref, turns, plain, turned, held):
    prepare(gathers, down_ref[0], data_ref, plain, turned)
    sum_offsets(gathers, 0, state_ref, plain, turned, turns, held)
    deal(held, 0, out_ref)


def radon(down, state, data, gathers):
    _, count, offsets = state.shape
    pairs, lanes = data.shape[2:]
    vmem = pl.BlockSpec(memory_space=pltpu.VMEM)
    return pl.pallas_call(
        functools.partial(radon_kernel, gathers),
        in_specs=[pl.BlockSpec(memory_space=pltpu.SMEM), vmem, vmem],
        out_specs=vmem,
        out_shape=jax.ShapeDtypeStruct((count * pairs, lanes), jnp.bfloat16),
        scratch_shapes=[
            pltpu.VMEM((pairs, 4, count, offsets), jnp.bfloat16),
            pltpu.VMEM((pairs, offsets, lanes), jnp.bfloat16),
            pltpu.VMEM((pairs, offsets, lanes), jnp.bfloat16),
            pltpu.VMEM((pairs, count, lanes), jnp.bfloat16),
        ],
        compiler_params=pltpu.CompilerParams(vmem_limit_bytes=24 * MIB),
    )(down, state, data)


def deal_half(held, me, first, out_refs):
    half = len(out_refs)
    each = held.shape[1] // half
    for s, out_ref in enumerate(out_refs):
        deal(held, remainder(me ^ (first + s), half) * each, out_ref)


def far_kernel(gathers, half, place_ref, state_ref, data_ref, plain, turned, sign_ref, *refs):
    *out_refs, turns, held = refs
    me = place_ref[1]
    prepare(gathers, place_ref[0], data_ref, plain, turned)
    sign_ref[...] = plain[0, :TILE]
    other = (1 - quotient(me, half)) * held.shape[1]
    sum_offsets(gathers, other, state_ref, plain, turned, turns, held)
    deal_half(held, me, half, out_refs)


def near_kernel(gathers, half, place_ref, state_ref, plain, turned, _, *refs):
    *out_refs, turns, held = refs
    me = place_ref[1]
    own = quotient(me, half) * held.shape[1]
    sum_offsets(gathers, own, state_ref, plain, turned, turns, held)
    deal_half(held, me, 0, out_refs)


def radon_swapped(place, state, data, gathers, offset_devices):
    _, count, offsets = state.shape
    pairs, lanes = data.shape[2:]
    half = offset_devices // 2
    vmem = pl.BlockSpec(memory_space=pltpu.VMEM)
    smem = pl.BlockSpec(memory_space=pltpu.SMEM)
    block = jax.ShapeDtypeStruct((count // offset_devices * pairs, lanes), jnp.bfloat16)
    spectra = jax.ShapeDtypeStruct((pairs, offsets, lanes), jnp.bfloat16)
    scratch = [
        pltpu.VMEM((pairs, 4, count // 2, offsets), jnp.bfloat16),
        pltpu.VMEM((pairs, count // 2, lanes), jnp.bfloat16),
    ]
    cost = pl.CostEstimate(
        flops=8 * count * offsets * pairs * lanes,
        bytes_accessed=8 * count * offsets,
        transcendentals=0,
    )
    sign = jax.ShapeDtypeStruct((TILE, lanes), jnp.bfloat16)
    plain, turned, sign, *far = pl.pallas_call(
        functools.partial(far_kernel, gathers, half),
        in_specs=[smem, vmem, vmem],
        out_specs=[vmem] * (3 + half),
        out_shape=[spectra, spectra, sign] + [block] * half,
        scratch_shapes=scratch,
        compiler_params=pltpu.CompilerParams(vmem_limit_bytes=20 * MIB),
        cost_estimate=cost,
    )(place, state, data)
    def swapped(part, s):
        swaps = [(o, o ^ s) for o in range(offset_devices)]
        return lax.ppermute(part, "offset", swaps)

    far = [swapped(part, half + s) for s, part in enumerate(far)]
    sign = swapped(sign, 1)
    near = pl.pallas_call(
        functools.partial(near_kernel, gathers, half),
        in_specs=[smem, vmem, vmem, vmem, vmem],
        out_specs=[vmem] * half,
        out_shape=[block] * half,
        scratch_shapes=scratch,
        compiler_params=pltpu.CompilerParams(vmem_limit_bytes=20 * MIB),
        cost_estimate=cost,
    )(place, state, plain, turned, sign)
    near = [swapped(part, s) if s else part for s, part in enumerate(near)]
    return list(range(half, offset_devices)) + list(range(half)), far + near


def join_kernel(scale, order, place_ref, *refs):
    *parts, out_ref, wide, ready, sems = refs
    groups, step, half_lanes, _ = ready.shape
    rows = wide.shape[1]
    pairs = rows // len(parts)
    copies = []
    for g in range(groups):
        for s, part in zip(order, parts):
            own = pl.ds(pl.multiple_of((place_ref[1] ^ s) * pairs, pairs), pairs)
            for i in range(step):
                p = g * step + i
                wide[p, own] = part[p * pairs : (p + 1) * pairs].astype(jnp.float32) * scale
        for i in range(step):
            block = wide[g * step + i].T
            ready[g, i, :, :rows] = block[:half_lanes]
            ready[g, i, :, rows:] = block[half_lanes:]
        copies.append(
            pltpu.make_async_copy(ready.at[g], out_ref.at[pl.ds(g * step, step)], sems.at[g])
        )
        copies[-1].start()
    for copy in copies:
        copy.wait()


def join(place, order, parts, slows, scale):
    pairs = parts[0].shape[0] // slows
    lanes = parts[0].shape[1]
    rows = len(parts) * pairs
    step = 4
    vmem = pl.BlockSpec(memory_space=pltpu.VMEM)
    return pl.pallas_call(
        functools.partial(join_kernel, scale, order),
        in_specs=[pl.BlockSpec(memory_space=pltpu.SMEM)] + [vmem] * len(parts),
        out_specs=pl.BlockSpec(memory_space=pl.ANY),
        out_shape=jax.ShapeDtypeStruct((slows, lanes // 2, 2 * rows), jnp.float32),
        scratch_shapes=[
            pltpu.VMEM((slows, rows, lanes), jnp.float32),
            pltpu.VMEM((slows // step, step, lanes // 2, 2 * rows), jnp.float32),
            pltpu.SemaphoreType.DMA((slows // step,)),
        ],
        compiler_params=pltpu.CompilerParams(vmem_limit_bytes=16 * MIB),
    )(place, *parts)


def finish_kernel(scale, in_ref, out_ref):
    devices, slows, pairs, lanes = in_ref.shape
    rows = devices * pairs
    for p in range(slows):
        block = in_ref[:, p].reshape(rows, lanes).astype(jnp.float32) * scale
        turned = block.T
        out_ref[p, :, :rows] = turned[: lanes // 2]
        out_ref[p, :, rows:] = turned[lanes // 2 :]


def finish(parts, scale):
    devices, slows, pairs, lanes = parts.shape
    rows = devices * pairs
    step = 8
    return pl.pallas_call(
        functools.partial(finish_kernel, scale),
        grid=(slows // step,),
        in_specs=[pl.BlockSpec((devices, step, pairs, lanes), lambda i: (0, i, 0, 0))],
        out_specs=pl.BlockSpec((step, lanes // 2, 2 * rows), lambda i: (i, 0, 0)),
        out_shape=jax.ShapeDtypeStruct((slows, lanes // 2, 2 * rows), jnp.float32),
        compiler_params=pltpu.CompilerParams(vmem_limit_bytes=32 * MIB),
    )(parts)


def local(raw_traces, trace_slot, offset_index, slowness_index):
    gathers, local_offsets = trace_slot.shape
    local_times = raw_traces.shape[1]
    freq_devices = lax.axis_size("freq")
    offset_devices = lax.axis_size("offset")
    devices = freq_devices * offset_devices
    total_time = local_times * freq_devices
    offsets = local_offsets * offset_devices
    band = NF // freq_devices
    own_freqs = NF // devices
    halves = 2
    pairs = own_freqs // halves
    own_offsets = local_offsets // freq_devices

    me = lax.axis_index("freq").astype(jnp.int32).reshape(1)
    series = list(pick(me, trace_slot.astype(jnp.float32), raw_traces, freq_devices))
    for s in list(range(2, freq_devices)) + [1]:
        swaps = [(f, f ^ s) for f in range(freq_devices)]
        series[s] = lax.ppermute(series[s], "freq", swaps)
    table = jnp.asarray(table_rows(total_time, freq_devices, offset_devices, halves, pairs))
    spectrum = transform(me, table, series, pairs, gathers)
    data = lax.all_to_all(spectrum, ("offset", "freq"), 0, 0, tiled=True)

    offs = offset_index.reshape(1, offsets).astype(jnp.float32)
    slows = slowness_index.astype(jnp.float32)[:, None]
    first = lax.axis_index("freq") * band + lax.axis_index("offset") * pairs
    base = (2 * first + 1).astype(jnp.float32) * (math.pi / total_time)
    state = moveout(base.reshape(1), slows, offs, band // halves, total_time)
    down = (2 * lax.axis_index("offset") // offset_devices).astype(jnp.int32)
    place = jnp.stack([down, lax.axis_index("offset").astype(jnp.int32)])
    slows_each = NP // offset_devices
    scale = 1.0 / math.sqrt(offsets)
    if slows_each % TILE == 0:
        order, blocks = radon_swapped(place, state, data, gathers, offset_devices)
        result = join(place, order, blocks, slows_each, scale)
    else:
        panel = radon(place, state, data, gathers)
        panel = panel.reshape(offset_devices, slows_each, pairs, 2 * halves * gathers)
        result = finish(lax.all_to_all(panel, "offset", 0, 0, tiled=True), scale)
    return jnp.transpose(result, (0, 2, 1))


def solution(mesh):
    placed = (P("offset", "freq"), P(None, "offset"), P(), P())
    return jax.shard_map(
        local, mesh=mesh, in_specs=placed, out_specs=P("offset", "freq", None), check_vma=False
    )
```

```python
import functools
import math

import jax
import jax.numpy as jnp
import ml_dtypes
import numpy as np
from jax import lax
from jax.experimental import pallas as pl
from jax.experimental.pallas import tpu as pltpu
from jax.sharding import PartitionSpec as P

NF = 1024
NP = 256
APEX_TIME = 100.0
CURVATURE = 0.0003
MIB = 1 << 20


def table_rows(total_time, freq_devices, offset_devices, halves, pairs):
    band = NF // freq_devices
    o, f, a, k = np.meshgrid(
        np.arange(offset_devices // 2),
        np.arange(freq_devices),
        np.arange(halves),
        np.arange(pairs),
        indexing="ij",
    )
    freq_ids = (f * band + a * (band // halves) + o * pairs + k).reshape(-1, pairs)
    times = np.concatenate([np.arange(0, total_time, 2), np.arange(1, total_time, 2)])
    turns = (2 * freq_ids[..., None] + 1) * times % (2 * total_time)
    angles = turns.astype(np.float32) * np.float32(math.pi / total_time)
    both = np.stack([np.cos(angles), -np.sin(angles)], axis=1).reshape(-1, total_time)
    return (both / np.float32(math.sqrt(total_time))).astype(ml_dtypes.bfloat16)


def pick_kernel(me_ref, slot_ref, raw_ref, *out_refs):
    gathers, local_offsets = slot_ref.shape
    own_offsets = local_offsets // len(out_refs)
    times = raw_ref.shape[1]
    half = times // 2
    row = lax.broadcasted_iota(jnp.int32, (times, times), 0)
    column = lax.broadcasted_iota(jnp.int32, (times, times), 1)
    source = jnp.where(column < half, 2 * column, 2 * (column - half) + 1)
    split = jnp.where(row == source, 1.0, 0.0).astype(jnp.bfloat16)
    raw = jnp.dot(raw_ref[...], split, preferred_element_type=jnp.float32).astype(jnp.bfloat16)
    lane = lax.broadcasted_iota(jnp.int32, (gathers, raw_ref.shape[0]), 1)
    slot = slot_ref[...]
    place = lax.broadcasted_iota(jnp.int32, slot.shape, 1)
    for s, out_ref in enumerate(out_refs):
        first = (me_ref[0] ^ s) * own_offsets
        picks = []
        for h in range(own_offsets):
            wanted = jnp.sum(jnp.where(place == first + h, slot, 0.0), axis=1, keepdims=True)
            picks.append(
                jnp.where(lane == wanted.astype(jnp.int32), 1.0, 0.0).astype(jnp.bfloat16)
            )
        out_ref[...] = jnp.dot(
            jnp.concatenate(picks, axis=0), raw, preferred_element_type=jnp.float32
        ).astype(out_ref.dtype)


def pick(me, trace_slot, raw_traces, groups):
    gathers, local_offsets = trace_slot.shape
    rows = gathers * local_offsets // groups
    vmem = pl.BlockSpec(memory_space=pltpu.VMEM)
    block = jax.ShapeDtypeStruct((rows, raw_traces.shape[1]), raw_traces.dtype)
    return pl.pallas_call(
        pick_kernel,
        in_specs=[pl.BlockSpec(memory_space=pltpu.SMEM), vmem, vmem],
        out_specs=[vmem] * groups,
        out_shape=[block] * groups,
        compiler_params=pltpu.CompilerParams(vmem_limit_bytes=24 * MIB),
    )(me, trace_slot, raw_traces)


def regroup(parts, gathers):
    lanes = 4 * gathers
    lane = lax.broadcasted_iota(jnp.int32, (1, lanes), 1)
    low_half = lane < 2 * gathers
    low_part = lane % (2 * gathers) < gathers
    found = []
    for q in range(parts[0].shape[1] // lanes):
        x = [part[:, q * lanes : (q + 1) * lanes] for part in parts]
        for top in range(2):
            pair = []
            for part in range(2):
                a, b = x[part], x[2 + part]
                if top == 0:
                    pair.append(jnp.where(low_half, a, pltpu.roll(b, 2 * gathers, 1)))
                else:
                    pair.append(jnp.where(low_half, pltpu.roll(a, 2 * gathers, 1), b))
            found.append(jnp.where(low_part, pair[0], pltpu.roll(pair[1], gathers, 1)))
            found.append(jnp.where(low_part, pltpu.roll(pair[0], lanes - gathers, 1), pair[1]))
    return found


def time_sums(me, first, table_ref, series_refs, even, odd, own):
    half = even.shape[1] // 2
    depth = table_ref.shape[1] // 2
    evens = odds = None
    for r in range(len(series_refs) // 2):
        start = (quotient(me, 2) ^ (first + r)) * 2 * half
        even_part = jnp.dot(
            table_ref[own, pl.ds(pl.multiple_of(start, 2 * half), 2 * half)],
            even[r],
            preferred_element_type=jnp.float32,
        )
        odd_part = jnp.dot(
            table_ref[own, pl.ds(pl.multiple_of(depth + start, 2 * half), 2 * half)],
            odd[r],
            preferred_element_type=jnp.float32,
        )
        evens = even_part if evens is None else evens + even_part
        odds = odd_part if odds is None else odds + odd_part
    return evens, odds


def turn_series(me, series_refs, even, odd):
    half = even.shape[1] // 2
    for s, series_ref in enumerate(series_refs):
        turned = series_ref[...].T
        place = pl.ds(pl.multiple_of(((me ^ s) & 1) * half, half), half)
        even[s // 2, place] = turned[:half]
        odd[s // 2, place] = turned[half:]


def begin_kernel(chunks, me_ref, table_ref, *refs):
    *series_refs, out_ref, even, odd = refs
    me = me_ref[0]
    turn_series(me, series_refs, even, odd)
    step = table_ref.shape[0] // chunks
    for i in range(chunks):
        own = slice(i * step, (i + 1) * step)
        out_ref[0, own], out_ref[1, own] = time_sums(
            me, 0, table_ref, series_refs, even, odd, own
        )


def transform_kernel(pairs, gathers, chunks, me_ref, table_ref, begun_ref, *refs):
    *series_refs, out_ref, even, odd = refs
    me = me_ref[0]
    turn_series(me, series_refs, even, odd)
    step = table_ref.shape[0] // chunks
    for i in range(chunks):
        own = slice(i * step, (i + 1) * step)
        evens, odds = time_sums(me, 1, table_ref, series_refs, even, odd, own)
        evens = evens + begun_ref[0, own]
        odds = odds + begun_ref[1, own]
        low = evens + odds
        high = evens - odds
        if len(out_ref.shape) == 3:
            row = lax.broadcasted_iota(jnp.int32, (step, 1), 0)
            out_ref[0, own] = low.astype(out_ref.dtype)
            out_ref[1, own] = jnp.where(row // pairs % 2 == 0, high, -high).astype(out_ref.dtype)
            continue
        targets = step // (4 * pairs)
        devices = out_ref.shape[0]
        for d in range(targets):
            cuts = [slice((4 * d + c) * pairs, (4 * d + c + 1) * pairs) for c in range(4)]
            place = i * targets + d
            for h, value in enumerate(regroup([low[cut] for cut in cuts], gathers)):
                out_ref[place, h] = value.astype(out_ref.dtype)
            mirrored = [high[cuts[2]], -high[cuts[3]], high[cuts[0]], -high[cuts[1]]]
            for h, value in enumerate(regroup(mirrored, gathers)):
                out_ref[devices - 1 - place, h] = value.astype(out_ref.dtype)


def transform(me, table, series, pairs, gathers):
    columns, total_time = table.shape
    rows, local_times = series[0].shape
    own_offsets = rows // gathers
    devices = columns // (2 * pairs)
    final = (devices, own_offsets, pairs, 4 * gathers)
    chunks = 4
    aligned = rows % (4 * gathers) == 0 and pairs % 8 == 0 and devices % (2 * chunks) == 0
    vmem = pl.BlockSpec(memory_space=pltpu.VMEM)
    smem = pl.BlockSpec(memory_space=pltpu.SMEM)
    early, late = series[:2], series[2:]

    def scratch(blocks):
        return [pltpu.VMEM((len(blocks) // 2, local_times, rows), jnp.bfloat16)] * 2

    params = pltpu.CompilerParams(vmem_limit_bytes=24 * MIB)
    begun = pl.pallas_call(
        functools.partial(begin_kernel, chunks),
        in_specs=[smem] + [vmem] * (1 + len(early)),
        out_specs=vmem,
        out_shape=jax.ShapeDtypeStruct((2, columns, rows), jnp.float32),
        scratch_shapes=scratch(early),
        compiler_params=params,
        cost_estimate=pl.CostEstimate(
            flops=columns * total_time * rows,
            bytes_accessed=2 * columns * total_time,
            transcendentals=0,
        ),
    )(me, table, *early)
    out = pl.pallas_call(
        functools.partial(transform_kernel, pairs, gathers, chunks),
        in_specs=[smem] + [vmem] * (2 + len(late)),
        out_specs=vmem,
        out_shape=jax.ShapeDtypeStruct(final if aligned else (2, columns, rows), jnp.bfloat16),
        scratch_shapes=scratch(late),
        compiler_params=params,
    )(me, table, begun, *late)
    if aligned:
        return out
    out = out.reshape(2, devices // 2, 2, 2, pairs, own_offsets, gathers)
    out = jnp.concatenate([out[0], jnp.flip(out[1], (0, 1))], axis=0)
    return out.transpose(0, 4, 3, 1, 2, 5).reshape(final)


def moveout_kernel(shift, total_time, base_ref, slow_ref, offs_ref, out_ref):
    spread = CURVATURE * slow_ref[...] * offs_ref[...]
    delay = jnp.sqrt(APEX_TIME * APEX_TIME + spread * spread) - APEX_TIME
    phase = base_ref[0] * delay
    c = jnp.cos(phase)
    s = jnp.sin(phase)
    far = delay * (2.0 * shift * math.pi / total_time)
    far_c = jnp.cos(far)
    far_s = jnp.sin(far)
    turn = delay * (2.0 * math.pi / total_time)
    out_ref[0] = c
    out_ref[1] = c * far_c - s * far_s
    out_ref[2] = s
    out_ref[3] = s * far_c + c * far_s
    out_ref[4] = jnp.cos(turn)
    out_ref[5] = jnp.sin(turn)


def moveout(base, slows, offs, shift, total_time):
    count = slows.shape[0]
    offsets = offs.shape[1]
    rows = min(count, 64)
    return pl.pallas_call(
        functools.partial(moveout_kernel, shift, total_time),
        grid=(count // rows,),
        in_specs=[
            pl.BlockSpec(memory_space=pltpu.SMEM),
            pl.BlockSpec((rows, 1), lambda i: (i, 0)),
            pl.BlockSpec((1, offsets), lambda i: (0, 0)),
        ],
        out_specs=pl.BlockSpec((6, rows, offsets), lambda i: (0, i, 0)),
        out_shape=jax.ShapeDtypeStruct((6, count, offsets), jnp.float32),
        compiler_params=pltpu.CompilerParams(vmem_limit_bytes=24 * MIB),
        cost_estimate=pl.CostEstimate(
            flops=300 * count * offsets,
            bytes_accessed=24 * count * offsets,
            transcendentals=6 * count * offsets,
        ),
    )(base, slows, offs)


def quotient(value, divisor):
    if divisor & (divisor - 1):
        return value // divisor
    return lax.shift_right_logical(value, jnp.int32(divisor.bit_length() - 1))


def remainder(value, divisor):
    if divisor & (divisor - 1):
        return value % divisor
    return value & (divisor - 1)


def one_hot(rows, columns, source):
    row = lax.broadcasted_iota(jnp.int32, (rows, 1), 0)
    column = lax.broadcasted_iota(jnp.int32, (rows, columns), 1)
    return jnp.where(column == source(row), 1.0, 0.0).astype(jnp.bfloat16)


TILE = 16


def prepare(gathers, down, data_ref, plain, turned):
    devices, own_offsets, pairs, lanes = data_ref.shape
    size = TILE * pairs
    together = TILE // own_offsets

    def received(r):
        k = quotient(r, TILE)
        return remainder(r, TILE) * pairs + k + down * (pairs - 1 - 2 * k)

    swap = one_hot(size, size, received)
    for d in range(devices // together):
        block = data_ref[d * together : (d + 1) * together].reshape(size, lanes)
        if pairs > 1:
            block = jnp.dot(swap, block, preferred_element_type=jnp.float32).astype(jnp.bfloat16)
        plain[:, d * TILE : (d + 1) * TILE] = block.reshape(pairs, TILE, lanes)
    row = lax.broadcasted_iota(jnp.int32, (lanes, lanes), 0)
    column = lax.broadcasted_iota(jnp.int32, (lanes, lanes), 1)
    quarter = jnp.where(
        remainder(column, 2 * gathers) < gathers,
        jnp.where(row == column + gathers, -1.0, 0.0),
        jnp.where(row == column - gathers, 1.0, 0.0),
    ).astype(jnp.bfloat16)
    for k in range(pairs):
        turned[k] = jnp.dot(plain[k], quarter, preferred_element_type=jnp.float32).astype(
            jnp.bfloat16
        )


def sum_offsets(gathers, first, state_ref, plain, turned, turns, held):
    pairs, slows, lanes = held.shape
    offsets = plain.shape[1]

    def fill(t, carry):
        source = pl.ds(pl.multiple_of(first + t * TILE, TILE), TILE)
        own = pl.ds(pl.multiple_of(t * TILE, TILE), TILE)
        step_c = state_ref[4, source]
        step_s = state_ref[5, source]
        twice = 2.0 * step_c
        now = [state_ref[i, source] for i in range(4)]
        past = [now[a] * step_c + now[2 + a] * step_s for a in range(2)]
        past += [now[2 + a] * step_c - now[a] * step_s for a in range(2)]
        for k in range(pairs):
            for i in range(4):
                turns[k, i, own] = now[i].astype(jnp.bfloat16)
                now[i], past[i] = twice * now[i] - past[i], now[i]
        return carry

    lax.fori_loop(0, slows // TILE, fill, 0)
    first_half = lax.broadcasted_iota(jnp.int32, (1, lanes), 1) < 2 * gathers
    for k in range(pairs):
        cosine = turns[k, :2].reshape(2 * slows, offsets)
        sines = turns[k, 2:].reshape(2 * slows, offsets)
        both = jnp.dot(cosine, plain[k], preferred_element_type=jnp.float32) + jnp.dot(
            sines, turned[k], preferred_element_type=jnp.float32
        )
        held[k] = jnp.where(first_half, both[:slows], both[slows:]).astype(jnp.bfloat16)


def dealing(pairs):
    size = TILE * pairs
    return one_hot(size, size, lambda r: remainder(r, pairs) * TILE + quotient(r, pairs))


def deal(swap, held, first, out_ref):
    pairs, _, lanes = held.shape
    size = TILE * pairs
    for p in range(out_ref.shape[0] // size):
        start = first + p * TILE
        if not isinstance(start, int):
            start = pl.multiple_of(start, TILE)
        block = held[:, pl.ds(start, TILE)].reshape(size, lanes)
        if pairs > 1:
            block = jnp.dot(swap, block, preferred_element_type=jnp.float32)
        out_ref[p * size : (p + 1) * size] = block.astype(out_ref.dtype)


def radon_kernel(gathers, down_ref, state_ref, data_ref, out_ref, turns, plain, turned, held):
    prepare(gathers, down_ref[0], data_ref, plain, turned)
    sum_offsets(gathers, 0, state_ref, plain, turned, turns, held)
    deal(dealing(held.shape[0]), held, 0, out_ref)


def radon(down, state, data, gathers):
    _, count, offsets = state.shape
    pairs, lanes = data.shape[2:]
    vmem = pl.BlockSpec(memory_space=pltpu.VMEM)
    return pl.pallas_call(
        functools.partial(radon_kernel, gathers),
        in_specs=[pl.BlockSpec(memory_space=pltpu.SMEM), vmem, vmem],
        out_specs=vmem,
        out_shape=jax.ShapeDtypeStruct((count * pairs, lanes), jnp.bfloat16),
        scratch_shapes=[
            pltpu.VMEM((pairs, 4, count, offsets), jnp.bfloat16),
            pltpu.VMEM((pairs, offsets, lanes), jnp.bfloat16),
            pltpu.VMEM((pairs, offsets, lanes), jnp.bfloat16),
            pltpu.VMEM((pairs, count, lanes), jnp.bfloat16),
        ],
        compiler_params=pltpu.CompilerParams(vmem_limit_bytes=24 * MIB),
    )(down, state, data)


def deal_half(held, me, first, out_refs):
    swap = dealing(held.shape[0])
    half = len(out_refs)
    each = held.shape[1] // half
    for s, out_ref in enumerate(out_refs):
        deal(swap, held, remainder(me ^ (first + s), half) * each, out_ref)


def far_kernel(gathers, half, place_ref, state_ref, data_ref, plain, turned, sign_ref, *refs):
    *out_refs, turns, held = refs
    me = place_ref[1]
    prepare(gathers, place_ref[0], data_ref, plain, turned)
    sign_ref[...] = plain[0, :TILE]
    other = (1 - quotient(me, half)) * held.shape[1]
    sum_offsets(gathers, other, state_ref, plain, turned, turns, held)
    deal_half(held, me, half, out_refs)


def near_kernel(gathers, half, place_ref, state_ref, plain, turned, _, *refs):
    *out_refs, turns, held = refs
    me = place_ref[1]
    own = quotient(me, half) * held.shape[1]
    sum_offsets(gathers, own, state_ref, plain, turned, turns, held)
    deal_half(held, me, 0, out_refs)


def radon_swapped(place, state, data, gathers, offset_devices):
    _, count, offsets = state.shape
    pairs, lanes = data.shape[2:]
    half = offset_devices // 2
    vmem = pl.BlockSpec(memory_space=pltpu.VMEM)
    smem = pl.BlockSpec(memory_space=pltpu.SMEM)
    block = jax.ShapeDtypeStruct((count // offset_devices * pairs, lanes), jnp.bfloat16)
    spectra = jax.ShapeDtypeStruct((pairs, offsets, lanes), jnp.bfloat16)
    scratch = [
        pltpu.VMEM((pairs, 4, count // 2, offsets), jnp.bfloat16),
        pltpu.VMEM((pairs, count // 2, lanes), jnp.bfloat16),
    ]
    cost = pl.CostEstimate(
        flops=8 * count * offsets * pairs * lanes,
        bytes_accessed=8 * count * offsets,
        transcendentals=0,
    )
    sign = jax.ShapeDtypeStruct((TILE, lanes), jnp.bfloat16)
    plain, turned, sign, *far = pl.pallas_call(
        functools.partial(far_kernel, gathers, half),
        in_specs=[smem, vmem, vmem],
        out_specs=[vmem] * (3 + half),
        out_shape=[spectra, spectra, sign] + [block] * half,
        scratch_shapes=scratch,
        compiler_params=pltpu.CompilerParams(vmem_limit_bytes=20 * MIB),
        cost_estimate=cost,
    )(place, state, data)
    def swapped(part, s):
        swaps = [(o, o ^ s) for o in range(offset_devices)]
        return lax.ppermute(part, "offset", swaps)

    far[:-1] = [swapped(part, half + s) for s, part in enumerate(far[:-1])]
    sign = swapped(sign, 1)
    near = pl.pallas_call(
        functools.partial(near_kernel, gathers, half),
        in_specs=[smem, vmem, vmem, vmem, vmem],
        out_specs=[vmem] * half,
        out_shape=[block] * half,
        scratch_shapes=scratch,
        compiler_params=pltpu.CompilerParams(vmem_limit_bytes=20 * MIB),
        cost_estimate=cost,
    )(place, state, plain, turned, sign)
    near = list(near)
    last, far[0] = lax.optimization_barrier((far[-1], far[0]))
    near = [swapped(part, s) if s else part for s, part in enumerate(near)]
    far[-1] = swapped(last, offset_devices - 1)
    parts = near + far
    return list(range(half, offset_devices - 1)) + list(range(half))[::-1] + [offset_devices - 1], [parts[s] for s in list(range(half, offset_devices - 1)) + list(range(half))[::-1] + [offset_devices - 1]]


def join_kernel(scale, order, place_ref, *refs):
    *parts, out_ref, wide, ready, sems = refs
    groups, step, half_lanes, _ = ready.shape
    rows = wide.shape[1]
    pairs = rows // len(parts)
    copies = []
    for g in range(groups):
        for s, part in zip(order, parts):
            own = pl.ds(pl.multiple_of((place_ref[1] ^ s) * pairs, pairs), pairs)
            for i in range(step):
                p = g * step + i
                wide[p, own] = part[p * pairs : (p + 1) * pairs].astype(jnp.float32) * scale
        for i in range(step):
            block = wide[g * step + i].T
            ready[g, i, :, :rows] = block[:half_lanes]
            ready[g, i, :, rows:] = block[half_lanes:]
        copies.append(
            pltpu.make_async_copy(ready.at[g], out_ref.at[pl.ds(g * step, step)], sems.at[g])
        )
        copies[-1].start()
    for copy in copies:
        copy.wait()


def join(place, order, parts, slows, scale):
    pairs = parts[0].shape[0] // slows
    lanes = parts[0].shape[1]
    rows = len(parts) * pairs
    step = 4
    vmem = pl.BlockSpec(memory_space=pltpu.VMEM)
    return pl.pallas_call(
        functools.partial(join_kernel, scale, order),
        in_specs=[pl.BlockSpec(memory_space=pltpu.SMEM)] + [vmem] * len(parts),
        out_specs=pl.BlockSpec(memory_space=pl.ANY),
        out_shape=jax.ShapeDtypeStruct((slows, lanes // 2, 2 * rows), jnp.float32),
        scratch_shapes=[
            pltpu.VMEM((slows, rows, lanes), jnp.float32),
            pltpu.VMEM((slows // step, step, lanes // 2, 2 * rows), jnp.float32),
            pltpu.SemaphoreType.DMA((slows // step,)),
        ],
        compiler_params=pltpu.CompilerParams(vmem_limit_bytes=16 * MIB),
    )(place, *parts)


def finish_kernel(scale, in_ref, out_ref):
    devices, slows, pairs, lanes = in_ref.shape
    rows = devices * pairs
    for p in range(slows):
        block = in_ref[:, p].reshape(rows, lanes).astype(jnp.float32) * scale
        turned = block.T
        out_ref[p, :, :rows] = turned[: lanes // 2]
        out_ref[p, :, rows:] = turned[lanes // 2 :]


def finish(parts, scale):
    devices, slows, pairs, lanes = parts.shape
    rows = devices * pairs
    step = 8
    return pl.pallas_call(
        functools.partial(finish_kernel, scale),
        grid=(slows // step,),
        in_specs=[pl.BlockSpec((devices, step, pairs, lanes), lambda i: (0, i, 0, 0))],
        out_specs=pl.BlockSpec((step, lanes // 2, 2 * rows), lambda i: (i, 0, 0)),
        out_shape=jax.ShapeDtypeStruct((slows, lanes // 2, 2 * rows), jnp.float32),
        compiler_params=pltpu.CompilerParams(vmem_limit_bytes=32 * MIB),
    )(parts)


def local(raw_traces, trace_slot, offset_index, slowness_index):
    gathers, local_offsets = trace_slot.shape
    local_times = raw_traces.shape[1]
    freq_devices = lax.axis_size("freq")
    offset_devices = lax.axis_size("offset")
    devices = freq_devices * offset_devices
    total_time = local_times * freq_devices
    offsets = local_offsets * offset_devices
    band = NF // freq_devices
    own_freqs = NF // devices
    halves = 2
    pairs = own_freqs // halves
    own_offsets = local_offsets // freq_devices

    me = lax.axis_index("freq").astype(jnp.int32).reshape(1)
    series = list(pick(me, trace_slot.astype(jnp.float32), raw_traces, freq_devices))
    for s in list(range(2, freq_devices)) + [1]:
        swaps = [(f, f ^ s) for f in range(freq_devices)]
        series[s] = lax.ppermute(series[s], "freq", swaps)
    table = jnp.asarray(table_rows(total_time, freq_devices, offset_devices, halves, pairs))
    spectrum = transform(me, table, series, pairs, gathers)
    data = lax.all_to_all(spectrum, ("offset", "freq"), 0, 0, tiled=True)

    offs = offset_index.reshape(1, offsets).astype(jnp.float32)
    slows = slowness_index.astype(jnp.float32)[:, None]
    first = lax.axis_index("freq") * band + lax.axis_index("offset") * pairs
    base = (2 * first + 1).astype(jnp.float32) * (math.pi / total_time)
    state = moveout(base.reshape(1), slows, offs, band // halves, total_time)
    down = (2 * lax.axis_index("offset") // offset_devices).astype(jnp.int32)
    place = jnp.stack([down, lax.axis_index("offset").astype(jnp.int32)])
    slows_each = NP // offset_devices
    scale = 1.0 / math.sqrt(offsets)
    if slows_each % TILE == 0:
        order, blocks = radon_swapped(place, state, data, gathers, offset_devices)
        result = join(place, order, blocks, slows_each, scale)
    else:
        panel = radon(place, state, data, gathers)
        panel = panel.reshape(offset_devices, slows_each, pairs, 2 * halves * gathers)
        result = finish(lax.all_to_all(panel, "offset", 0, 0, tiled=True), scale)
    return jnp.transpose(result, (0, 2, 1))


def solution(mesh):
    placed = (P("offset", "freq"), P(None, "offset"), P(), P())
    return jax.shard_map(
        local, mesh=mesh, in_specs=placed, out_specs=P("offset", "freq", None), check_vma=False
    )
```

```python
import functools
import math

import jax
import jax.numpy as jnp
import ml_dtypes
import numpy as np
from jax import lax
from jax.experimental import pallas as pl
from jax.experimental.pallas import tpu as pltpu
from jax.sharding import PartitionSpec as P

NF = 1024
NP = 256
APEX_TIME = 100.0
CURVATURE = 0.0003
MIB = 1 << 20


def table_rows(total_time, freq_devices, offset_devices, halves, pairs):
    band = NF // freq_devices
    o, f, a, k = np.meshgrid(
        np.arange(offset_devices // 2),
        np.arange(freq_devices),
        np.arange(halves),
        np.arange(pairs),
        indexing="ij",
    )
    freq_ids = (f * band + a * (band // halves) + o * pairs + k).reshape(-1, pairs)
    times = np.concatenate([np.arange(0, total_time, 2), np.arange(1, total_time, 2)])
    turns = (2 * freq_ids[..., None] + 1) * times % (2 * total_time)
    angles = turns.astype(np.float32) * np.float32(math.pi / total_time)
    both = np.stack([np.cos(angles), -np.sin(angles)], axis=1).reshape(-1, total_time)
    return (both / np.float32(math.sqrt(total_time))).astype(ml_dtypes.bfloat16)


def pick_kernel(me_ref, slot_ref, raw_ref, *out_refs):
    gathers, local_offsets = slot_ref.shape
    own_offsets = local_offsets // len(out_refs)
    times = raw_ref.shape[1]
    half = times // 2
    row = lax.broadcasted_iota(jnp.int32, (times, times), 0)
    column = lax.broadcasted_iota(jnp.int32, (times, times), 1)
    source = jnp.where(column < half, 2 * column, 2 * (column - half) + 1)
    split = jnp.where(row == source, 1.0, 0.0).astype(jnp.bfloat16)
    raw = jnp.dot(raw_ref[...], split, preferred_element_type=jnp.float32).astype(jnp.bfloat16)
    lane = lax.broadcasted_iota(jnp.int32, (gathers, raw_ref.shape[0]), 1)
    slot = slot_ref[...]
    place = lax.broadcasted_iota(jnp.int32, slot.shape, 1)
    for s, out_ref in enumerate(out_refs):
        first = (me_ref[0] ^ s) * own_offsets
        picks = []
        for h in range(own_offsets):
            wanted = jnp.sum(jnp.where(place == first + h, slot, 0.0), axis=1, keepdims=True)
            picks.append(
                jnp.where(lane == wanted.astype(jnp.int32), 1.0, 0.0).astype(jnp.bfloat16)
            )
        out_ref[...] = jnp.dot(
            jnp.concatenate(picks, axis=0), raw, preferred_element_type=jnp.float32
        ).astype(out_ref.dtype)


def pick(me, trace_slot, raw_traces, groups):
    gathers, local_offsets = trace_slot.shape
    rows = gathers * local_offsets // groups
    vmem = pl.BlockSpec(memory_space=pltpu.VMEM)
    block = jax.ShapeDtypeStruct((rows, raw_traces.shape[1]), raw_traces.dtype)
    return pl.pallas_call(
        pick_kernel,
        in_specs=[pl.BlockSpec(memory_space=pltpu.SMEM), vmem, vmem],
        out_specs=[vmem] * groups,
        out_shape=[block] * groups,
        compiler_params=pltpu.CompilerParams(vmem_limit_bytes=24 * MIB),
    )(me, trace_slot, raw_traces)


def regroup(parts, gathers):
    lanes = 4 * gathers
    lane = lax.broadcasted_iota(jnp.int32, (1, lanes), 1)
    low_half = lane < 2 * gathers
    low_part = lane % (2 * gathers) < gathers
    found = []
    for q in range(parts[0].shape[1] // lanes):
        x = [part[:, q * lanes : (q + 1) * lanes] for part in parts]
        for top in range(2):
            pair = []
            for part in range(2):
                a, b = x[part], x[2 + part]
                if top == 0:
                    pair.append(jnp.where(low_half, a, pltpu.roll(b, 2 * gathers, 1)))
                else:
                    pair.append(jnp.where(low_half, pltpu.roll(a, 2 * gathers, 1), b))
            found.append(jnp.where(low_part, pair[0], pltpu.roll(pair[1], gathers, 1)))
            found.append(jnp.where(low_part, pltpu.roll(pair[0], lanes - gathers, 1), pair[1]))
    return found


def time_sums(me, first, table_ref, series_refs, even, odd, own):
    half = even.shape[1] // 2
    depth = table_ref.shape[1] // 2
    evens = odds = None
    for r in range(len(series_refs) // 2):
        start = (quotient(me, 2) ^ (first + r)) * 2 * half
        even_part = jnp.dot(
            table_ref[own, pl.ds(pl.multiple_of(start, 2 * half), 2 * half)],
            even[r],
            preferred_element_type=jnp.float32,
        )
        odd_part = jnp.dot(
            table_ref[own, pl.ds(pl.multiple_of(depth + start, 2 * half), 2 * half)],
            odd[r],
            preferred_element_type=jnp.float32,
        )
        evens = even_part if evens is None else evens + even_part
        odds = odd_part if odds is None else odds + odd_part
    return evens, odds


def turn_series(me, series_refs, even, odd):
    half = even.shape[1] // 2
    for s, series_ref in enumerate(series_refs):
        turned = series_ref[...].T
        place = pl.ds(pl.multiple_of(((me ^ s) & 1) * half, half), half)
        even[s // 2, place] = turned[:half]
        odd[s // 2, place] = turned[half:]


def begin_kernel(chunks, me_ref, table_ref, *refs):
    *series_refs, out_ref, even, odd = refs
    me = me_ref[0]
    turn_series(me, series_refs, even, odd)
    step = table_ref.shape[0] // chunks
    for i in range(chunks):
        own = slice(i * step, (i + 1) * step)
        out_ref[0, own], out_ref[1, own] = time_sums(
            me, 0, table_ref, series_refs, even, odd, own
        )


def transform_kernel(pairs, gathers, chunks, me_ref, table_ref, begun_ref, *refs):
    *series_refs, out_ref, even, odd = refs
    me = me_ref[0]
    turn_series(me, series_refs, even, odd)
    step = table_ref.shape[0] // chunks
    for i in range(chunks):
        own = slice(i * step, (i + 1) * step)
        evens, odds = time_sums(me, 1, table_ref, series_refs, even, odd, own)
        evens = evens + begun_ref[0, own]
        odds = odds + begun_ref[1, own]
        low = evens + odds
        high = evens - odds
        if len(out_ref.shape) == 3:
            row = lax.broadcasted_iota(jnp.int32, (step, 1), 0)
            out_ref[0, own] = low.astype(out_ref.dtype)
            out_ref[1, own] = jnp.where(row // pairs % 2 == 0, high, -high).astype(out_ref.dtype)
            continue
        targets = step // (4 * pairs)
        devices = out_ref.shape[0]
        for d in range(targets):
            cuts = [slice((4 * d + c) * pairs, (4 * d + c + 1) * pairs) for c in range(4)]
            place = i * targets + d
            for h, value in enumerate(regroup([low[cut] for cut in cuts], gathers)):
                out_ref[place, h] = value.astype(out_ref.dtype)
            mirrored = [high[cuts[2]], -high[cuts[3]], high[cuts[0]], -high[cuts[1]]]
            for h, value in enumerate(regroup(mirrored, gathers)):
                out_ref[devices - 1 - place, h] = value.astype(out_ref.dtype)


def transform(me, table, series, pairs, gathers):
    columns, total_time = table.shape
    rows, local_times = series[0].shape
    own_offsets = rows // gathers
    devices = columns // (2 * pairs)
    final = (devices, own_offsets, pairs, 4 * gathers)
    chunks = 4
    aligned = rows % (4 * gathers) == 0 and pairs % 8 == 0 and devices % (2 * chunks) == 0
    vmem = pl.BlockSpec(memory_space=pltpu.VMEM)
    smem = pl.BlockSpec(memory_space=pltpu.SMEM)
    early, late = series[:2], series[2:]

    def scratch(blocks):
        return [pltpu.VMEM((len(blocks) // 2, local_times, rows), jnp.bfloat16)] * 2

    params = pltpu.CompilerParams(vmem_limit_bytes=24 * MIB)
    begun = pl.pallas_call(
        functools.partial(begin_kernel, chunks),
        in_specs=[smem] + [vmem] * (1 + len(early)),
        out_specs=vmem,
        out_shape=jax.ShapeDtypeStruct((2, columns, rows), jnp.float32),
        scratch_shapes=scratch(early),
        compiler_params=params,
        cost_estimate=pl.CostEstimate(
            flops=columns * total_time * rows,
            bytes_accessed=2 * columns * total_time,
            transcendentals=0,
        ),
    )(me, table, *early)
    out = pl.pallas_call(
        functools.partial(transform_kernel, pairs, gathers, chunks),
        in_specs=[smem] + [vmem] * (2 + len(late)),
        out_specs=vmem,
        out_shape=jax.ShapeDtypeStruct(final if aligned else (2, columns, rows), jnp.bfloat16),
        scratch_shapes=scratch(late),
        compiler_params=params,
    )(me, table, begun, *late)
    if aligned:
        return out
    out = out.reshape(2, devices // 2, 2, 2, pairs, own_offsets, gathers)
    out = jnp.concatenate([out[0], jnp.flip(out[1], (0, 1))], axis=0)
    return out.transpose(0, 4, 3, 1, 2, 5).reshape(final)


def moveout_kernel(shift, total_time, base_ref, slow_ref, offs_ref, out_ref):
    spread = CURVATURE * slow_ref[...] * offs_ref[...]
    delay = jnp.sqrt(APEX_TIME * APEX_TIME + spread * spread) - APEX_TIME
    phase = base_ref[0] * delay
    c = jnp.cos(phase)
    s = jnp.sin(phase)
    far = delay * (2.0 * shift * math.pi / total_time)
    far_c = jnp.cos(far)
    far_s = jnp.sin(far)
    turn = delay * (2.0 * math.pi / total_time)
    out_ref[0] = c
    out_ref[1] = c * far_c - s * far_s
    out_ref[2] = s
    out_ref[3] = s * far_c + c * far_s
    out_ref[4] = jnp.cos(turn)
    out_ref[5] = jnp.sin(turn)


def moveout(base, slows, offs, shift, total_time):
    count = slows.shape[0]
    offsets = offs.shape[1]
    rows = min(count, 64)
    return pl.pallas_call(
        functools.partial(moveout_kernel, shift, total_time),
        grid=(count // rows,),
        in_specs=[
            pl.BlockSpec(memory_space=pltpu.SMEM),
            pl.BlockSpec((rows, 1), lambda i: (i, 0)),
            pl.BlockSpec((1, offsets), lambda i: (0, 0)),
        ],
        out_specs=pl.BlockSpec((6, rows, offsets), lambda i: (0, i, 0)),
        out_shape=jax.ShapeDtypeStruct((6, count, offsets), jnp.float32),
        compiler_params=pltpu.CompilerParams(vmem_limit_bytes=24 * MIB),
        cost_estimate=pl.CostEstimate(
            flops=300 * count * offsets,
            bytes_accessed=24 * count * offsets,
            transcendentals=6 * count * offsets,
        ),
    )(base, slows, offs)


def quotient(value, divisor):
    if divisor & (divisor - 1):
        return value // divisor
    return lax.shift_right_logical(value, jnp.int32(divisor.bit_length() - 1))


def remainder(value, divisor):
    if divisor & (divisor - 1):
        return value % divisor
    return value & (divisor - 1)


def one_hot(rows, columns, source):
    row = lax.broadcasted_iota(jnp.int32, (rows, 1), 0)
    column = lax.broadcasted_iota(jnp.int32, (rows, columns), 1)
    return jnp.where(column == source(row), 1.0, 0.0).astype(jnp.bfloat16)


TILE = 16


def prepare(gathers, down, data_ref, plain, turned):
    devices, own_offsets, pairs, lanes = data_ref.shape
    size = TILE * pairs
    together = TILE // own_offsets

    def received(r):
        k = quotient(r, TILE)
        return remainder(r, TILE) * pairs + k + down * (pairs - 1 - 2 * k)

    swap = one_hot(size, size, received)
    for d in range(devices // together):
        block = data_ref[d * together : (d + 1) * together].reshape(size, lanes)
        if pairs > 1:
            block = jnp.dot(swap, block, preferred_element_type=jnp.float32).astype(jnp.bfloat16)
        plain[:, d * TILE : (d + 1) * TILE] = block.reshape(pairs, TILE, lanes)
    row = lax.broadcasted_iota(jnp.int32, (lanes, lanes), 0)
    column = lax.broadcasted_iota(jnp.int32, (lanes, lanes), 1)
    quarter = jnp.where(
        remainder(column, 2 * gathers) < gathers,
        jnp.where(row == column + gathers, -1.0, 0.0),
        jnp.where(row == column - gathers, 1.0, 0.0),
    ).astype(jnp.bfloat16)
    for k in range(pairs):
        turned[k] = jnp.dot(plain[k], quarter, preferred_element_type=jnp.float32).astype(
            jnp.bfloat16
        )


def sum_offsets(gathers, first, state_ref, plain, turned, turns, held):
    pairs, slows, lanes = held.shape
    offsets = plain.shape[1]

    def fill(t, carry):
        source = pl.ds(pl.multiple_of(first + t * TILE, TILE), TILE)
        own = pl.ds(pl.multiple_of(t * TILE, TILE), TILE)
        step_c = state_ref[4, source]
        step_s = state_ref[5, source]
        twice = 2.0 * step_c
        now = [state_ref[i, source] for i in range(4)]
        past = [now[a] * step_c + now[2 + a] * step_s for a in range(2)]
        past += [now[2 + a] * step_c - now[a] * step_s for a in range(2)]
        for k in range(pairs):
            for i in range(4):
                turns[k, i, own] = now[i].astype(jnp.bfloat16)
                now[i], past[i] = twice * now[i] - past[i], now[i]
        return carry

    lax.fori_loop(0, slows // TILE, fill, 0)
    first_half = lax.broadcasted_iota(jnp.int32, (1, lanes), 1) < 2 * gathers
    for k in range(pairs):
        cosine = turns[k, :2].reshape(2 * slows, offsets)
        sines = turns[k, 2:].reshape(2 * slows, offsets)
        both = jnp.dot(cosine, plain[k], preferred_element_type=jnp.float32) + jnp.dot(
            sines, turned[k], preferred_element_type=jnp.float32
        )
        held[k] = jnp.where(first_half, both[:slows], both[slows:]).astype(jnp.bfloat16)


def dealing(pairs):
    size = TILE * pairs
    return one_hot(size, size, lambda r: remainder(r, pairs) * TILE + quotient(r, pairs))


def deal(swap, held, first, out_ref):
    pairs, _, lanes = held.shape
    size = TILE * pairs
    for p in range(out_ref.shape[0] // size):
        start = first + p * TILE
        if not isinstance(start, int):
            start = pl.multiple_of(start, TILE)
        block = held[:, pl.ds(start, TILE)].reshape(size, lanes)
        if pairs > 1:
            block = jnp.dot(swap, block, preferred_element_type=jnp.float32)
        out_ref[p * size : (p + 1) * size] = block.astype(out_ref.dtype)


def radon_kernel(gathers, down_ref, state_ref, data_ref, out_ref, turns, plain, turned, held):
    prepare(gathers, down_ref[0], data_ref, plain, turned)
    sum_offsets(gathers, 0, state_ref, plain, turned, turns, held)
    deal(dealing(held.shape[0]), held, 0, out_ref)


def radon(down, state, data, gathers):
    _, count, offsets = state.shape
    pairs, lanes = data.shape[2:]
    vmem = pl.BlockSpec(memory_space=pltpu.VMEM)
    return pl.pallas_call(
        functools.partial(radon_kernel, gathers),
        in_specs=[pl.BlockSpec(memory_space=pltpu.SMEM), vmem, vmem],
        out_specs=vmem,
        out_shape=jax.ShapeDtypeStruct((count * pairs, lanes), jnp.bfloat16),
        scratch_shapes=[
            pltpu.VMEM((pairs, 4, count, offsets), jnp.bfloat16),
            pltpu.VMEM((pairs, offsets, lanes), jnp.bfloat16),
            pltpu.VMEM((pairs, offsets, lanes), jnp.bfloat16),
            pltpu.VMEM((pairs, count, lanes), jnp.bfloat16),
        ],
        compiler_params=pltpu.CompilerParams(vmem_limit_bytes=24 * MIB),
    )(down, state, data)


def deal_half(held, me, first, out_refs):
    swap = dealing(held.shape[0])
    half = len(out_refs)
    each = held.shape[1] // half
    for s, out_ref in enumerate(out_refs):
        deal(swap, held, remainder(me ^ (first + s), half) * each, out_ref)


def far_kernel(gathers, half, place_ref, state_ref, data_ref, plain, turned, sign_ref, *refs):
    *out_refs, turns, held = refs
    me = place_ref[1]
    prepare(gathers, place_ref[0], data_ref, plain, turned)
    sign_ref[...] = plain[0, :TILE]
    other = (1 - quotient(me, half)) * held.shape[1]
    sum_offsets(gathers, other, state_ref, plain, turned, turns, held)
    deal_half(held, me, half, out_refs)


def near_kernel(gathers, half, place_ref, state_ref, plain, turned, _, *refs):
    *out_refs, turns, held = refs
    me = place_ref[1]
    own = quotient(me, half) * held.shape[1]
    sum_offsets(gathers, own, state_ref, plain, turned, turns, held)
    deal_half(held, me, 0, out_refs)


def radon_swapped(place, state, data, gathers, offset_devices):
    _, count, offsets = state.shape
    pairs, lanes = data.shape[2:]
    half = offset_devices // 2
    vmem = pl.BlockSpec(memory_space=pltpu.VMEM)
    smem = pl.BlockSpec(memory_space=pltpu.SMEM)
    block = jax.ShapeDtypeStruct((count // offset_devices * pairs, lanes), jnp.bfloat16)
    spectra = jax.ShapeDtypeStruct((pairs, offsets, lanes), jnp.bfloat16)
    scratch = [
        pltpu.VMEM((pairs, 4, count // 2, offsets), jnp.bfloat16),
        pltpu.VMEM((pairs, count // 2, lanes), jnp.bfloat16),
    ]
    cost = pl.CostEstimate(
        flops=8 * count * offsets * pairs * lanes,
        bytes_accessed=8 * count * offsets,
        transcendentals=0,
    )
    sign = jax.ShapeDtypeStruct((TILE, lanes), jnp.bfloat16)
    plain, turned, sign, *far = pl.pallas_call(
        functools.partial(far_kernel, gathers, half),
        in_specs=[smem, vmem, vmem],
        out_specs=[vmem] * (3 + half),
        out_shape=[spectra, spectra, sign] + [block] * half,
        scratch_shapes=scratch,
        compiler_params=pltpu.CompilerParams(vmem_limit_bytes=20 * MIB),
        cost_estimate=cost,
    )(place, state, data)
    def swapped(part, s):
        swaps = [(o, o ^ s) for o in range(offset_devices)]
        return lax.ppermute(part, "offset", swaps)

    far[:-1] = [swapped(part, half + s) for s, part in enumerate(far[:-1])]
    sign = swapped(sign, 1)
    near = pl.pallas_call(
        functools.partial(near_kernel, gathers, half),
        in_specs=[smem, vmem, vmem, vmem, vmem],
        out_specs=[vmem] * half,
        out_shape=[block] * half,
        scratch_shapes=scratch,
        compiler_params=pltpu.CompilerParams(vmem_limit_bytes=20 * MIB),
        cost_estimate=cost,
    )(place, state, plain, turned, sign)
    near = list(near)
    last, far[0] = lax.optimization_barrier((far[-1], far[0]))
    near = [swapped(part, s) if s else part for s, part in enumerate(near)]
    far[-1] = swapped(last, offset_devices - 1)
    parts = near + far
    return list(range(half, offset_devices - 1)) + list(range(half))[::-1] + [offset_devices - 1], [parts[s] for s in list(range(half, offset_devices - 1)) + list(range(half))[::-1] + [offset_devices - 1]]


def join_kernel(scale, order, place_ref, *refs):
    *parts, out_ref, wide, ready, sems = refs
    groups, step, half_lanes, _ = ready.shape
    rows = wide.shape[1]
    pairs = rows // len(parts)
    copies = []
    for g in range(groups):
        for s, part in zip(order, parts):
            own = pl.ds(pl.multiple_of((place_ref[1] ^ s) * pairs, pairs), pairs)
            for i in range(step):
                p = g * step + i
                wide[p, own] = part[p * pairs : (p + 1) * pairs]
        for i in range(step):
            block = wide[g * step + i].T.astype(jnp.float32) * scale
            ready[g, i, :, :rows] = block[:half_lanes]
            ready[g, i, :, rows:] = block[half_lanes:]
        copies.append(
            pltpu.make_async_copy(ready.at[g], out_ref.at[pl.ds(g * step, step)], sems.at[g])
        )
        copies[-1].start()
    for copy in copies:
        copy.wait()


def join(place, order, parts, slows, scale):
    pairs = parts[0].shape[0] // slows
    lanes = parts[0].shape[1]
    rows = len(parts) * pairs
    step = 4
    vmem = pl.BlockSpec(memory_space=pltpu.VMEM)
    return pl.pallas_call(
        functools.partial(join_kernel, scale, order),
        in_specs=[pl.BlockSpec(memory_space=pltpu.SMEM)] + [vmem] * len(parts),
        out_specs=pl.BlockSpec(memory_space=pl.ANY),
        out_shape=jax.ShapeDtypeStruct((slows, lanes // 2, 2 * rows), jnp.float32),
        scratch_shapes=[
            pltpu.VMEM((slows, rows, lanes), jnp.bfloat16),
            pltpu.VMEM((slows // step, step, lanes // 2, 2 * rows), jnp.float32),
            pltpu.SemaphoreType.DMA((slows // step,)),
        ],
        compiler_params=pltpu.CompilerParams(vmem_limit_bytes=16 * MIB),
    )(place, *parts)


def finish_kernel(scale, in_ref, out_ref):
    devices, slows, pairs, lanes = in_ref.shape
    rows = devices * pairs
    for p in range(slows):
        block = in_ref[:, p].reshape(rows, lanes).astype(jnp.float32) * scale
        turned = block.T
        out_ref[p, :, :rows] = turned[: lanes // 2]
        out_ref[p, :, rows:] = turned[lanes // 2 :]


def finish(parts, scale):
    devices, slows, pairs, lanes = parts.shape
    rows = devices * pairs
    step = 8
    return pl.pallas_call(
        functools.partial(finish_kernel, scale),
        grid=(slows // step,),
        in_specs=[pl.BlockSpec((devices, step, pairs, lanes), lambda i: (0, i, 0, 0))],
        out_specs=pl.BlockSpec((step, lanes // 2, 2 * rows), lambda i: (i, 0, 0)),
        out_shape=jax.ShapeDtypeStruct((slows, lanes // 2, 2 * rows), jnp.float32),
        compiler_params=pltpu.CompilerParams(vmem_limit_bytes=32 * MIB),
    )(parts)


def local(raw_traces, trace_slot, offset_index, slowness_index):
    gathers, local_offsets = trace_slot.shape
    local_times = raw_traces.shape[1]
    freq_devices = lax.axis_size("freq")
    offset_devices = lax.axis_size("offset")
    devices = freq_devices * offset_devices
    total_time = local_times * freq_devices
    offsets = local_offsets * offset_devices
    band = NF // freq_devices
    own_freqs = NF // devices
    halves = 2
    pairs = own_freqs // halves
    own_offsets = local_offsets // freq_devices

    me = lax.axis_index("freq").astype(jnp.int32).reshape(1)
    series = list(pick(me, trace_slot.astype(jnp.float32), raw_traces, freq_devices))
    for s in list(range(2, freq_devices)) + [1]:
        swaps = [(f, f ^ s) for f in range(freq_devices)]
        series[s] = lax.ppermute(series[s], "freq", swaps)
    table = jnp.asarray(table_rows(total_time, freq_devices, offset_devices, halves, pairs))
    spectrum = transform(me, table, series, pairs, gathers)
    data = lax.all_to_all(spectrum, ("offset", "freq"), 0, 0, tiled=True)

    offs = offset_index.reshape(1, offsets).astype(jnp.float32)
    slows = slowness_index.astype(jnp.float32)[:, None]
    first = lax.axis_index("freq") * band + lax.axis_index("offset") * pairs
    base = (2 * first + 1).astype(jnp.float32) * (math.pi / total_time)
    state = moveout(base.reshape(1), slows, offs, band // halves, total_time)
    down = (2 * lax.axis_index("offset") // offset_devices).astype(jnp.int32)
    place = jnp.stack([down, lax.axis_index("offset").astype(jnp.int32)])
    slows_each = NP // offset_devices
    scale = 1.0 / math.sqrt(offsets)
    if slows_each % TILE == 0:
        order, blocks = radon_swapped(place, state, data, gathers, offset_devices)
        result = join(place, order, blocks, slows_each, scale)
    else:
        panel = radon(place, state, data, gathers)
        panel = panel.reshape(offset_devices, slows_each, pairs, 2 * halves * gathers)
        result = finish(lax.all_to_all(panel, "offset", 0, 0, tiled=True), scale)
    return jnp.transpose(result, (0, 2, 1))


def solution(mesh):
    placed = (P("offset", "freq"), P(None, "offset"), P(), P())
    return jax.shard_map(
        local, mesh=mesh, in_specs=placed, out_specs=P("offset", "freq", None), check_vma=False
    )
```

```python
import functools
import math

import jax
import jax.numpy as jnp
import ml_dtypes
import numpy as np
from jax import lax
from jax.experimental import pallas as pl
from jax.experimental.pallas import tpu as pltpu
from jax.sharding import PartitionSpec as P

NF = 1024
NP = 256
APEX_TIME = 100.0
CURVATURE = 0.0003
MIB = 1 << 20


def table_rows(total_time, freq_devices, offset_devices, halves, pairs):
    band = NF // freq_devices
    o, f, a, k = np.meshgrid(
        np.arange(offset_devices // 2),
        np.arange(freq_devices),
        np.arange(halves),
        np.arange(pairs),
        indexing="ij",
    )
    freq_ids = (f * band + a * (band // halves) + o * pairs + k).reshape(-1, pairs)
    times = np.concatenate([np.arange(0, total_time, 2), np.arange(1, total_time, 2)])
    turns = (2 * freq_ids[..., None] + 1) * times % (2 * total_time)
    angles = turns.astype(np.float32) * np.float32(math.pi / total_time)
    both = np.stack([np.cos(angles), -np.sin(angles)], axis=1).reshape(-1, total_time)
    return (both / np.float32(math.sqrt(total_time))).astype(ml_dtypes.bfloat16)


def pick_kernel(me_ref, slot_ref, raw_ref, *out_refs):
    gathers, local_offsets = slot_ref.shape
    own_offsets = local_offsets // len(out_refs)
    times = raw_ref.shape[1]
    half = times // 2
    row = lax.broadcasted_iota(jnp.int32, (times, times), 0)
    column = lax.broadcasted_iota(jnp.int32, (times, times), 1)
    source = jnp.where(column < half, 2 * column, 2 * (column - half) + 1)
    split = jnp.where(row == source, 1.0, 0.0).astype(jnp.bfloat16)
    raw = jnp.dot(raw_ref[...], split, preferred_element_type=jnp.float32).astype(jnp.bfloat16)
    lane = lax.broadcasted_iota(jnp.int32, (gathers, raw_ref.shape[0]), 1)
    slot = slot_ref[...]
    place = lax.broadcasted_iota(jnp.int32, slot.shape, 1)
    for s, out_ref in enumerate(out_refs):
        first = (me_ref[0] ^ s) * own_offsets
        picks = []
        for h in range(own_offsets):
            wanted = jnp.sum(jnp.where(place == first + h, slot, 0.0), axis=1, keepdims=True)
            picks.append(
                jnp.where(lane == wanted.astype(jnp.int32), 1.0, 0.0).astype(jnp.bfloat16)
            )
        out_ref[...] = jnp.dot(
            jnp.concatenate(picks, axis=0), raw, preferred_element_type=jnp.float32
        ).astype(out_ref.dtype)


def pick(me, trace_slot, raw_traces, groups):
    gathers, local_offsets = trace_slot.shape
    rows = gathers * local_offsets // groups
    vmem = pl.BlockSpec(memory_space=pltpu.VMEM)
    block = jax.ShapeDtypeStruct((rows, raw_traces.shape[1]), raw_traces.dtype)
    return pl.pallas_call(
        pick_kernel,
        in_specs=[pl.BlockSpec(memory_space=pltpu.SMEM), vmem, vmem],
        out_specs=[vmem] * groups,
        out_shape=[block] * groups,
        compiler_params=pltpu.CompilerParams(vmem_limit_bytes=24 * MIB),
    )(me, trace_slot, raw_traces)


def regroup(parts, gathers):
    lanes = 4 * gathers
    lane = lax.broadcasted_iota(jnp.int32, (1, lanes), 1)
    low_half = lane < 2 * gathers
    low_part = lane % (2 * gathers) < gathers
    found = []
    for q in range(parts[0].shape[1] // lanes):
        x = [part[:, q * lanes : (q + 1) * lanes] for part in parts]
        for top in range(2):
            pair = []
            for part in range(2):
                a, b = x[part], x[2 + part]
                if top == 0:
                    pair.append(jnp.where(low_half, a, pltpu.roll(b, 2 * gathers, 1)))
                else:
                    pair.append(jnp.where(low_half, pltpu.roll(a, 2 * gathers, 1), b))
            found.append(jnp.where(low_part, pair[0], pltpu.roll(pair[1], gathers, 1)))
            found.append(jnp.where(low_part, pltpu.roll(pair[0], lanes - gathers, 1), pair[1]))
    return found


def time_sums(me, first, table_ref, series_refs, even, odd, own):
    half = even.shape[1] // 2
    depth = table_ref.shape[1] // 2
    evens = odds = None
    for r in range(len(series_refs) // 2):
        start = (quotient(me, 2) ^ (first + r)) * 2 * half
        even_part = jnp.dot(
            table_ref[own, pl.ds(pl.multiple_of(start, 2 * half), 2 * half)],
            even[r],
            preferred_element_type=jnp.float32,
        )
        odd_part = jnp.dot(
            table_ref[own, pl.ds(pl.multiple_of(depth + start, 2 * half), 2 * half)],
            odd[r],
            preferred_element_type=jnp.float32,
        )
        evens = even_part if evens is None else evens + even_part
        odds = odd_part if odds is None else odds + odd_part
    return evens, odds


def turn_series(me, series_refs, even, odd):
    half = even.shape[1] // 2
    for s, series_ref in enumerate(series_refs):
        turned = series_ref[...].T
        place = pl.ds(pl.multiple_of(((me ^ s) & 1) * half, half), half)
        even[s // 2, place] = turned[:half]
        odd[s // 2, place] = turned[half:]


def begin_kernel(chunks, me_ref, table_ref, *refs):
    *series_refs, out_ref, even, odd = refs
    me = me_ref[0]
    turn_series(me, series_refs, even, odd)
    step = table_ref.shape[0] // chunks
    for i in range(chunks):
        own = slice(i * step, (i + 1) * step)
        out_ref[0, own], out_ref[1, own] = time_sums(
            me, 0, table_ref, series_refs, even, odd, own
        )


def transform_kernel(pairs, gathers, chunks, me_ref, table_ref, begun_ref, *refs):
    *series_refs, out_ref, even, odd = refs
    me = me_ref[0]
    turn_series(me, series_refs, even, odd)
    step = table_ref.shape[0] // chunks
    for i in range(chunks):
        own = slice(i * step, (i + 1) * step)
        evens, odds = time_sums(me, 1, table_ref, series_refs, even, odd, own)
        evens = evens + begun_ref[0, own]
        odds = odds + begun_ref[1, own]
        low = evens + odds
        high = evens - odds
        if len(out_ref.shape) == 3:
            row = lax.broadcasted_iota(jnp.int32, (step, 1), 0)
            out_ref[0, own] = low.astype(out_ref.dtype)
            out_ref[1, own] = jnp.where(row // pairs % 2 == 0, high, -high).astype(out_ref.dtype)
            continue
        targets = step // (4 * pairs)
        devices = out_ref.shape[0]
        for d in range(targets):
            cuts = [slice((4 * d + c) * pairs, (4 * d + c + 1) * pairs) for c in range(4)]
            place = i * targets + d
            for h, value in enumerate(regroup([low[cut] for cut in cuts], gathers)):
                out_ref[place, h] = value.astype(out_ref.dtype)
            mirrored = [high[cuts[2]], -high[cuts[3]], high[cuts[0]], -high[cuts[1]]]
            for h, value in enumerate(regroup(mirrored, gathers)):
                out_ref[devices - 1 - place, h] = value.astype(out_ref.dtype)


def transform(me, table, series, pairs, gathers):
    columns, total_time = table.shape
    rows, local_times = series[0].shape
    own_offsets = rows // gathers
    devices = columns // (2 * pairs)
    final = (devices, own_offsets, pairs, 4 * gathers)
    chunks = 4
    aligned = rows % (4 * gathers) == 0 and pairs % 8 == 0 and devices % (2 * chunks) == 0
    vmem = pl.BlockSpec(memory_space=pltpu.VMEM)
    smem = pl.BlockSpec(memory_space=pltpu.SMEM)
    early, late = series[:2], series[2:]

    def scratch(blocks):
        return [pltpu.VMEM((len(blocks) // 2, local_times, rows), jnp.bfloat16)] * 2

    params = pltpu.CompilerParams(vmem_limit_bytes=24 * MIB)
    begun = pl.pallas_call(
        functools.partial(begin_kernel, chunks),
        in_specs=[smem] + [vmem] * (1 + len(early)),
        out_specs=vmem,
        out_shape=jax.ShapeDtypeStruct((2, columns, rows), jnp.float32),
        scratch_shapes=scratch(early),
        compiler_params=params,
        cost_estimate=pl.CostEstimate(
            flops=columns * total_time * rows,
            bytes_accessed=2 * columns * total_time,
            transcendentals=0,
        ),
    )(me, table, *early)
    out = pl.pallas_call(
        functools.partial(transform_kernel, pairs, gathers, chunks),
        in_specs=[smem] + [vmem] * (2 + len(late)),
        out_specs=vmem,
        out_shape=jax.ShapeDtypeStruct(final if aligned else (2, columns, rows), jnp.bfloat16),
        scratch_shapes=scratch(late),
        compiler_params=params,
    )(me, table, begun, *late)
    if aligned:
        return out
    out = out.reshape(2, devices // 2, 2, 2, pairs, own_offsets, gathers)
    out = jnp.concatenate([out[0], jnp.flip(out[1], (0, 1))], axis=0)
    return out.transpose(0, 4, 3, 1, 2, 5).reshape(final)


def moveout_kernel(shift, total_time, base_ref, slow_ref, offs_ref, out_ref):
    spread = CURVATURE * slow_ref[...] * offs_ref[...]
    delay = jnp.sqrt(APEX_TIME * APEX_TIME + spread * spread) - APEX_TIME
    phase = base_ref[0] * delay
    c = jnp.cos(phase)
    s = jnp.sin(phase)
    far = delay * (2.0 * shift * math.pi / total_time)
    far_c = jnp.cos(far)
    far_s = jnp.sin(far)
    turn = delay * (2.0 * math.pi / total_time)
    out_ref[0] = c
    out_ref[1] = c * far_c - s * far_s
    out_ref[2] = s
    out_ref[3] = s * far_c + c * far_s
    out_ref[4] = jnp.cos(turn)
    out_ref[5] = jnp.sin(turn)


def moveout(base, slows, offs, shift, total_time):
    count = slows.shape[0]
    offsets = offs.shape[1]
    rows = min(count, 64)
    return pl.pallas_call(
        functools.partial(moveout_kernel, shift, total_time),
        grid=(count // rows,),
        in_specs=[
            pl.BlockSpec(memory_space=pltpu.SMEM),
            pl.BlockSpec((rows, 1), lambda i: (i, 0)),
            pl.BlockSpec((1, offsets), lambda i: (0, 0)),
        ],
        out_specs=pl.BlockSpec((6, rows, offsets), lambda i: (0, i, 0)),
        out_shape=jax.ShapeDtypeStruct((6, count, offsets), jnp.float32),
        compiler_params=pltpu.CompilerParams(vmem_limit_bytes=24 * MIB),
        cost_estimate=pl.CostEstimate(
            flops=300 * count * offsets,
            bytes_accessed=24 * count * offsets,
            transcendentals=6 * count * offsets,
        ),
    )(base, slows, offs)


def quotient(value, divisor):
    if divisor & (divisor - 1):
        return value // divisor
    return lax.shift_right_logical(value, jnp.int32(divisor.bit_length() - 1))


def remainder(value, divisor):
    if divisor & (divisor - 1):
        return value % divisor
    return value & (divisor - 1)


def one_hot(rows, columns, source):
    row = lax.broadcasted_iota(jnp.int32, (rows, 1), 0)
    column = lax.broadcasted_iota(jnp.int32, (rows, columns), 1)
    return jnp.where(column == source(row), 1.0, 0.0).astype(jnp.bfloat16)


TILE = 16


def prepare(gathers, down, data_ref, plain, turned):
    devices, own_offsets, pairs, lanes = data_ref.shape
    size = TILE * pairs
    together = TILE // own_offsets

    def received(r):
        k = quotient(r, TILE)
        return remainder(r, TILE) * pairs + k + down * (pairs - 1 - 2 * k)

    swap = one_hot(size, size, received)
    for d in range(devices // together):
        block = data_ref[d * together : (d + 1) * together].reshape(size, lanes)
        if pairs > 1:
            block = jnp.dot(swap, block, preferred_element_type=jnp.float32).astype(jnp.bfloat16)
        plain[:, d * TILE : (d + 1) * TILE] = block.reshape(pairs, TILE, lanes)
    row = lax.broadcasted_iota(jnp.int32, (lanes, lanes), 0)
    column = lax.broadcasted_iota(jnp.int32, (lanes, lanes), 1)
    quarter = jnp.where(
        remainder(column, 2 * gathers) < gathers,
        jnp.where(row == column + gathers, -1.0, 0.0),
        jnp.where(row == column - gathers, 1.0, 0.0),
    ).astype(jnp.bfloat16)
    for k in range(pairs):
        turned[k] = jnp.dot(plain[k], quarter, preferred_element_type=jnp.float32).astype(
            jnp.bfloat16
        )


def sum_offsets(gathers, first, state_ref, plain, turned, turns, held):
    pairs, slows, lanes = held.shape
    offsets = plain.shape[1]

    def fill(t, carry):
        source = pl.ds(pl.multiple_of(first + t * TILE, TILE), TILE)
        own = pl.ds(pl.multiple_of(t * TILE, TILE), TILE)
        step_c = state_ref[4, source]
        step_s = state_ref[5, source]
        twice = 2.0 * step_c
        now = [state_ref[i, source] for i in range(4)]
        past = [now[a] * step_c + now[2 + a] * step_s for a in range(2)]
        past += [now[2 + a] * step_c - now[a] * step_s for a in range(2)]
        for k in range(pairs):
            for i in range(4):
                turns[k, i, own] = now[i].astype(jnp.bfloat16)
                now[i], past[i] = twice * now[i] - past[i], now[i]
        return carry

    lax.fori_loop(0, slows // TILE, fill, 0)
    first_half = lax.broadcasted_iota(jnp.int32, (1, lanes), 1) < 2 * gathers
    for k in range(pairs):
        cosine = turns[k, :2].reshape(2 * slows, offsets)
        sines = turns[k, 2:].reshape(2 * slows, offsets)
        both = jnp.dot(cosine, plain[k], preferred_element_type=jnp.float32) + jnp.dot(
            sines, turned[k], preferred_element_type=jnp.float32
        )
        held[k] = jnp.where(first_half, both[:slows], both[slows:]).astype(jnp.bfloat16)


def dealing(pairs):
    size = TILE * pairs
    return one_hot(size, size, lambda r: remainder(r, pairs) * TILE + quotient(r, pairs))


def deal(swap, held, first, out_ref):
    pairs, _, lanes = held.shape
    size = TILE * pairs
    for p in range(out_ref.shape[0] // size):
        start = first + p * TILE
        if not isinstance(start, int):
            start = pl.multiple_of(start, TILE)
        block = held[:, pl.ds(start, TILE)].reshape(size, lanes)
        if pairs > 1:
            block = jnp.dot(swap, block, preferred_element_type=jnp.float32)
        out_ref[p * size : (p + 1) * size] = block.astype(out_ref.dtype)


def radon_kernel(gathers, down_ref, state_ref, data_ref, out_ref, turns, plain, turned, held):
    prepare(gathers, down_ref[0], data_ref, plain, turned)
    sum_offsets(gathers, 0, state_ref, plain, turned, turns, held)
    deal(dealing(held.shape[0]), held, 0, out_ref)


def radon(down, state, data, gathers):
    _, count, offsets = state.shape
    pairs, lanes = data.shape[2:]
    vmem = pl.BlockSpec(memory_space=pltpu.VMEM)
    return pl.pallas_call(
        functools.partial(radon_kernel, gathers),
        in_specs=[pl.BlockSpec(memory_space=pltpu.SMEM), vmem, vmem],
        out_specs=vmem,
        out_shape=jax.ShapeDtypeStruct((count * pairs, lanes), jnp.bfloat16),
        scratch_shapes=[
            pltpu.VMEM((pairs, 4, count, offsets), jnp.bfloat16),
            pltpu.VMEM((pairs, offsets, lanes), jnp.bfloat16),
            pltpu.VMEM((pairs, offsets, lanes), jnp.bfloat16),
            pltpu.VMEM((pairs, count, lanes), jnp.bfloat16),
        ],
        compiler_params=pltpu.CompilerParams(vmem_limit_bytes=24 * MIB),
    )(down, state, data)


def deal_half(held, me, first, out_refs):
    swap = dealing(held.shape[0])
    half = len(out_refs)
    each = held.shape[1] // half
    for s, out_ref in enumerate(out_refs):
        deal(swap, held, remainder(me ^ (first + s), half) * each, out_ref)


def far_kernel(gathers, half, place_ref, state_ref, data_ref, plain, turned, sign_ref, *refs):
    *out_refs, turns, held = refs
    me = place_ref[1]
    prepare(gathers, place_ref[0], data_ref, plain, turned)
    sign_ref[...] = plain[0, :TILE]
    other = (1 - quotient(me, half)) * held.shape[1]
    sum_offsets(gathers, other, state_ref, plain, turned, turns, held)
    deal_half(held, me, half, out_refs)


def near_kernel(gathers, half, place_ref, state_ref, plain, turned, _, *refs):
    *out_refs, turns, held = refs
    me = place_ref[1]
    own = quotient(me, half) * held.shape[1]
    sum_offsets(gathers, own, state_ref, plain, turned, turns, held)
    deal_half(held, me, 0, out_refs)


def radon_swapped(place, state, data, gathers, offset_devices):
    _, count, offsets = state.shape
    pairs, lanes = data.shape[2:]
    half = offset_devices // 2
    vmem = pl.BlockSpec(memory_space=pltpu.VMEM)
    smem = pl.BlockSpec(memory_space=pltpu.SMEM)
    block = jax.ShapeDtypeStruct((count // offset_devices * pairs, lanes), jnp.bfloat16)
    spectra = jax.ShapeDtypeStruct((pairs, offsets, lanes), jnp.bfloat16)
    scratch = [
        pltpu.VMEM((pairs, 4, count // 2, offsets), jnp.bfloat16),
        pltpu.VMEM((pairs, count // 2, lanes), jnp.bfloat16),
    ]
    cost = pl.CostEstimate(
        flops=8 * count * offsets * pairs * lanes,
        bytes_accessed=8 * count * offsets,
        transcendentals=0,
    )
    sign = jax.ShapeDtypeStruct((TILE, lanes), jnp.bfloat16)
    plain, turned, sign, *far = pl.pallas_call(
        functools.partial(far_kernel, gathers, half),
        in_specs=[smem, vmem, vmem],
        out_specs=[vmem] * (3 + half),
        out_shape=[spectra, spectra, sign] + [block] * half,
        scratch_shapes=scratch,
        compiler_params=pltpu.CompilerParams(vmem_limit_bytes=20 * MIB),
        cost_estimate=cost,
    )(place, state, data)
    def swapped(part, s):
        swaps = [(o, o ^ s) for o in range(offset_devices)]
        return lax.ppermute(part, "offset", swaps)

    far[:-1] = [swapped(part, half + s) for s, part in enumerate(far[:-1])]
    sign = swapped(sign, 1)
    near = pl.pallas_call(
        functools.partial(near_kernel, gathers, half),
        in_specs=[smem, vmem, vmem, vmem, vmem],
        out_specs=[vmem] * half,
        out_shape=[block] * half,
        scratch_shapes=scratch,
        compiler_params=pltpu.CompilerParams(vmem_limit_bytes=20 * MIB),
        cost_estimate=cost,
    )(place, state, plain, turned, sign)
    near = list(near)
    last, far[0] = lax.optimization_barrier((far[-1], far[0]))
    near = [swapped(part, s) if s else part for s, part in enumerate(near)]
    far[-1] = swapped(last, offset_devices - 1)
    parts = near + far
    return list(range(half, offset_devices - 1)) + list(range(half))[::-1] + [offset_devices - 1], [parts[s] for s in list(range(half, offset_devices - 1)) + list(range(half))[::-1] + [offset_devices - 1]]


def join_kernel(scale, order, place_ref, *refs):
    *parts, out_ref, wide, ready, sems = refs
    groups, step, half_lanes, _ = ready.shape
    rows = wide.shape[1]
    pairs = rows // len(parts)
    copies = []
    for g in range(groups):
        for s, part in zip(order, parts):
            own = pl.ds(pl.multiple_of((place_ref[1] ^ s) * pairs, pairs), pairs)
            for i in range(step):
                p = g * step + i
                wide[p, own] = part[p * pairs : (p + 1) * pairs]
        for i in range(step):
            block = wide[g * step + i].T.astype(jnp.float32) * scale
            ready[g, i, :, :rows] = block[:half_lanes]
            ready[g, i, :, rows:] = block[half_lanes:]
        copies.append(
            pltpu.make_async_copy(ready.at[g], out_ref.at[pl.ds(g * step, step)], sems.at[g])
        )
        copies[-1].start()
    for copy in copies:
        copy.wait()


def join(place, order, parts, slows, scale):
    pairs = parts[0].shape[0] // slows
    lanes = parts[0].shape[1]
    rows = len(parts) * pairs
    step = 2
    vmem = pl.BlockSpec(memory_space=pltpu.VMEM)
    return pl.pallas_call(
        functools.partial(join_kernel, scale, order),
        in_specs=[pl.BlockSpec(memory_space=pltpu.SMEM)] + [vmem] * len(parts),
        out_specs=pl.BlockSpec(memory_space=pl.ANY),
        out_shape=jax.ShapeDtypeStruct((slows, lanes // 2, 2 * rows), jnp.float32),
        scratch_shapes=[
            pltpu.VMEM((slows, rows, lanes), jnp.bfloat16),
            pltpu.VMEM((slows // step, step, lanes // 2, 2 * rows), jnp.float32),
            pltpu.SemaphoreType.DMA((slows // step,)),
        ],
        compiler_params=pltpu.CompilerParams(vmem_limit_bytes=16 * MIB),
    )(place, *parts)


def finish_kernel(scale, in_ref, out_ref):
    devices, slows, pairs, lanes = in_ref.shape
    rows = devices * pairs
    for p in range(slows):
        block = in_ref[:, p].reshape(rows, lanes).astype(jnp.float32) * scale
        turned = block.T
        out_ref[p, :, :rows] = turned[: lanes // 2]
        out_ref[p, :, rows:] = turned[lanes // 2 :]


def finish(parts, scale):
    devices, slows, pairs, lanes = parts.shape
    rows = devices * pairs
    step = 8
    return pl.pallas_call(
        functools.partial(finish_kernel, scale),
        grid=(slows // step,),
        in_specs=[pl.BlockSpec((devices, step, pairs, lanes), lambda i: (0, i, 0, 0))],
        out_specs=pl.BlockSpec((step, lanes // 2, 2 * rows), lambda i: (i, 0, 0)),
        out_shape=jax.ShapeDtypeStruct((slows, lanes // 2, 2 * rows), jnp.float32),
        compiler_params=pltpu.CompilerParams(vmem_limit_bytes=32 * MIB),
    )(parts)


def local(raw_traces, trace_slot, offset_index, slowness_index):
    gathers, local_offsets = trace_slot.shape
    local_times = raw_traces.shape[1]
    freq_devices = lax.axis_size("freq")
    offset_devices = lax.axis_size("offset")
    devices = freq_devices * offset_devices
    total_time = local_times * freq_devices
    offsets = local_offsets * offset_devices
    band = NF // freq_devices
    own_freqs = NF // devices
    halves = 2
    pairs = own_freqs // halves
    own_offsets = local_offsets // freq_devices

    me = lax.axis_index("freq").astype(jnp.int32).reshape(1)
    series = list(pick(me, trace_slot.astype(jnp.float32), raw_traces, freq_devices))
    for s in list(range(2, freq_devices)) + [1]:
        swaps = [(f, f ^ s) for f in range(freq_devices)]
        series[s] = lax.ppermute(series[s], "freq", swaps)
    table = jnp.asarray(table_rows(total_time, freq_devices, offset_devices, halves, pairs))
    spectrum = transform(me, table, series, pairs, gathers)
    data = lax.all_to_all(spectrum, ("offset", "freq"), 0, 0, tiled=True)

    offs = offset_index.reshape(1, offsets).astype(jnp.float32)
    slows = slowness_index.astype(jnp.float32)[:, None]
    first = lax.axis_index("freq") * band + lax.axis_index("offset") * pairs
    base = (2 * first + 1).astype(jnp.float32) * (math.pi / total_time)
    state = moveout(base.reshape(1), slows, offs, band // halves, total_time)
    down = (2 * lax.axis_index("offset") // offset_devices).astype(jnp.int32)
    place = jnp.stack([down, lax.axis_index("offset").astype(jnp.int32)])
    slows_each = NP // offset_devices
    scale = 1.0 / math.sqrt(offsets)
    if slows_each % TILE == 0:
        order, blocks = radon_swapped(place, state, data, gathers, offset_devices)
        result = join(place, order, blocks, slows_each, scale)
    else:
        panel = radon(place, state, data, gathers)
        panel = panel.reshape(offset_devices, slows_each, pairs, 2 * halves * gathers)
        result = finish(lax.all_to_all(panel, "offset", 0, 0, tiled=True), scale)
    return jnp.transpose(result, (0, 2, 1))


def solution(mesh):
    placed = (P("offset", "freq"), P(None, "offset"), P(), P())
    return jax.shard_map(
        local, mesh=mesh, in_specs=placed, out_specs=P("offset", "freq", None), check_vma=False
    )
```
